32 devices in a mesh: wide: 16 (over z, x, core), narrow: 2 (over y).
Axes of the slice: x: 2, y: 2, z: 4, core: 2. Of those that a mesh axis runs over, the one named last changes fastest.
Arguments:
- first_in: float32 [2, 4096, 1024], P(None, 'wide', 'narrow'), may hold values from -6 to 6
- second_in: float32 [2, 4096, 1024], P(None, 'wide', 'narrow'), may hold values from -6 to 6
- attn_norm_gain: float32 [2, 1024], replicated, may hold values from 0.5 to 1.5
- attn_norm_bias: float32 [2, 1024], replicated, may hold values from -1 to 1
- qk_weight: bfloat16 [2, 1024, 1024], P(None, 'wide', 'narrow'), may hold values from -0.1875 to 0.1875
- value_weight: bfloat16 [2, 1024, 1024], P(None, 'wide', 'narrow'), may hold values from -0.1875 to 0.1875
- out_weight: bfloat16 [2, 1024, 1024], P(None, 'wide', 'narrow'), may hold values from -0.75 to 0.75
- out_bias: float32 [2, 1024], P(None, 'narrow'), may hold values from -1 to 1
- ffn_norm_gain: float32 [2, 1024], replicated, may hold values from 0.5 to 1.5
- ffn_norm_bias: float32 [2, 1024], replicated, may hold values from -1 to 1
- up_weight: bfloat16 [2, 1024, 4096], P(None, None, 'narrow'), may hold values from -0.1875 to 0.1875
- up_bias: float32 [2, 4096], P(None, 'narrow'), may hold values from -2.5 to 2.5
- down_weight: bfloat16 [2, 1024, 4096], P(None, None, 'narrow'), may hold values from -0.125 to 0.125
- down_bias: float32 [2, 1024], P(None, 'narrow'), may hold values from -1 to 1
- bucket_perm: int32 [4, 2, 4096], P(None, None, 'wide'), may hold values from 0 to 4095, as said below
- first_cot: float32 [2, 4096, 1024], P(None, 'wide', 'narrow'), may hold values from -6 to 6
- second_cot: float32 [2, 4096, 1024], P(None, 'wide', 'narrow'), may hold values from -6 to 6
Outputs:
- first_out: float32 [2, 4096, 1024], P(None, 'wide', 'narrow')
- second_out: float32 [2, 4096, 1024], P(None, 'wide', 'narrow')
- first_grad: float32 [2, 4096, 1024], P(None, 'wide', 'narrow')
- second_grad: float32 [2, 4096, 1024], P(None, 'wide', 'narrow')
- grad_attn_norm_gain: float32 [2, 1024], replicated
- grad_attn_norm_bias: float32 [2, 1024], replicated
- grad_qk_weight: float32 [2, 1024, 1024], P(None, 'wide', 'narrow')
- grad_value_weight: float32 [2, 1024, 1024], P(None, 'wide', 'narrow')
- grad_out_weight: float32 [2, 1024, 1024], P(None, 'wide', 'narrow')
- grad_out_bias: float32 [2, 1024], P(None, 'narrow')
- grad_ffn_norm_gain: float32 [2, 1024], replicated
- grad_ffn_norm_bias: float32 [2, 1024], replicated
- grad_up_weight: float32 [2, 1024, 4096], P(None, 'wide', 'narrow')
- grad_up_bias: float32 [2, 4096], P(None, 'narrow')
- grad_down_weight: float32 [2, 1024, 4096], P(None, 'wide', 'narrow')
- grad_down_bias: float32 [2, 1024], P(None, 'narrow')
The draws below stay inside these ranges and needn't reach their ends.
Inputs may be any that keep to these rules, and one draw needn't show every extreme that they name: `bucket_perm`: for each round and sequence the row is a permutation of the positions 0 to 4095; the sorted positions k*256 to (k+1)*256 - 1 take exactly 16 tokens from each run of 256 positions j*256 to (j+1)*256 - 1.
All inputs are finite; a program needn't handle non-finite values.
Results may differ from the reference program's by a relative error of at most 0.02.
Values may be sent and summed in bfloat16 or wider, within the bound.
No kernel may reach another device: no remote copies, remote signals or barrier semaphores. Data moves between devices by JAX's collectives and lax.ppermute only.
A program may use at most 256 MiB of HBM per device.

```python
import jax
import jax.numpy as jnp
from jax import lax

D = 1024
FF = 4096
HEADS = 8
HD = 128
GROUP = 64
ROUNDS = 4
LAYERS = 2
SEQ_LEN = 4096
SEQS = 2
ROWS_SEQ = 256
PAIR_ROWS = 16
N_WIDE = 16


def draw_bucket_perm(key, part):
    key = jax.random.fold_in(key, 7)

    def one_block(block_key):
        source_key, slot_key = jax.random.split(block_key)
        row_orders = jax.vmap(lambda subkey: jax.random.permutation(subkey, ROWS_SEQ))(jax.random.split(source_key, N_WIDE))
        slot_orders = jax.vmap(lambda subkey: jax.random.permutation(subkey, ROWS_SEQ))(jax.random.split(slot_key, N_WIDE))
        incoming = jnp.arange(ROWS_SEQ, dtype=jnp.int32)
        sources = incoming // PAIR_ROWS
        rank_of = incoming % PAIR_ROWS
        owners = jnp.arange(N_WIDE, dtype=jnp.int32)[:, None]
        chosen = sources[None, :] * ROWS_SEQ + row_orders[sources[None, :], owners * PAIR_ROWS + rank_of[None, :]]
        placed = jnp.zeros((N_WIDE, ROWS_SEQ), jnp.int32).at[owners, slot_orders].set(chosen.astype(jnp.int32))
        return placed.reshape(SEQ_LEN)
    blocks = jax.vmap(one_block)(jax.random.split(key, ROUNDS * SEQS))
    return blocks.reshape(ROUNDS, SEQS, SEQ_LEN).astype(jnp.int32)


def steps_of(own_key, dims, pieces, low, largest):
    level = 1.0
    for dim, parts in pieces:
        heights = jax.random.uniform(jax.random.fold_in(jax.random.fold_in(own_key, 6), dim), (parts,), jnp.float32, low / len(pieces), largest / len(pieces))
        level = level * jnp.repeat(jnp.exp(heights), dims[dim] // parts).reshape((-1,) + (1,) * (len(dims) - 1 - dim))
    return level


def noise(rng, shape, width, most, shards=(), kind=jnp.bfloat16):
    array = jax.random.normal(rng, shape, jnp.float32) * width
    if len(shards) > 0:
        array = steps_of(rng, shape, shards, -0.22, 0.18) * array
    return jnp.clip(array, min=-most, max=most).astype(kind)


def setup_inputs(seed: int = 0) -> dict:
    streams_of = jax.random.split(jax.random.key(seed), 18)
    return {
        "first_in": noise(streams_of[0], (SEQS, SEQ_LEN, D), 1.0, 6.0, ((1, 16), (2, 2)), jnp.float32),
        "second_in": noise(streams_of[1], (SEQS, SEQ_LEN, D), 1.0, 6.0, ((1, 16), (2, 2)), jnp.float32),
        "attn_norm_gain": jnp.clip(1.0 + 0.1 * jax.random.normal(streams_of[2], (LAYERS, D), jnp.float32), 0.5, 1.5),
        "attn_norm_bias": noise(streams_of[3], (LAYERS, D), 0.2, 1.0, (), jnp.float32),
        "qk_weight": noise(streams_of[4], (LAYERS, D, D), D ** -0.5, 0.1875, ((1, 16), (2, 2))),
        "value_weight": noise(streams_of[5], (LAYERS, D, D), D ** -0.5, 0.1875, ((1, 16), (2, 2))),
        "out_weight": noise(streams_of[6], (LAYERS, D, D), (D // 16) ** -0.5, 0.75, ((1, 16), (2, 2))),
        "out_bias": noise(streams_of[7], (LAYERS, D), 0.2, 1.0, ((1, 2),), jnp.float32),
        "ffn_norm_gain": jnp.clip(1.0 + 0.1 * jax.random.normal(streams_of[8], (LAYERS, D), jnp.float32), 0.5, 1.5),
        "ffn_norm_bias": noise(streams_of[9], (LAYERS, D), 0.2, 1.0, (), jnp.float32),
        "up_weight": noise(streams_of[10], (LAYERS, D, FF), D ** -0.5, 0.1875, ((2, 2),)),
        "up_bias": noise(streams_of[11], (LAYERS, FF), 0.5, 2.5, ((1, 2),), jnp.float32),
        "down_weight": noise(streams_of[12], (LAYERS, D, FF), (FF // 2) ** -0.5, 0.125, ((2, 2),)),
        "down_bias": noise(streams_of[13], (LAYERS, D), 0.2, 1.0, ((1, 2),), jnp.float32),
        "bucket_perm": draw_bucket_perm(jax.random.fold_in(streams_of[17], 71), 0),
        "first_cot": noise(streams_of[15], (SEQS, SEQ_LEN, D), 1.0, 6.0, ((1, 16), (2, 2)), jnp.float32),
        "second_cot": noise(streams_of[16], (SEQS, SEQ_LEN, D), 1.0, 6.0, ((1, 16), (2, 2)), jnp.float32),
    }


@jax.custom_vjp
def low(v):
    return lax.optimization_barrier(v.astype(jnp.bfloat16)).astype(jnp.float32)

@jax.custom_vjp
def low_back(v):
    return v

def low_keep(v):
    return (low(v), None)

def low_pass(kept, grad):
    return (grad,)

def back_keep(v):
    return (v, None)

def back_low(kept, grad):
    return (low(grad),)
low.defvjp(low_keep, low_pass)
low_back.defvjp(back_keep, back_low)

def layer_norm(stream, gain, shift):
    centre = stream - lax.optimization_barrier(jnp.mean(stream, axis=-1, keepdims=True))
    spread = lax.optimization_barrier(jnp.mean(centre * centre, axis=-1, keepdims=True))
    return centre * lax.rsqrt(spread + 1e-05) * gain + shift

def unit_keys(raw_rows):
    return raw_rows * lax.rsqrt(lax.optimization_barrier(jnp.mean(raw_rows * raw_rows, axis=-1, keepdims=True)) + 1e-06)

def project(inputs, weight):
    return jnp.einsum('slj,jk->slk', inputs, weight, precision=lax.Precision.HIGHEST)

def project_back(inputs, weight):
    return jnp.einsum('slk,jk->slj', inputs, weight, precision=lax.Precision.HIGHEST)

def self_mask():
    return jnp.arange(GROUP)[:, None] + GROUP == jnp.arange(2 * GROUP)[None, :]

def lsh_sequence(members):
    queries, values, perm = members
    round_count = perm.shape[0]
    bucket_queries = low_back(queries[perm])
    bucket_values = low_back(values[perm])
    block_shape = (round_count, SEQ_LEN // GROUP, GROUP, HEADS, HD)
    query_blocks = bucket_queries.reshape(block_shape)
    value_blocks = bucket_values.reshape(block_shape)
    key_blocks = low(unit_keys(query_blocks))
    key_window = jnp.concatenate([jnp.roll(key_blocks, 1, axis=1), key_blocks], axis=2)
    value_window = jnp.concatenate([jnp.roll(value_blocks, 1, axis=1), value_blocks], axis=2)
    raw_scores = jnp.einsum('rcqhd,rckhd->rchqk', query_blocks, key_window, precision=lax.Precision.HIGHEST)
    raw_scores = low_back(raw_scores * HD ** (-0.5))
    scores = jnp.where(self_mask(), -1000000000.0, raw_scores)
    row_top = lax.optimization_barrier(jnp.max(scores, axis=-1, keepdims=True))
    log_total = row_top[..., 0] + jnp.log(lax.optimization_barrier(jnp.sum(jnp.exp(scores - row_top), axis=-1)))
    probs = jnp.exp(scores - log_total[..., None])
    round_out = jnp.einsum('rchqk,rckhd->rcqhd', low(probs), value_window, precision=lax.Precision.HIGHEST)
    round_out = low(low_back(round_out)).reshape(round_count, SEQ_LEN, HEADS * HD)
    log_rows = jnp.transpose(log_total, (0, 1, 3, 2)).reshape(round_count, SEQ_LEN, HEADS)
    round_idx = jnp.arange(round_count)[:, None]
    out_tokens = jnp.zeros((round_count, SEQ_LEN, HEADS * HD), jnp.float32).at[round_idx, perm].set(round_out)
    log_tokens = jnp.zeros((round_count, SEQ_LEN, HEADS), jnp.float32).at[round_idx, perm].set(log_rows)
    round_top = lax.optimization_barrier(jnp.max(log_tokens, axis=0, keepdims=True))
    round_weights = jnp.exp(log_tokens - round_top)
    round_weights = round_weights / lax.optimization_barrier(jnp.sum(round_weights, axis=0, keepdims=True))
    mixed = lax.optimization_barrier(jnp.sum(round_weights[..., None] * out_tokens.reshape(round_count, SEQ_LEN, HEADS, HD), axis=0))
    return mixed.reshape(SEQ_LEN, HEADS * HD)

def forward(first_stream, second_stream, attn_norm_gain, attn_norm_bias, qk_weight, value_weight, out_weight, out_bias, ffn_norm_gain, ffn_norm_bias, up_weight, up_bias, down_weight, down_bias, perm_by_seq):
    for layer_index in range(LAYERS):
        normed = low(layer_norm(second_stream, attn_norm_gain[layer_index], attn_norm_bias[layer_index]))
        queries = low(low_back(project(normed, qk_weight[layer_index])))
        values = low(low_back(project(normed, value_weight[layer_index])))
        mixed = lax.map(jax.checkpoint(lsh_sequence), (queries, values, perm_by_seq))
        attn = low(mixed)
        first_stream = first_stream + low_back(project_back(attn, out_weight[layer_index])) + out_bias[layer_index]
        ffn_in = low(layer_norm(first_stream, ffn_norm_gain[layer_index], ffn_norm_bias[layer_index]))
        pre_act = low_back(project(ffn_in, up_weight[layer_index])) + up_bias[layer_index]
        hidden = low(jax.nn.gelu(pre_act, approximate=True))
        second_stream = second_stream + low_back(project_back(hidden, down_weight[layer_index])) + down_bias[layer_index]
    return (first_stream, second_stream)

def reference(first_in, second_in, attn_norm_gain, attn_norm_bias, qk_weight, value_weight, out_weight, out_bias, ffn_norm_gain, ffn_norm_bias, up_weight, up_bias, down_weight, down_bias, bucket_perm, first_cot, second_cot):
    floats = tuple((member.astype(jnp.float32) for member in (first_in, second_in, attn_norm_gain, attn_norm_bias, qk_weight, value_weight, out_weight, out_bias, ffn_norm_gain, ffn_norm_bias, up_weight, up_bias, down_weight, down_bias)))
    perm_by_seq = jnp.transpose(bucket_perm, (1, 0, 2)).astype(jnp.int32)

    def run_layers(*members):
        return forward(*members, perm_by_seq)
    outputs, pullback = jax.vjp(run_layers, *floats)
    gradients = pullback((first_cot.astype(jnp.float32), second_cot.astype(jnp.float32)))
    return (outputs[0], outputs[1], gradients[0], gradients[1], gradients[2], gradients[3], gradients[4], gradients[5], gradients[6], gradients[7], gradients[8], gradients[9], gradients[10], gradients[11], gradients[12], gradients[13])
```

```python
import functools

import jax
import jax.numpy as jnp
from jax import lax
from jax.experimental import pallas as pl
from jax.experimental.pallas import tpu as pltpu
from jax.sharding import PartitionSpec as P

HD = 128
GROUP = 64
ROUNDS = 4
LAYERS = 2
BLOCK = 256
F32 = jnp.float32
BF16 = jnp.bfloat16
SCALE = HD ** (-0.5)
VMEM_LIMIT = 56 * 1024 * 1024


def swap(value, axis, mask):
    count = lax.axis_size(axis)
    return lax.ppermute(value, axis, [(source, source ^ mask) for source in range(count)])


def dot(left, right, dims):
    return lax.dot_general(left, right, (dims, ((), ())), preferred_element_type=F32)


def mm(left, right):
    return dot(left, right, ((1,), (0,)))


def mm_t(left, right):
    return dot(left, right, ((1,), (1,)))


def t_mm(left, right):
    return dot(left, right, ((0,), (0,)))


def chip_exchange(slots):
    return [slots[0]] + [swap(slots[k], "wide", 2 * k) for k in range(1, len(slots))]


def split3(value):
    high = value.astype(BF16)
    rest = value - high.astype(F32)
    mid = rest.astype(BF16)
    low = (rest - mid.astype(F32)).astype(BF16)
    return high.astype(F32), mid.astype(F32), low.astype(F32)


def exact_split3(value):
    high = lax.reduce_precision(value, 8, 7)
    mid = lax.reduce_precision(value - high, 8, 7)
    low = lax.reduce_precision(value - high - mid, 8, 7)
    return high, mid, low


def layer_norm(stream, gain, shift):
    centre = stream - jnp.mean(stream, axis=-1, keepdims=True)
    spread = jnp.mean(centre * centre, axis=-1, keepdims=True)
    return centre * lax.rsqrt(spread + 1e-05) * gain + shift


def layer_norm_back(stream, gain, grad):
    centre = stream - jnp.mean(stream, axis=-1, keepdims=True)
    inv = lax.rsqrt(jnp.mean(centre * centre, axis=-1, keepdims=True) + 1e-05)
    unit = centre * inv
    scaled = grad * gain
    back = inv * (
        scaled
        - jnp.mean(scaled, axis=-1, keepdims=True)
        - unit * jnp.mean(scaled * unit, axis=-1, keepdims=True)
    )
    return back, unit


def build_tables(tokens):
    rounds, seq = tokens.shape
    blocks = seq // BLOCK
    rank_rows = BLOCK // blocks
    tokens = tokens.reshape(rounds, blocks, BLOCK)
    run = tokens // BLOCK
    row = tokens % BLOCK
    onehot = (run[..., None] == jnp.arange(blocks, dtype=jnp.int32)).astype(BF16)
    before = (jnp.arange(BLOCK)[:, None] > jnp.arange(BLOCK)[None, :]).astype(BF16)
    counts = jnp.einsum("jl,rkla->rkja", before, onehot, preferred_element_type=F32)
    rank = jnp.sum(onehot.astype(F32) * counts, axis=-1).astype(jnp.int32)
    slot = run * rank_rows + rank
    iota = jnp.arange(BLOCK, dtype=jnp.int32)
    into = (slot[..., None] == iota).astype(BF16)
    into_t = (slot[..., None, :] == iota[:, None]).astype(BF16)
    wants = jnp.einsum("rknj,rkj->rkn", into_t, row.astype(BF16), preferred_element_type=F32)
    wants = wants.reshape(rounds, blocks, blocks, rank_rows)
    wants = jnp.transpose(wants, (0, 2, 1, 3)).reshape(rounds, blocks, BLOCK).astype(jnp.int32)
    out_of = (wants[..., None] == iota).astype(BF16)
    out_of_t = (wants[..., None, :] == iota[:, None]).astype(BF16)
    return out_of, into, out_of_t, into_t


def load_tokens(pos_ref, own_ref, sib_ref, tok, sems, slots, rows):
    chip, core = pos_ref[0], pos_ref[1]
    copies = []
    for k in range(slots):
        other = chip ^ k
        for half, source in ((0, own_ref), (1, sib_ref)):
            start = pl.multiple_of((2 * other + (core ^ half)) * rows, rows)
            copies.append(
                pltpu.make_async_copy(
                    source.at[k], tok.at[pl.ds(start, rows)], sems.at[2 * k + half]
                )
            )
    for copy in copies:
        copy.start()
    for copy in copies:
        copy.wait()


def store_run(pos_ref, out_ref, run, value, rows):
    chip, core = pos_ref[0], pos_ref[1]
    for part in range(BLOCK // rows):
        device = run * (BLOCK // rows) + part
        out_ref[(device & 1) ^ core, (device >> 1) ^ chip] = value[part * rows : (part + 1) * rows]


def permute_in(tok, out_of, mixed, blocks):
    def body(a, carry):
        source = tok[pl.ds(pl.multiple_of(a * BLOCK, BLOCK), BLOCK), :]
        moved = mm(out_of[0, a], source).astype(BF16)
        mixed[:, a] = moved.reshape(blocks, BLOCK // blocks, 2 * HD)
        return carry

    lax.fori_loop(0, blocks, body, 0)


def self_mask():
    row = lax.broadcasted_iota(jnp.int32, (GROUP, 2 * GROUP), 0)
    col = lax.broadcasted_iota(jnp.int32, (GROUP, 2 * GROUP), 1)
    return col == row + GROUP


def forward_kernel(
    slots, rows, pos_ref, own_ref, sib_ref, out_of, into, out_of_t, into_t,
    sorted_ref, mix_ref, tok, mixed, keys, vals, first_out, first_lse, sems,
):
    seq = tok.shape[0]
    blocks = seq // BLOCK
    step = pl.program_id(0)

    @pl.when(step == 0)
    def _():
        load_tokens(pos_ref, own_ref, sib_ref, tok, sems, slots, rows)

    permute_in(tok, out_of, mixed, blocks)

    def place(k, carry):
        base = pl.multiple_of(k * BLOCK, BLOCK)
        rows_sorted = mm(into[0, k], mixed[k].reshape(BLOCK, 2 * HD))
        sorted_ref[0, pl.ds(base, BLOCK), :] = rows_sorted.astype(BF16)
        query = rows_sorted[:, :HD]
        unit = query * lax.rsqrt(jnp.mean(query * query, axis=-1, keepdims=True) + 1e-06)
        where = pl.ds(pl.multiple_of(base + GROUP, GROUP), BLOCK)
        keys[where, :] = unit.astype(BF16)
        vals[where, :] = rows_sorted[:, HD:].astype(BF16)
        return carry

    lax.fori_loop(0, blocks, place, 0)
    keys[0:GROUP, :] = keys[seq : seq + GROUP, :]
    vals[0:GROUP, :] = vals[seq : seq + GROUP, :]

    def attend(k, carry):
        lane = lax.broadcasted_iota(jnp.int32, (GROUP, HD), 1)
        own = self_mask()
        pieces = []
        for b in range(BLOCK // GROUP):
            base = pl.multiple_of(k * BLOCK + b * GROUP, GROUP)
            query = sorted_ref[0, pl.ds(base, GROUP), 0:HD]
            window = pl.ds(base, 2 * GROUP)
            scores = jnp.where(own, -1000000000.0, mm_t(query, keys[window, :]) * SCALE)
            top = jnp.max(scores, axis=-1, keepdims=True)
            weight = jnp.exp(scores - top)
            total = jnp.sum(weight, axis=-1, keepdims=True)
            result = mm(weight.astype(BF16), vals[window, :]) / total
            high, mid, low = split3(top + jnp.log(total))
            extra = jnp.where(
                lane == 0, high, jnp.where(lane == 1, mid, jnp.where(lane == 2, low, 0.0))
            )
            pieces.append(jnp.concatenate([result, extra], axis=1).astype(BF16))
        packed = jnp.concatenate(pieces, axis=0)
        back = mm(into_t[0, k], packed).astype(BF16)
        mixed[k] = back.reshape(blocks, BLOCK // blocks, 2 * HD)
        return carry

    lax.fori_loop(0, blocks, attend, 0)

    def back_tokens(a):
        source = mixed[:, a].reshape(BLOCK, 2 * HD)
        moved = mm(out_of_t[0, a], source)
        return moved[:, :HD], jnp.sum(moved[:, HD:], axis=-1, keepdims=True)

    @pl.when(step == 0)
    def _():
        def body(a, carry):
            where = pl.ds(pl.multiple_of(a * BLOCK, BLOCK), BLOCK)
            value, lse = back_tokens(a)
            first_out[where, :] = value
            first_lse[where, :] = jnp.broadcast_to(lse, (BLOCK, HD))
            return carry

        lax.fori_loop(0, blocks, body, 0)

    @pl.when(step == 1)
    def _():
        def body(a, carry):
            where = pl.ds(pl.multiple_of(a * BLOCK, BLOCK), BLOCK)
            value, lse = back_tokens(a)
            lse_a = first_lse[where, :]
            top = jnp.maximum(lse_a, lse)
            both = top + jnp.log(jnp.exp(lse_a - top) + jnp.exp(lse - top))
            value = first_out[where, :] * jnp.exp(lse_a - both) + value * jnp.exp(lse - both)
            high, mid, low = split3(both)
            lane = lax.broadcasted_iota(jnp.int32, (BLOCK, HD), 1)
            extra = jnp.where(
                lane == 0, high, jnp.where(lane == 1, mid, jnp.where(lane == 2, low, 0.0))
            )
            packed = jnp.concatenate([value, extra], axis=1).astype(BF16)
            store_run(pos_ref, mix_ref, a, packed, rows)
            return carry

        lax.fori_loop(0, blocks, body, 0)


def backward_kernel(
    slots, rows, pos_ref, own_ref, sib_ref, sorted_ref, out_of, into, out_of_t, into_t,
    out_ref, tok, mixed, keys, vals, grads, query_use, key_grad, val_grad, acc, sems,
):
    seq = tok.shape[0]
    blocks = seq // BLOCK
    step = pl.program_id(0)

    @pl.when(step == 0)
    def _():
        load_tokens(pos_ref, own_ref, sib_ref, tok, sems, slots, rows)

    permute_in(tok, out_of, mixed, blocks)

    def place(k, carry):
        base = pl.multiple_of(k * BLOCK, BLOCK)
        grads[pl.ds(base, BLOCK), :] = mm(
            into[0, k], mixed[k].reshape(BLOCK, 2 * HD)
        ).astype(BF16)
        query = sorted_ref[0, pl.ds(base, BLOCK), 0:HD].astype(F32)
        unit = query * lax.rsqrt(jnp.mean(query * query, axis=-1, keepdims=True) + 1e-06)
        where = pl.ds(pl.multiple_of(base + GROUP, GROUP), BLOCK)
        keys[where, :] = unit.astype(BF16)
        vals[where, :] = sorted_ref[0, pl.ds(base, BLOCK), HD:]
        return carry

    lax.fori_loop(0, blocks, place, 0)
    keys[0:GROUP, :] = keys[seq : seq + GROUP, :]
    vals[0:GROUP, :] = vals[seq : seq + GROUP, :]
    key_grad[0:GROUP, :] = jnp.zeros((GROUP, HD), F32)
    val_grad[0:GROUP, :] = jnp.zeros((GROUP, HD), F32)

    def attend(k, carry):
        lane = lax.broadcasted_iota(jnp.int32, (GROUP, HD), 1)
        own = self_mask()
        for b in range(BLOCK // GROUP):
            base = pl.multiple_of(k * BLOCK + b * GROUP, GROUP)
            here = pl.ds(base, GROUP)
            window = pl.ds(base, 2 * GROUP)
            later = pl.ds(pl.multiple_of(base + GROUP, GROUP), GROUP)
            query = sorted_ref[0, here, 0:HD]
            grad = grads[here, 0:HD]
            stats = grads[here, HD:].astype(F32)
            delta = jnp.sum(jnp.where(lane < 3, stats, 0.0), axis=-1, keepdims=True)
            lse = jnp.sum(jnp.where(lane >= 3, stats, 0.0), axis=-1, keepdims=True)
            key = keys[window, :]
            scores = jnp.where(own, -1000000000.0, mm_t(query, key) * SCALE)
            probs = jnp.exp(scores - lse)
            prob_grad = mm_t(grad, vals[window, :])
            score_grad = (probs * (prob_grad - delta)).astype(BF16)
            query_use[here, :] = mm(score_grad, key) * SCALE
            key_part = t_mm(score_grad, query) * SCALE
            val_part = t_mm(probs.astype(BF16), grad)
            key_grad[here, :] += key_part[:GROUP]
            val_grad[here, :] += val_part[:GROUP]
            key_grad[later, :] = key_part[GROUP:]
            val_grad[later, :] = val_part[GROUP:]
        return carry

    lax.fori_loop(0, blocks, attend, 0)
    key_grad[seq : seq + GROUP, :] += key_grad[0:GROUP, :]
    val_grad[seq : seq + GROUP, :] += val_grad[0:GROUP, :]

    def gather_back(k, carry):
        base = pl.multiple_of(k * BLOCK, BLOCK)
        where = pl.ds(pl.multiple_of(base + GROUP, GROUP), BLOCK)
        query = sorted_ref[0, pl.ds(base, BLOCK), 0:HD].astype(F32)
        inv = lax.rsqrt(jnp.mean(query * query, axis=-1, keepdims=True) + 1e-06)
        grad = key_grad[where, :]
        inner = jnp.mean(grad * query, axis=-1, keepdims=True)
        total = query_use[pl.ds(base, BLOCK), :] + inv * (grad - query * (inner * inv * inv))
        packed = jnp.concatenate([total, val_grad[where, :]], axis=1).astype(BF16)
        back = mm(into_t[0, k], packed).astype(BF16)
        mixed[k] = back.reshape(blocks, BLOCK // blocks, 2 * HD)
        return carry

    lax.fori_loop(0, blocks, gather_back, 0)

    @pl.when(step == 0)
    def _():
        def body(a, carry):
            where = pl.ds(pl.multiple_of(a * BLOCK, BLOCK), BLOCK)
            acc[where, :] = mm(out_of_t[0, a], mixed[:, a].reshape(BLOCK, 2 * HD))
            return carry

        lax.fori_loop(0, blocks, body, 0)

    @pl.when(step == 1)
    def _():
        def body(a, carry):
            where = pl.ds(pl.multiple_of(a * BLOCK, BLOCK), BLOCK)
            total = acc[where, :] + mm(out_of_t[0, a], mixed[:, a].reshape(BLOCK, 2 * HD))
            store_run(pos_ref, out_ref, a, total.astype(BF16), rows)
            return carry

        lax.fori_loop(0, blocks, body, 0)


def table_specs(blocks):
    return [pl.BlockSpec((1, blocks, BLOCK, BLOCK), lambda r: (r, 0, 0, 0))] * 4


def params():
    return pltpu.CompilerParams(vmem_limit_bytes=VMEM_LIMIT)


def attention_forward(pos, own, sib, tables):
    slots, rows, width = own.shape
    seq = 2 * slots * rows
    blocks = seq // BLOCK
    return pl.pallas_call(
        functools.partial(forward_kernel, slots, rows),
        grid=(2,),
        out_shape=(
            jax.ShapeDtypeStruct((2, seq, width), BF16),
            jax.ShapeDtypeStruct((2, slots, rows, width), BF16),
        ),
        in_specs=[pl.BlockSpec(memory_space=pltpu.SMEM)]
        + [pl.BlockSpec(memory_space=pl.ANY)] * 2
        + table_specs(blocks),
        out_specs=(
            pl.BlockSpec((1, seq, width), lambda r: (r, 0, 0)),
            pl.BlockSpec((2, slots, rows, width), lambda r: (0, 0, 0, 0)),
        ),
        scratch_shapes=[
            pltpu.VMEM((seq, width), BF16),
            pltpu.VMEM((blocks, blocks, BLOCK // blocks, width), BF16),
            pltpu.VMEM((seq + GROUP, HD), BF16),
            pltpu.VMEM((seq + GROUP, HD), BF16),
            pltpu.VMEM((seq, HD), F32),
            pltpu.VMEM((seq, HD), F32),
            pltpu.SemaphoreType.DMA((2 * slots,)),
        ],
        compiler_params=params(),
        name="attend_forward",
    )(pos, own, sib, *tables)


def attention_backward(pos, own, sib, sorted_rows, tables):
    slots, rows, width = own.shape
    seq = 2 * slots * rows
    blocks = seq // BLOCK
    return pl.pallas_call(
        functools.partial(backward_kernel, slots, rows),
        grid=(2,),
        out_shape=jax.ShapeDtypeStruct((2, slots, rows, width), BF16),
        in_specs=[pl.BlockSpec(memory_space=pltpu.SMEM)]
        + [pl.BlockSpec(memory_space=pl.ANY)] * 2
        + [pl.BlockSpec((1, seq, width), lambda r: (r, 0, 0))]
        + table_specs(blocks),
        out_specs=pl.BlockSpec((2, slots, rows, width), lambda r: (0, 0, 0, 0)),
        scratch_shapes=[
            pltpu.VMEM((seq, width), BF16),
            pltpu.VMEM((blocks, blocks, BLOCK // blocks, width), BF16),
            pltpu.VMEM((seq + GROUP, HD), BF16),
            pltpu.VMEM((seq + GROUP, HD), BF16),
            pltpu.VMEM((seq, width), BF16),
            pltpu.VMEM((seq, HD), F32),
            pltpu.VMEM((seq + GROUP, HD), F32),
            pltpu.VMEM((seq + GROUP, HD), F32),
            pltpu.VMEM((seq, width), F32),
            pltpu.SemaphoreType.DMA((2 * slots,)),
        ],
        compiler_params=params(),
        name="attend_backward",
    )(pos, own, sib, sorted_rows, *tables)


def project_kernel(slots, rows, heads, pos_ref, normed_ref, weight_ref, *out_refs):
    for k in range(slots):
        unit = pos_ref[0] ^ k
        start = pl.multiple_of((unit // heads) * rows, rows)
        value = mm(normed_ref[pl.ds(start, rows), :], weight_ref[unit % heads])
        out_refs[k][...] = value.astype(BF16)


def project_units(pos, normed, weight, rows):
    heads, _, width = weight.shape
    slots = normed.shape[0] // rows * heads
    return pl.pallas_call(
        functools.partial(project_kernel, slots, rows, heads),
        out_shape=[jax.ShapeDtypeStruct((rows, width), BF16)] * slots,
        in_specs=[pl.BlockSpec(memory_space=pltpu.SMEM)]
        + [pl.BlockSpec(memory_space=pltpu.VMEM)] * 2,
        out_specs=[pl.BlockSpec(memory_space=pltpu.VMEM)] * slots,
        compiler_params=params(),
        name="project_units",
    )(pos, normed, weight)


def merge_kernel(slots, rows, heads, pos_ref, weight_ref, *refs):
    ins, (part_ref, tok_ref) = refs[:slots], refs[slots:]
    width = ins[0].shape[1]
    for k in range(slots):
        unit = pos_ref[0] ^ k
        start = pl.multiple_of((unit // heads) * rows, rows)
        lane = pl.multiple_of((unit % heads) * width, width)
        tok_ref[pl.ds(start, rows), pl.ds(lane, width)] = ins[k][...]
    part_ref[...] = mm_t(tok_ref[...], weight_ref[...]).astype(BF16)


def merge_units(pos, pieces, weight, seqs):
    slots = len(pieces)
    rows, width = pieces[0].shape
    heads = slots // seqs
    return pl.pallas_call(
        functools.partial(merge_kernel, slots, rows, heads),
        out_shape=(
            jax.ShapeDtypeStruct((seqs * rows, weight.shape[0]), BF16),
            jax.ShapeDtypeStruct((seqs * rows, heads * width), BF16),
        ),
        in_specs=[pl.BlockSpec(memory_space=pltpu.SMEM)]
        + [pl.BlockSpec(memory_space=pltpu.VMEM)] * (1 + slots),
        out_specs=(
            pl.BlockSpec(memory_space=pltpu.VMEM),
            pl.BlockSpec(memory_space=pltpu.VMEM),
        ),
        compiler_params=params(),
        name="merge_units",
    )(pos, weight, *pieces)


def reduce_rows(value):
    count = lax.axis_size("wide")
    index = lax.axis_index("wide")
    width = value.shape[1]
    block = value.shape[0] // count
    value = value.astype(BF16)
    bit = 1
    parts = count
    while bit < count:
        view = value.reshape(parts // 2, 2, block, width)
        mine = (index // bit) % 2
        sent = lax.dynamic_index_in_dim(view, 1 - mine, 1, keepdims=False)
        kept = lax.dynamic_index_in_dim(view, mine, 1, keepdims=False)
        value = kept.astype(F32) + swap(sent, "wide", bit).astype(F32)
        parts //= 2
        bit *= 2
        if bit < count:
            value = value.astype(BF16)
    return value.reshape(block, width)


def sum_all(value):
    for bit in range(lax.axis_size("wide").bit_length() - 1):
        value = value + swap(value, "wide", 1 << bit)
    return value + swap(value, "narrow", 1)


def shards(
    first_in, second_in, attn_norm_gain, attn_norm_bias, qk_weight, value_weight, out_weight,
    out_bias, ffn_norm_gain, ffn_norm_bias, up_weight, up_bias, down_weight, down_bias,
    bucket_perm, first_cot, second_cot,
):
    seqs, rows, half = first_in.shape
    toks = seqs * rows
    wide = lax.axis_size("wide")
    wide_index = lax.axis_index("wide")
    narrow_index = lax.axis_index("narrow")
    chip, core = wide_index // 2, wide_index % 2
    pos = jnp.stack([chip, core]).astype(jnp.int32)
    weight_rows, head_width = qk_weight.shape[1:]
    heads = head_width // HD
    width = 2 * half

    def whole(mine, other):
        other = other.astype(mine.dtype)
        return jnp.where(
            narrow_index == 0,
            jnp.concatenate([mine, other], axis=-1),
            jnp.concatenate([other, mine], axis=-1),
        )

    def widen(mine):
        return whole(mine, swap(mine.astype(BF16), "narrow", 1))

    def own_half(full):
        return lax.dynamic_slice_in_dim(full, narrow_index * half, half, full.ndim - 1)

    second = widen(second_in.reshape(toks, half))
    first = widen(first_in.reshape(toks, half))
    grad_second = widen(second_cot.reshape(toks, half))
    grad_first = widen(first_cot.reshape(toks, half))
    out_bias = whole(out_bias, swap(out_bias, "narrow", 1))
    down_bias = whole(down_bias, swap(down_bias, "narrow", 1))

    perm_parts = bucket_perm.reshape(2, ROUNDS // 2, seqs, rows)
    target = jnp.arange(wide)
    perm_send = jnp.transpose(perm_parts, (2, 0, 1, 3))
    perm_send = jnp.broadcast_to(
        perm_send[:, None], (seqs, heads, 2, ROUNDS // 2, rows)
    ).reshape(wide, ROUNDS // 2, rows)
    perm_got = lax.all_to_all(perm_send, "wide", 0, 0, tiled=True)
    tables = build_tables(jnp.transpose(perm_got, (1, 0, 2)).reshape(ROUNDS // 2, wide * rows))

    gathered = lax.all_gather(
        jnp.stack([qk_weight, value_weight, out_weight]), "wide", axis=0
    )

    def unit_weight(layer):
        pair = gathered[:, 0:2, layer].reshape(wide, 2, weight_rows, heads, HD)
        return jnp.transpose(pair, (3, 0, 2, 1, 4)).reshape(heads, wide * weight_rows, 2 * HD)

    unit_weights = [unit_weight(layer) for layer in range(LAYERS)]
    out_weights = [
        gathered[:, 2, layer].reshape(wide * weight_rows, head_width) for layer in range(LAYERS)
    ]
    saved = []
    for layer in range(LAYERS):
        normed = layer_norm(second, attn_norm_gain[layer], attn_norm_bias[layer]).astype(BF16)
        pieces = project_units(pos, normed, unit_weights[layer], rows)
        own = jnp.stack(chip_exchange(pieces))
        sib = swap(own, "wide", 1)
        sorted_rows, mix = attention_forward(pos, own, sib, tables)
        got = swap(mix[1], "wide", 1)
        lse_a = jnp.sum(mix[0, :, :, HD:].astype(F32), axis=-1, keepdims=True)
        lse_b = jnp.sum(got[:, :, HD:].astype(F32), axis=-1, keepdims=True)
        top = jnp.maximum(lse_a, lse_b)
        lse = top + jnp.log(jnp.exp(lse_a - top) + jnp.exp(lse_b - top))
        attn = mix[0, :, :, :HD].astype(F32) * jnp.exp(lse_a - lse) + got[:, :, :HD].astype(
            F32
        ) * jnp.exp(lse_b - lse)
        attn_low = attn.astype(BF16)
        back = chip_exchange([attn_low[k] for k in range(wide // 2)])
        part, attn_tok = merge_units(pos, back, out_weights[layer], seqs)
        other = swap(part, "narrow", 1)
        first = first + (part.astype(F32) + other.astype(F32)) + out_bias[layer]
        ffn_in = layer_norm(first, ffn_norm_gain[layer], ffn_norm_bias[layer]).astype(BF16)
        pre_act = mm(ffn_in, up_weight[layer]) + up_bias[layer]
        hidden = jax.nn.gelu(pre_act, approximate=True).astype(BF16)
        part = mm_t(hidden, down_weight[layer]).astype(BF16)
        other = swap(part, "narrow", 1)
        saved.append((second, normed, sorted_rows, attn, lse, attn_tok, first, ffn_in, pre_act, hidden))
        second = second + (part.astype(F32) + other.astype(F32)) + down_bias[layer]
    first_out, second_out = own_half(first), own_half(second)

    weight_grads = [None] * LAYERS
    small_grads = [None] * LAYERS
    for layer in reversed(range(LAYERS)):
        second_l, normed, sorted_rows, attn, lse, attn_tok, first_l, ffn_in, pre_act, hidden = saved[layer]
        branch = grad_second.astype(BF16)
        down_bias_grad = jnp.sum(own_half(grad_second), axis=0)
        hidden_grad = mm(branch, down_weight[layer])
        pre_grad = jax.vjp(lambda u: jax.nn.gelu(u, approximate=True), pre_act)[1](hidden_grad)[0]
        up_bias_grad = jnp.sum(pre_grad, axis=0)
        pre_low = pre_grad.astype(BF16)
        part = mm_t(pre_low, up_weight[layer]).astype(BF16)
        other = swap(part, "narrow", 1)
        down_weight_grad = reduce_rows(t_mm(branch, hidden))
        up_weight_grad = reduce_rows(t_mm(ffn_in, pre_low))
        ffn_in_grad = part.astype(F32) + other.astype(F32)
        stream_part, unit = layer_norm_back(first_l, ffn_norm_gain[layer], ffn_in_grad)
        ffn_gain_grad = jnp.sum(own_half(ffn_in_grad * unit), axis=0)
        ffn_bias_grad = jnp.sum(own_half(ffn_in_grad), axis=0)
        grad_first = grad_first + stream_part
        out_low = grad_first.astype(BF16)
        out_bias_grad = jnp.sum(own_half(grad_first), axis=0)
        by_head = jnp.transpose(out_weights[layer].reshape(width, heads, HD), (1, 0, 2))
        pieces = project_units(pos, out_low, by_head, rows)
        attn_grad = jnp.stack(chip_exchange(pieces))
        delta = jnp.sum(attn * attn_grad.astype(F32), axis=-1, keepdims=True)
        lane = jnp.arange(HD)
        extra = jnp.zeros(attn.shape, F32)
        for place, column in enumerate(exact_split3(delta) + exact_split3(lse)):
            extra = jnp.where(lane == place, column, extra)
        own = jnp.concatenate([attn_grad, extra.astype(BF16)], axis=-1)
        sib = swap(own, "wide", 1)
        grads = attention_backward(pos, own, sib, sorted_rows, tables)
        total = grads[0].astype(F32) + swap(grads[1], "wide", 1).astype(F32)
        total = total.astype(BF16)
        back = chip_exchange([total[k] for k in range(wide // 2)])
        flat = jnp.transpose(unit_weights[layer], (1, 0, 2)).reshape(width, heads * 2 * HD)
        part, grad_tok = merge_units(pos, back, flat, seqs)
        other = swap(part, "narrow", 1)
        out_weight_grad = reduce_rows(t_mm(out_low, attn_tok))
        unit_weight_grad = reduce_rows(t_mm(normed, grad_tok))
        normed_grad = part.astype(F32) + other.astype(F32)
        stream_part, unit = layer_norm_back(second_l, attn_norm_gain[layer], normed_grad)
        attn_gain_grad = jnp.sum(own_half(normed_grad * unit), axis=0)
        attn_bias_grad = jnp.sum(own_half(normed_grad), axis=0)
        grad_second = grad_second + stream_part
        by_unit = unit_weight_grad.reshape(weight_rows, heads, 2, HD)
        weight_grads[layer] = (
            by_unit[:, :, 0].reshape(weight_rows, head_width),
            by_unit[:, :, 1].reshape(weight_rows, head_width),
            out_weight_grad,
            up_weight_grad,
            down_weight_grad,
        )
        own_parts = jnp.concatenate(
            [
                jnp.stack(
                    [attn_gain_grad, attn_bias_grad, ffn_gain_grad, ffn_bias_grad,
                     out_bias_grad, down_bias_grad]
                ),
                up_bias_grad.reshape(-1, half),
            ]
        )
        blank = jnp.zeros_like(own_parts)
        both = jnp.where(
            narrow_index == 0, jnp.stack([own_parts, blank]), jnp.stack([blank, own_parts])
        )
        small_grads[layer] = sum_all(both)

    def full_small(row):
        return jnp.stack([small_grads[layer][:, row].reshape(width) for layer in range(LAYERS)])

    def own_small(low, high):
        return jnp.stack(
            [
                lax.dynamic_index_in_dim(small_grads[layer], narrow_index, 0, keepdims=False)[
                    low:high
                ].reshape(-1)
                for layer in range(LAYERS)
            ]
        )

    def stacked(slot):
        return jnp.stack([weight_grads[layer][slot] for layer in range(LAYERS)])

    shape = (seqs, rows, half)
    return (
        first_out.reshape(shape),
        second_out.reshape(shape),
        own_half(grad_first).reshape(shape),
        own_half(grad_second).reshape(shape),
        full_small(0),
        full_small(1),
        stacked(0),
        stacked(1),
        stacked(2),
        own_small(4, 5),
        full_small(2),
        full_small(3),
        stacked(3),
        own_small(6, 6 + up_bias.shape[1] // half),
        stacked(4),
        own_small(5, 6),
    )


def solution(mesh):
    streams = P(None, "wide", "narrow")
    features = P(None, "narrow")
    hidden = P(None, None, "narrow")
    return jax.shard_map(
        shards,
        mesh=mesh,
        in_specs=(
            streams, streams, P(), P(), streams, streams, streams, features, P(), P(),
            hidden, features, hidden, features, P(None, None, "wide"), streams, streams,
        ),
        out_specs=(
            streams, streams, streams, streams, P(), P(), streams, streams, streams,
            features, P(), P(), streams, features, streams, features,
        ),
        check_vma=False,
    )
```

```python
import functools

import jax
import jax.numpy as jnp
from jax import lax
from jax.experimental import pallas as pl
from jax.experimental.pallas import tpu as pltpu
from jax.sharding import PartitionSpec as P

HD = 128
GROUP = 64
ROUNDS = 4
LAYERS = 2
BLOCK = 256
F32 = jnp.float32
BF16 = jnp.bfloat16
SCALE = HD ** (-0.5)
VMEM_LIMIT = 56 * 1024 * 1024
PAIRS = 8
CHUNKS = 2
FFN_STEPS = 4


def swap(value, axis, mask):
    count = lax.axis_size(axis)
    return lax.ppermute(value, axis, [(source, source ^ mask) for source in range(count)])


def dot(left, right, dims):
    return lax.dot_general(left, right, (dims, ((), ())), preferred_element_type=F32)


def mm(left, right):
    return dot(left, right, ((1,), (0,)))


def mm_t(left, right):
    return dot(left, right, ((1,), (1,)))


def t_mm(left, right):
    return dot(left, right, ((0,), (0,)))


def chip_exchange(units):
    count = lax.axis_size("wide")
    groups = [list(range(core, count, 2)) for core in range(2)]
    return lax.all_to_all(units, "wide", 0, 0, tiled=True, axis_index_groups=groups)


def split3(value):
    high = value.astype(BF16)
    rest = value - high.astype(F32)
    mid = rest.astype(BF16)
    low = (rest - mid.astype(F32)).astype(BF16)
    return high.astype(F32), mid.astype(F32), low.astype(F32)


def layer_norm(stream, gain, shift):
    centre = stream - jnp.mean(stream, axis=-1, keepdims=True)
    spread = jnp.mean(centre * centre, axis=-1, keepdims=True)
    return centre * lax.rsqrt(spread + 1e-05) * gain + shift


def layer_norm_back(stream, gain, grad):
    centre = stream - jnp.mean(stream, axis=-1, keepdims=True)
    inv = lax.rsqrt(jnp.mean(centre * centre, axis=-1, keepdims=True) + 1e-05)
    unit = centre * inv
    scaled = grad * gain
    back = inv * (
        scaled
        - jnp.mean(scaled, axis=-1, keepdims=True)
        - unit * jnp.mean(scaled * unit, axis=-1, keepdims=True)
    )
    return back, unit


def build_tables(tokens):
    rounds, seq = tokens.shape
    blocks = seq // BLOCK
    rank_rows = BLOCK // blocks
    tokens = tokens.reshape(rounds, blocks, BLOCK)
    run = tokens // BLOCK
    row = tokens % BLOCK
    onehot = (run[..., None] == jnp.arange(blocks, dtype=jnp.int32)).astype(BF16)
    before = (jnp.arange(BLOCK)[:, None] > jnp.arange(BLOCK)[None, :]).astype(BF16)
    counts = jnp.einsum("jl,rkla->rkja", before, onehot, preferred_element_type=F32)
    rank = jnp.sum(onehot.astype(F32) * counts, axis=-1).astype(jnp.int32)
    slot = run * rank_rows + rank
    iota = jnp.arange(BLOCK, dtype=jnp.int32)
    into = (slot[..., None] == iota).astype(BF16)
    into_t = (slot[..., None, :] == iota[:, None]).astype(BF16)
    wants = jnp.einsum("rknj,rkj->rkn", into_t, row.astype(BF16), preferred_element_type=F32)
    wants = wants.reshape(rounds, blocks, blocks, rank_rows)
    wants = jnp.transpose(wants, (0, 2, 1, 3)).reshape(rounds, blocks, BLOCK).astype(jnp.int32)
    out_of = (wants[..., None] == iota).astype(BF16)
    out_of_t = (wants[..., None, :] == iota[:, None]).astype(BF16)
    return jnp.transpose(out_of, (1, 0, 2, 3)), into, out_of_t, into_t


def token_copies(pos_ref, sources, tok, sems):
    core = pos_ref[0]
    chunks = len(sources) // 2
    slots, rows, _ = sources[0].shape
    copies = []
    for place, source in enumerate(sources):
        chunk, half = place // 2, place % 2
        for k in range(slots):
            device = 2 * k + (core ^ half)
            start = pl.multiple_of((device * chunks + chunk) * rows, rows)
            copies.append(
                pltpu.make_async_copy(
                    source.at[k], tok.at[pl.ds(start, rows)], sems.at[len(copies)]
                )
            )
    return copies


def table_copies(sources, targets, sems):
    return [
        pltpu.make_async_copy(source, target, sems.at[k])
        for k, (source, target) in enumerate(zip(sources, targets))
    ]


def store_run(pos_ref, buffer, run, value):
    core = pos_ref[0]
    _, chunks, _, rows, _ = buffer.shape
    for part in range(BLOCK // rows):
        device = run * (BLOCK // (rows * chunks)) + part // chunks
        buffer[(device & 1) ^ core, part % chunks, device >> 1] = value[
            part * rows : (part + 1) * rows
        ]


def send_halves(buffer, own_hbm, sib_hbm, sems):
    copies = [
        pltpu.make_async_copy(buffer.at[1], sib_hbm, sems.at[0]),
        pltpu.make_async_copy(buffer.at[0], own_hbm, sems.at[1]),
    ]
    for copy in copies:
        copy.start()
    for copy in copies:
        copy.wait()


def spread(first, count, width):
    row = lax.broadcasted_iota(jnp.int32, (HD, width), 0)
    return jnp.where((row >= first) & (row < first + count), 1.0, 0.0).astype(BF16)


def pack_stats(columns):
    lane = lax.broadcasted_iota(jnp.int32, columns[0].shape, 1)
    extra = jnp.zeros(columns[0].shape, F32)
    for place, column in enumerate(columns):
        extra = jnp.where(lane == place, column, extra)
    return extra


def permute_in(tok, out_of, mixed, blocks):
    rank = BLOCK // blocks
    for a in range(blocks):
        source = tok[a * BLOCK : (a + 1) * BLOCK, :]
        moved = mm(out_of[a].reshape(2 * BLOCK, BLOCK), source).astype(BF16)
        for r in range(2):
            mixed[r, :, a] = moved[r * BLOCK : (r + 1) * BLOCK].reshape(blocks, rank, 2 * HD)


def split_rows(tile):
    lane = lax.broadcasted_iota(jnp.int32, tile.shape, 1)
    zero = jnp.zeros_like(tile)
    return jnp.concatenate(
        [jnp.where(lane < GROUP, tile, zero), jnp.where(lane >= GROUP, tile, zero)], axis=0
    )


def split_lanes(tile):
    row = lax.broadcasted_iota(jnp.int32, tile.shape, 0)
    zero = jnp.zeros_like(tile)
    return jnp.concatenate(
        [jnp.where(row < GROUP, tile, zero), jnp.where(row >= GROUP, tile, zero)], axis=1
    )


def side_by_side(ref, base):
    return jnp.concatenate(
        [ref[base : base + 2 * GROUP, :], ref[base + GROUP : base + 3 * GROUP, :]], axis=1
    )


def one_above(ref, base):
    return jnp.concatenate(
        [ref[base : base + 2 * GROUP, :], ref[base + GROUP : base + 3 * GROUP, :]], axis=0
    )


def self_mask():
    row = lax.broadcasted_iota(jnp.int32, (2 * GROUP, 2 * GROUP), 0)
    lane = lax.broadcasted_iota(jnp.int32, (2 * GROUP, 2 * GROUP), 1)
    return row == lane % GROUP + GROUP


def unit_keys(query):
    return query * lax.rsqrt(jnp.mean(query * query, axis=-1, keepdims=True) + 1e-06)


def forward_kernel(chunks, extras, pos_ref, *refs):
    sources, refs = refs[: 2 * chunks], refs[2 * chunks + extras :]
    (
        out_of_hbm, into_hbm, out_of_t_hbm, into_t_hbm, sorted_hbm, own_hbm, sib_hbm,
        tok, mixed, keys, vals, placed, buffer, out_of, into, out_of_t, into_t,
        tok_sems, table_sems, out_sems, send_sems,
    ) = refs
    seq = tok.shape[0]
    blocks = seq // BLOCK
    rank = BLOCK // blocks
    loads = token_copies(pos_ref, sources, tok, tok_sems)
    tables = table_copies(
        (out_of_hbm, into_hbm, into_t_hbm, out_of_t_hbm), (out_of, into, into_t, out_of_t), table_sems
    )
    for copy in loads:
        copy.start()
    for copy in tables:
        copy.start()
    for copy in loads:
        copy.wait()
    tables[0].wait()
    permute_in(tok, out_of, mixed, blocks)
    tables[1].wait()
    outs = []
    for r in range(2):
        for k in range(blocks):
            base = k * BLOCK
            rows_sorted = mm(into[r, k], mixed[r, k].reshape(BLOCK, 2 * HD))
            placed[r, base : base + BLOCK, :] = rows_sorted.astype(BF16)
            where = slice(base + GROUP, base + GROUP + BLOCK)
            keys[r, where, :] = unit_keys(rows_sorted[:, :HD]).astype(BF16)
            vals[r, where, :] = rows_sorted[:, HD:].astype(BF16)
        keys[r, 0:GROUP, :] = keys[r, seq : seq + GROUP, :]
        vals[r, 0:GROUP, :] = vals[r, seq : seq + GROUP, :]
        outs.append(pltpu.make_async_copy(placed.at[r], sorted_hbm.at[r], out_sems.at[r]))
        outs[-1].start()
    tables[2].wait()
    own = jnp.concatenate([self_mask()] * PAIRS, axis=1)
    wide = PAIRS * 2 * GROUP
    for r in range(2):
        for first in range(0, seq, wide):
            bases = [first + p * 2 * GROUP for p in range(PAIRS)]
            flipped = [placed[r, base : base + 2 * GROUP, 0:HD].T for base in bases]
            raw = jnp.concatenate(
                [
                    mm(side_by_side(keys.at[r], base), split_rows(tile))
                    for base, tile in zip(bases, flipped)
                ],
                axis=1,
            )
            scores = jnp.where(own, -1000000000.0, raw * SCALE)
            top = jnp.max(scores, axis=0, keepdims=True)
            weight = jnp.exp(scores - top)
            total = jnp.sum(weight, axis=0, keepdims=True)
            probs = (weight * (1.0 / total)).astype(BF16)
            row = lax.broadcasted_iota(jnp.int32, (8, wide), 0)
            stats = jnp.zeros((8, wide), F32)
            for place, part in enumerate(split3(top + jnp.log(total))):
                stats = jnp.where(row == place, part, stats)
            stats = jnp.concatenate([stats, jnp.zeros((HD - 8, wide), F32)], axis=0)
            lanes = [slice(p * 2 * GROUP, (p + 1) * 2 * GROUP) for p in range(PAIRS)]
            turned = [probs[:, lane].T for lane in lanes]
            extra = [stats[:, lane].T.astype(BF16) for lane in lanes]
            result = [
                mm(split_lanes(tile), one_above(vals.at[r], base)).astype(BF16)
                for tile, base in zip(turned, bases)
            ]
            packed = jnp.concatenate(
                [jnp.concatenate(pair, axis=1) for pair in zip(result, extra)], axis=0
            )
            for part in range(wide // BLOCK):
                k = first // BLOCK + part
                back = mm(into_t[r, k], packed[part * BLOCK : (part + 1) * BLOCK]).astype(BF16)
                mixed[r, k] = back.reshape(blocks, rank, 2 * HD)
    tables[3].wait()
    zero = jnp.zeros((HD, HD), BF16)
    ones = spread(0, 3, HD)
    ones = jnp.concatenate(
        [jnp.concatenate([ones, zero], axis=1), jnp.concatenate([zero, ones], axis=1)], axis=0
    )
    for a in range(blocks):
        moved = [mm(out_of_t[r, a], mixed[r, :, a].reshape(BLOCK, 2 * HD)) for r in range(2)]
        lse = mm(jnp.concatenate([m[:, HD:] for m in moved], axis=1).astype(BF16), ones)
        lse_a, lse_b = lse[:, :HD], lse[:, HD:]
        top = jnp.maximum(lse_a, lse_b)
        weight_a, weight_b = jnp.exp(lse_a - top), jnp.exp(lse_b - top)
        total = weight_a + weight_b
        value = (moved[0][:, :HD] * weight_a + moved[1][:, :HD] * weight_b) * (1.0 / total)
        extra = pack_stats(split3(top + jnp.log(total)))
        store_run(pos_ref, buffer, a, jnp.concatenate([value, extra], axis=1).astype(BF16))
    send_halves(buffer, own_hbm, sib_hbm, send_sems)
    for copy in outs:
        copy.wait()


def backward_kernel(chunks, extras, pos_ref, *refs):
    sources, refs = refs[: 2 * chunks], refs[2 * chunks + extras :]
    (
        sorted_hbm, out_of_hbm, into_hbm, out_of_t_hbm, into_t_hbm, own_hbm, sib_hbm,
        tok, mixed, keys, vals, placed, grads, query_use, key_grad, val_grad, buffer,
        out_of, into, out_of_t, into_t, tok_sems, table_sems, in_sems, send_sems,
    ) = refs
    seq = tok.shape[0]
    blocks = seq // BLOCK
    rank = BLOCK // blocks
    loads = token_copies(pos_ref, sources, tok, tok_sems)
    tables = table_copies(
        (out_of_hbm, into_hbm, into_t_hbm, out_of_t_hbm), (out_of, into, into_t, out_of_t), table_sems
    )
    sorted_in = pltpu.make_async_copy(sorted_hbm, placed, in_sems.at[0])
    for copy in loads:
        copy.start()
    tables[0].start()
    sorted_in.start()
    for copy in tables[1:]:
        copy.start()
    for copy in loads:
        copy.wait()
    tables[0].wait()
    permute_in(tok, out_of, mixed, blocks)
    sorted_in.wait()
    tables[1].wait()
    for r in range(2):
        for k in range(blocks):
            here = slice(k * BLOCK, (k + 1) * BLOCK)
            where = slice(k * BLOCK + GROUP, (k + 1) * BLOCK + GROUP)
            grads[r, here, :] = mm(into[r, k], mixed[r, k].reshape(BLOCK, 2 * HD)).astype(BF16)
            keys[r, where, :] = unit_keys(placed[r, here, 0:HD].astype(F32)).astype(BF16)
            vals[r, where, :] = placed[r, here, HD:]
        keys[r, 0:GROUP, :] = keys[r, seq : seq + GROUP, :]
        vals[r, 0:GROUP, :] = vals[r, seq : seq + GROUP, :]
        key_grad[r, 0:GROUP, :] = jnp.zeros((GROUP, HD), F32)
        val_grad[r, 0:GROUP, :] = jnp.zeros((GROUP, HD), F32)
    own = jnp.concatenate([self_mask()] * PAIRS, axis=1)
    wide = PAIRS * 2 * GROUP
    lanes = [slice(p * 2 * GROUP, (p + 1) * 2 * GROUP) for p in range(PAIRS)]
    for r in range(2):
        for first in range(0, seq, wide):
            bases = [first + p * 2 * GROUP for p in range(PAIRS)]
            query = [placed[r, base : base + 2 * GROUP, 0:HD] for base in bases]
            grad = [grads[r, base : base + 2 * GROUP, 0:HD] for base in bases]
            stats = jnp.concatenate(
                [
                    grads[r, base : base + 2 * GROUP, HD:].astype(F32).T[0:8] for base in bases
                ],
                axis=1,
            )
            delta = stats[0:1] + stats[1:2] + stats[2:3]
            lse = stats[3:4] + stats[4:5] + stats[5:6]
            query_t = [split_rows(tile.T) for tile in query]
            grad_t = [split_rows(tile.T) for tile in grad]
            raw = jnp.concatenate(
                [mm(side_by_side(keys.at[r], base), tile) for base, tile in zip(bases, query_t)],
                axis=1,
            )
            prob_grad = jnp.concatenate(
                [mm(side_by_side(vals.at[r], base), tile) for base, tile in zip(bases, grad_t)],
                axis=1,
            )
            probs = jnp.exp(jnp.where(own, -1000000000.0, raw * SCALE) - lse)
            score_grad = (probs * (prob_grad - delta)).astype(BF16)
            probs = probs.astype(BF16)
            turned = [score_grad[:, lane].T for lane in lanes]
            for tile, base in zip(turned, bases):
                query_use[r, base : base + 2 * GROUP, :] = (
                    mm(split_lanes(tile), one_above(keys.at[r], base)) * SCALE
                )
            key_parts = [
                mm(split_rows(score_grad[:, lane]), tile) * SCALE for lane, tile in zip(lanes, query)
            ]
            val_parts = [mm(split_rows(probs[:, lane]), tile) for lane, tile in zip(lanes, grad)]
            for target, parts in ((key_grad, key_parts), (val_grad, val_parts)):
                target[r, first : first + GROUP, :] += parts[0][:GROUP]
                for p, (part, base) in enumerate(zip(parts, bases)):
                    target[r, base + GROUP : base + 2 * GROUP, :] = (
                        part[GROUP : 2 * GROUP] + part[2 * GROUP : 3 * GROUP]
                    )
                    last = part[3 * GROUP :]
                    if p + 1 < PAIRS:
                        last = last + parts[p + 1][:GROUP]
                    target[r, base + 2 * GROUP : base + 3 * GROUP, :] = last
        key_grad[r, seq : seq + GROUP, :] += key_grad[r, 0:GROUP, :]
        val_grad[r, seq : seq + GROUP, :] += val_grad[r, 0:GROUP, :]
    tables[2].wait()
    for r in range(2):
        for k in range(blocks):
            here = slice(k * BLOCK, (k + 1) * BLOCK)
            where = slice(k * BLOCK + GROUP, (k + 1) * BLOCK + GROUP)
            query = placed[r, here, 0:HD].astype(F32)
            inv = lax.rsqrt(jnp.mean(query * query, axis=-1, keepdims=True) + 1e-06)
            grad = key_grad[r, where, :]
            inner = jnp.mean(grad * query, axis=-1, keepdims=True)
            total = query_use[r, here, :] + inv * (grad - query * (inner * inv * inv))
            packed = jnp.concatenate([total, val_grad[r, where, :]], axis=1).astype(BF16)
            back = mm(into_t[r, k], packed).astype(BF16)
            mixed[r, k] = back.reshape(blocks, rank, 2 * HD)
    tables[3].wait()
    for a in range(blocks):
        total = mm(out_of_t[0, a], mixed[0, :, a].reshape(BLOCK, 2 * HD)) + mm(
            out_of_t[1, a], mixed[1, :, a].reshape(BLOCK, 2 * HD)
        )
        store_run(pos_ref, buffer, a, total.astype(BF16))
    send_halves(buffer, own_hbm, sib_hbm, send_sems)


def params():
    return pltpu.CompilerParams(vmem_limit_bytes=VMEM_LIMIT)


def cost(flops, moved):
    return pl.CostEstimate(flops=int(flops), bytes_accessed=int(moved), transcendentals=0)


IN_SMEM = pl.BlockSpec(memory_space=pltpu.SMEM)
IN_VMEM = pl.BlockSpec(memory_space=pltpu.VMEM)
ANYWHERE = pl.BlockSpec(memory_space=pl.ANY)


def bf16_out(*shape):
    return jax.ShapeDtypeStruct(shape, BF16)


def f32_out(*shape):
    return jax.ShapeDtypeStruct(shape, F32)


def table_scratch(blocks):
    return [
        pltpu.VMEM((blocks, 2, BLOCK, BLOCK), BF16),
        pltpu.VMEM((2, blocks, BLOCK, BLOCK), BF16),
        pltpu.VMEM((2, blocks, BLOCK, BLOCK), BF16),
        pltpu.VMEM((2, blocks, BLOCK, BLOCK), BF16),
    ]


def attention_forward(pos, sources, tables, after):
    chunks = len(sources) // 2
    slots, rows, width = sources[0].shape
    seq = 2 * slots * rows * chunks
    blocks = seq // BLOCK
    half = bf16_out(chunks, slots, rows, width)
    return pl.pallas_call(
        functools.partial(forward_kernel, chunks, len(after)),
        out_shape=(bf16_out(2, seq, width), half, half),
        in_specs=[IN_SMEM] + [ANYWHERE] * (2 * chunks + len(after) + 4),
        out_specs=(ANYWHERE, ANYWHERE, ANYWHERE),
        scratch_shapes=[
            pltpu.VMEM((seq, width), BF16),
            pltpu.VMEM((2, blocks, blocks, BLOCK // blocks, width), BF16),
            pltpu.VMEM((2, seq + GROUP, HD), BF16),
            pltpu.VMEM((2, seq + GROUP, HD), BF16),
            pltpu.VMEM((2, seq, width), BF16),
            pltpu.VMEM((2, chunks, slots, rows, width), BF16),
            *table_scratch(blocks),
            pltpu.SemaphoreType.DMA((2 * slots * chunks,)),
            pltpu.SemaphoreType.DMA((4,)),
            pltpu.SemaphoreType.DMA((2,)),
            pltpu.SemaphoreType.DMA((2,)),
        ],
        compiler_params=params(),
        cost_estimate=cost(16e9, 24e6),
        name="attend_forward",
    )(pos, *sources, *after, *tables)


def attention_backward(pos, sources, sorted_rows, tables, after):
    chunks = len(sources) // 2
    slots, rows, width = sources[0].shape
    seq = 2 * slots * rows * chunks
    blocks = seq // BLOCK
    half = bf16_out(chunks, slots, rows, width)
    return pl.pallas_call(
        functools.partial(backward_kernel, chunks, len(after)),
        out_shape=(half, half),
        in_specs=[IN_SMEM] + [ANYWHERE] * (2 * chunks + len(after) + 5),
        out_specs=(ANYWHERE, ANYWHERE),
        scratch_shapes=[
            pltpu.VMEM((seq, width), BF16),
            pltpu.VMEM((2, blocks, blocks, BLOCK // blocks, width), BF16),
            pltpu.VMEM((2, seq + GROUP, HD), BF16),
            pltpu.VMEM((2, seq + GROUP, HD), BF16),
            pltpu.VMEM((2, seq, width), BF16),
            pltpu.VMEM((2, seq, width), BF16),
            pltpu.VMEM((2, seq, HD), F32),
            pltpu.VMEM((2, seq + GROUP, HD), F32),
            pltpu.VMEM((2, seq + GROUP, HD), F32),
            pltpu.VMEM((2, chunks, slots, rows, width), BF16),
            *table_scratch(blocks),
            pltpu.SemaphoreType.DMA((2 * slots * chunks,)),
            pltpu.SemaphoreType.DMA((4,)),
            pltpu.SemaphoreType.DMA((1,)),
            pltpu.SemaphoreType.DMA((2,)),
        ],
        compiler_params=params(),
        cost_estimate=cost(18e9, 26e6),
        name="attend_backward",
    )(pos, *sources, *after, sorted_rows, *tables)


def unit_slices(seqs, heads, rows, width):
    return [
        (slice(seq * rows, (seq + 1) * rows), slice(head * width, (head + 1) * width))
        for seq in range(seqs)
        for head in range(heads)
    ]


def column_block(rows, width, place):
    return pl.BlockSpec((rows, width), lambda i: (0, place))


def whole_block(array):
    return pl.BlockSpec(array.shape, lambda i: (0,) * len(array.shape))


def pack_kernel(count, *refs):
    out_ref = refs[-1]
    start = 0
    for ref in refs[:count]:
        out_ref[:, start : start + ref.shape[1]] = ref[...]
        start += ref.shape[1]


def pack_columns(pieces, after):
    rows, columns = pieces[0].shape[0], sum(piece.shape[1] for piece in pieces)
    return pl.pallas_call(
        functools.partial(pack_kernel, len(pieces)),
        out_shape=bf16_out(rows, columns),
        in_specs=[IN_VMEM] * len(pieces) + [ANYWHERE] * len(after),
        out_specs=IN_VMEM,
        compiler_params=params(),
        name="pack_columns",
    )(*pieces, *after)


def lower_kernel(count, *refs):
    for source, target in zip(refs[:count], refs[-count:]):
        target[...] = source[...].astype(BF16)


def lower_arrays(arrays, after):
    return pl.pallas_call(
        functools.partial(lower_kernel, len(arrays)),
        out_shape=[bf16_out(*array.shape) for array in arrays],
        in_specs=[IN_VMEM] * len(arrays) + [ANYWHERE] * len(after),
        out_specs=[IN_VMEM] * len(arrays),
        compiler_params=params(),
        name="lower_arrays",
    )(*arrays, *after)


def widen_kernel(pos_ref, mine_ref, other_ref, *out_refs):
    seqs, rows, half = mine_ref.shape
    count = rows // len(out_refs)
    mine_at = pl.ds(pl.multiple_of(pos_ref[1] * half, half), half)
    other_at = pl.ds(pl.multiple_of((1 - pos_ref[1]) * half, half), half)
    for q, out_ref in enumerate(out_refs):
        for seq in range(seqs):
            at = slice(seq * count, (seq + 1) * count)
            source = slice(q * count, (q + 1) * count)
            out_ref[at, mine_at] = mine_ref[seq, source]
            out_ref[at, other_at] = other_ref[seq, source].astype(F32)


def widen_chunks(pos, mine, other):
    seqs, rows, half = mine.shape
    out = f32_out(seqs * rows // CHUNKS, 2 * half)
    return list(
        pl.pallas_call(
            widen_kernel,
            out_shape=[out] * CHUNKS,
            in_specs=[IN_SMEM, IN_VMEM, IN_VMEM],
            out_specs=[IN_VMEM] * CHUNKS,
            compiler_params=params(),
            cost_estimate=cost(1e6, 4e6),
            name="widen_chunks",
        )(pos, mine, other)
    )


def narrow_kernel(layer, pos_ref, *refs):
    refs, out_ref = refs[:-1], refs[-1]
    seqs, rows, half = out_ref.shape
    count = rows // CHUNKS
    lanes = pl.ds(pl.multiple_of(pos_ref[1] * half, half), half)
    for q in range(CHUNKS):
        for seq in range(seqs):
            at = slice(seq * count, (seq + 1) * count)
            value = refs[q][at, lanes]
            if layer is not None:
                own, other = refs[CHUNKS + 2 * q : CHUNKS + 2 * q + 2]
                value = value + (own[at, lanes].astype(F32) + other[at, lanes].astype(F32))
                value = value + refs[-1][layer : layer + 1, lanes]
            out_ref[seq, q * count : (q + 1) * count] = value


def narrow_chunks(pos, chunks, seqs, layer=None, parts=()):
    toks, width = chunks[0].shape
    return pl.pallas_call(
        functools.partial(narrow_kernel, layer),
        out_shape=f32_out(seqs, toks * CHUNKS // seqs, width // 2),
        in_specs=[IN_SMEM] + [IN_VMEM] * (CHUNKS + len(parts)),
        out_specs=IN_VMEM,
        compiler_params=params(),
        cost_estimate=cost(1e6, 4e6),
        name="narrow_chunks",
    )(pos, *chunks, *parts)


def enter_kernel(
    seqs, layer, parts, after, stream_ref, gain_ref, shift_ref, weight_ref, *refs
):
    stream = stream_ref[...]
    if parts:
        own_ref, other_ref, bias_ref, *refs = refs
        stream = stream + (own_ref[...].astype(F32) + other_ref[...].astype(F32))
        stream = stream + bias_ref[layer - 1 : layer]
    refs = refs[after:]
    if parts:
        refs[0][...] = stream
    normed_ref, out_ref = refs[-2:]
    row = slice(layer, layer + 1)
    normed = layer_norm(stream, gain_ref[row], shift_ref[row]).astype(BF16)
    normed_ref[...] = normed
    flat = mm(normed, weight_ref[...]).astype(BF16)
    slots, rows, width = out_ref.shape
    for k, at in enumerate(unit_slices(seqs, slots // seqs, rows, width)):
        out_ref[k] = flat[at]


def enter_attention(seqs, layer, stream, gain, shift, weight, place, columns, parts=(), after=()):
    toks, width = stream.shape
    slots = seqs * columns // (2 * HD)
    shapes = [bf16_out(toks, width), bf16_out(slots, toks // seqs, 2 * HD)]
    if parts:
        shapes = [f32_out(toks, width)] + shapes
    results = pl.pallas_call(
        functools.partial(enter_kernel, seqs, layer, len(parts) > 0, len(after)),
        grid=(1,),
        out_shape=shapes,
        in_specs=[whole_block(stream), whole_block(gain), whole_block(shift)]
        + [column_block(width, columns, place)]
        + [whole_block(part) for part in parts]
        + [ANYWHERE] * len(after),
        out_specs=[whole_block(shape) for shape in shapes],
        compiler_params=params(),
        cost_estimate=cost(2 * toks * width * columns, 5e6),
        name="enter_attention",
    )(stream, gain, shift, weight, *parts, *after)
    return results if parts else (stream, *results)


def merge_kernel(seqs, weight_ref, in_ref, *refs):
    part_ref, tok_ref = refs[-2:]
    slots, rows, width = in_ref.shape
    for k, at in enumerate(unit_slices(seqs, slots // seqs, rows, width)):
        tok_ref[at] = in_ref[k]
    part_ref[...] = mm_t(tok_ref[...], weight_ref[...]).astype(BF16)


def merge_units(seqs, units, weight, place, after=()):
    slots, rows, width = units.shape
    toks, columns = seqs * rows, slots // seqs * width
    shapes = (bf16_out(toks, weight.shape[0]), bf16_out(toks, columns))
    return pl.pallas_call(
        functools.partial(merge_kernel, seqs),
        grid=(1,),
        out_shape=shapes,
        in_specs=[column_block(weight.shape[0], columns, place), whole_block(units)]
        + [ANYWHERE] * len(after),
        out_specs=[whole_block(shape) for shape in shapes],
        compiler_params=params(),
        cost_estimate=cost(2 * toks * columns * weight.shape[0], 3e6),
        name="merge_units",
    )(weight, units, *after)


def both_stats(own, got):
    zero = jnp.zeros((HD, HD), BF16)
    ones = spread(0, 3, HD)
    ones = jnp.concatenate(
        [jnp.concatenate([ones, zero], axis=1), jnp.concatenate([zero, ones], axis=1)], axis=0
    )
    lse = mm(jnp.concatenate([own, got], axis=1), ones)
    return lse[:, :HD], lse[:, HD:]


def combine_kernel(own_ref, got_ref, attn_ref, stats_ref, *out_refs):
    chunks, slots, rows, _ = own_ref.shape
    for q in range(chunks):
        for k in range(slots):
            lse_a, lse_b = both_stats(own_ref[q, k, :, HD:], got_ref[q, k, :, HD:])
            top = jnp.maximum(lse_a, lse_b)
            weight_a, weight_b = jnp.exp(lse_a - top), jnp.exp(lse_b - top)
            total = weight_a + weight_b
            own = own_ref[q, k, :, :HD].astype(F32)
            got = got_ref[q, k, :, :HD].astype(F32)
            value = (own * weight_a + got * weight_b) * (1.0 / total)
            attn_ref[q, k] = value
            zero = jnp.zeros_like(total)
            stats_ref[q, k] = pack_stats(
                (zero, zero, zero) + split3(top + jnp.log(total))
            ).astype(BF16)
            out_refs[q][k] = value.astype(BF16)


def combine_cores(own, got):
    chunks, slots, rows, _ = own.shape
    results = pl.pallas_call(
        combine_kernel,
        out_shape=[f32_out(chunks, slots, rows, HD), bf16_out(chunks, slots, rows, HD)]
        + [bf16_out(slots, rows, HD)] * chunks,
        in_specs=[IN_VMEM] * 2,
        out_specs=[IN_VMEM] * (2 + chunks),
        compiler_params=params(),
        cost_estimate=cost(1e8, 5e6),
        name="combine_cores",
    )(own, got)
    return results[0], results[1], results[2:]


def join_kernel(attn_ref, stats_ref, in_ref, *refs):
    out_ref = refs[-1]
    for k in range(in_ref.shape[0]):
        grad = in_ref[k]
        delta = jnp.sum(attn_ref[0, k] * grad.astype(F32), axis=-1, keepdims=True)
        delta = jnp.broadcast_to(delta, grad.shape)
        extra = pack_stats(split3(delta)) + stats_ref[0, k].astype(F32)
        out_ref[k] = jnp.concatenate([grad, extra.astype(BF16)], axis=1)


def join_grads(chunk, attn, stats, units, after=()):
    slots, rows, _ = units.shape
    spec = pl.BlockSpec((1, slots, rows, HD), lambda i: (chunk, 0, 0, 0))
    return pl.pallas_call(
        join_kernel,
        grid=(1,),
        out_shape=bf16_out(slots, rows, 2 * HD),
        in_specs=[spec, spec, pl.BlockSpec((slots, rows, HD), lambda i: (0, 0, 0))]
        + [ANYWHERE] * len(after),
        out_specs=pl.BlockSpec((slots, rows, 2 * HD), lambda i: (0, 0, 0)),
        compiler_params=params(),
        cost_estimate=cost(1e7, 2e6),
        name="join_grads",
    )(attn, stats, units, *after)


def add_kernel(own_ref, got_ref, *out_refs):
    for q, out_ref in enumerate(out_refs):
        total = own_ref[q].astype(F32) + got_ref[q].astype(F32)
        out_ref[...] = total.astype(BF16)


def add_cores(own, got):
    chunks, slots, rows, width = own.shape
    return pl.pallas_call(
        add_kernel,
        out_shape=[bf16_out(slots, rows, width)] * chunks,
        in_specs=[IN_VMEM] * 2,
        out_specs=[IN_VMEM] * chunks,
        compiler_params=params(),
        cost_estimate=cost(1e6, 3e6),
        name="add_cores",
    )(own, got)


def ffn_kernel(
    layer, stream_ref, own_ref, other_ref, bias_ref, gain_ref, shift_ref, up_ref, up_bias_ref,
    down_ref, new_ref, normed_ref, pre_ref, part_ref, acc,
):
    step = pl.program_id(0)
    row = slice(layer, layer + 1)

    @pl.when(step == 0)
    def _():
        stream = stream_ref[...] + (own_ref[...].astype(F32) + other_ref[...].astype(F32))
        stream = stream + bias_ref[row]
        new_ref[...] = stream
        normed_ref[...] = layer_norm(stream, gain_ref[row], shift_ref[row]).astype(BF16)

    pre = mm(normed_ref[...], up_ref[0]) + up_bias_ref[row]
    pre_ref[...] = pre
    hidden = jax.nn.gelu(pre, approximate=True).astype(BF16)
    part = mm_t(hidden, down_ref[0])

    @pl.when(step == 0)
    def _():
        acc[...] = part

    @pl.when(step > 0)
    def _():
        acc[...] += part

    @pl.when(step == pl.num_programs(0) - 1)
    def _():
        part_ref[...] = acc[...].astype(BF16)


def feed_forward(layer, stream, own, other, bias, gain, shift, up, up_bias, down):
    toks, width = stream.shape
    hidden = up.shape[2]
    step = hidden // FFN_STEPS
    full = pl.BlockSpec((toks, width), lambda i: (0, 0))
    slab = pl.BlockSpec((1, width, step), lambda i: (layer, 0, i))
    return pl.pallas_call(
        functools.partial(ffn_kernel, layer),
        grid=(FFN_STEPS,),
        out_shape=(
            f32_out(toks, width), bf16_out(toks, width), f32_out(toks, hidden), bf16_out(toks, width),
        ),
        in_specs=[
            full, full, full, whole_block(bias), whole_block(gain), whole_block(shift), slab,
            pl.BlockSpec((LAYERS, step), lambda i: (0, i)), slab,
        ],
        out_specs=(full, full, pl.BlockSpec((toks, step), lambda i: (0, i)), full),
        scratch_shapes=[pltpu.VMEM((toks, width), F32)],
        compiler_params=params(),
        cost_estimate=cost(4 * toks * width * hidden, 14e6),
        name="feed_forward",
    )(stream, own, other, bias, gain, shift, up, up_bias, down)


def ffn_back_kernel(
    grad_ref, up_ref, down_ref, pre_ref,
    branch_ref, hidden_ref, low_ref, down_bias_ref, up_bias_ref, part_ref, acc,
):
    step = pl.program_id(0)

    @pl.when(step == 0)
    def _():
        grad = grad_ref[...]
        branch_ref[...] = grad.astype(BF16)
        down_bias_ref[...] = jnp.sum(grad, axis=0, keepdims=True)

    hidden_grad = mm(branch_ref[...], down_ref[0])
    pre = pre_ref[...]
    root = 0.7978845608028654
    square = pre * pre
    bend = jnp.tanh(root * (pre + 0.044715 * (square * pre)))
    half = 0.5 * (1.0 + bend)
    hidden_ref[...] = (pre * half).astype(BF16)
    slope = half + 0.5 * pre * (1.0 - bend * bend) * (root * (1.0 + 3 * 0.044715 * square))
    pre_grad = hidden_grad * slope
    up_bias_ref[...] = jnp.sum(pre_grad, axis=0, keepdims=True)
    low = pre_grad.astype(BF16)
    low_ref[...] = low
    part = mm_t(low, up_ref[0])

    @pl.when(step == 0)
    def _():
        acc[...] = part

    @pl.when(step > 0)
    def _():
        acc[...] += part

    @pl.when(step == pl.num_programs(0) - 1)
    def _():
        part_ref[...] = acc[...].astype(BF16)


def feed_back(layer, grad, up, down, pre):
    toks, width = grad.shape
    hidden = down.shape[2]
    step = hidden // FFN_STEPS
    full = pl.BlockSpec((toks, width), lambda i: (0, 0))
    slab = pl.BlockSpec((1, width, step), lambda i: (layer, 0, i))
    tall = pl.BlockSpec((toks, step), lambda i: (0, i))
    return pl.pallas_call(
        ffn_back_kernel,
        grid=(FFN_STEPS,),
        out_shape=(
            bf16_out(toks, width), bf16_out(toks, hidden), bf16_out(toks, hidden),
            f32_out(1, width), f32_out(1, hidden), bf16_out(toks, width),
        ),
        in_specs=[full, slab, slab, tall],
        out_specs=(
            full, tall, tall, pl.BlockSpec((1, width), lambda i: (0, 0)),
            pl.BlockSpec((1, step), lambda i: (0, i)), full,
        ),
        scratch_shapes=[pltpu.VMEM((toks, width), F32)],
        compiler_params=params(),
        cost_estimate=cost(4 * toks * width * hidden, 15e6),
        name="feed_back",
    )(grad, up, down, pre)


def products_kernel(counts, *refs):
    out_ref, turned = refs[-2:]
    step = pl.program_id(0)
    start = 0
    for place, count in enumerate(counts):
        lefts = refs[2 * CHUNKS * place : 2 * CHUNKS * place + CHUNKS]
        rights = refs[2 * CHUNKS * place + CHUNKS : 2 * CHUNKS * (place + 1)]

        @pl.when(step == start)
        def _(lefts=lefts):
            for q, left in enumerate(lefts):
                toks = left.shape[0]
                turned[:, q * toks : (q + 1) * toks] = left[...].T

        @pl.when((step >= start) & (step < start + count))
        def _(rights=rights):
            right = jnp.concatenate([right[...] for right in rights], axis=0)
            out_ref[...] = mm(turned[...], right).astype(BF16)

        start += count


def weight_products(pairs, columns, at=0, target=None, after=()):
    block = min(right[0].shape[1] for _, right in pairs)
    block = min(block, 512)
    counts = [right[0].shape[1] // block for _, right in pairs]
    toks, rows = pairs[0][0][0].shape
    specs, operands, start = [], [], 0
    for (left, right), count in zip(pairs, counts):
        specs += [pl.BlockSpec((toks, rows), lambda i: (0, 0))] * CHUNKS
        specs += [
            pl.BlockSpec(
                (toks, block),
                lambda i, start=start, count=count: (0, jnp.clip(i - start, 0, count - 1)),
            )
        ] * CHUNKS
        operands += [*left, *right]
        start += count
    more = [*after] if target is None else [target, *after]
    return pl.pallas_call(
        functools.partial(products_kernel, counts),
        grid=(start,),
        out_shape=bf16_out(rows, columns),
        in_specs=specs + [ANYWHERE] * len(more),
        out_specs=pl.BlockSpec((rows, block), lambda i: (0, i + at // block)),
        scratch_shapes=[pltpu.VMEM((rows, CHUNKS * toks), BF16)],
        input_output_aliases={} if target is None else {len(operands): 0},
        compiler_params=params(),
        cost_estimate=cost(2 * rows * CHUNKS * toks * start * block, 20e6),
        name="weight_products",
    )(*operands, *more)


def norm_back(
    layer, stream_ref, own_ref, other_ref, grad_ref, gain_ref, gain_out, shift_out
):
    grad = own_ref[...].astype(F32) + other_ref[...].astype(F32)
    back, unit = layer_norm_back(stream_ref[...], gain_ref[layer : layer + 1], grad)
    gain_out[...] = jnp.sum(grad * unit, axis=0, keepdims=True)
    shift_out[...] = jnp.sum(grad, axis=0, keepdims=True)
    return grad_ref[...] + back


def leave_kernel(
    seqs, layer, after, stream_ref, own_ref, other_ref, grad_ref, gain_ref, weight_ref, *refs
):
    new_ref, low_ref, gain_out, shift_out, bias_out, out_ref = refs[after:]
    grad = norm_back(
        layer, stream_ref, own_ref, other_ref, grad_ref, gain_ref, gain_out, shift_out
    )
    new_ref[...] = grad
    bias_out[...] = jnp.sum(grad, axis=0, keepdims=True)
    low = grad.astype(BF16)
    low_ref[...] = low
    flat = mm(low, weight_ref[...]).astype(BF16)
    slots, rows, width = out_ref.shape
    for k, at in enumerate(unit_slices(seqs, slots // seqs, rows, width)):
        out_ref[k] = flat[at]


def leave_ffn(
    seqs, layer, stream, own, other, grad, gain, weight, place, columns, after=()
):
    toks, width = stream.shape
    shapes = [f32_out(toks, width), bf16_out(toks, width)] + [f32_out(1, width)] * 3
    shapes.append(bf16_out(seqs * columns // HD, toks // seqs, HD))
    operands = (stream, own, other, grad, gain)
    return pl.pallas_call(
        functools.partial(leave_kernel, seqs, layer, len(after)),
        grid=(1,),
        out_shape=shapes,
        in_specs=[whole_block(operand) for operand in operands]
        + [column_block(width, columns, place)]
        + [ANYWHERE] * len(after),
        out_specs=[whole_block(shape) for shape in shapes],
        compiler_params=params(),
        cost_estimate=cost(2 * toks * width * columns, 6e6),
        name="leave_ffn",
    )(*operands, weight, *after)


def finish_kernel(
    layer, stream_ref, own_ref, other_ref, grad_ref, gain_ref, new_ref, gain_out, shift_out
):
    new_ref[...] = norm_back(
        layer, stream_ref, own_ref, other_ref, grad_ref, gain_ref, gain_out, shift_out
    )


def finish_attention(layer, stream, own, other, grad, gain):
    toks, width = stream.shape
    return pl.pallas_call(
        functools.partial(finish_kernel, layer),
        out_shape=(f32_out(toks, width), f32_out(1, width), f32_out(1, width)),
        in_specs=[IN_VMEM] * 5,
        out_specs=(IN_VMEM,) * 3,
        compiler_params=params(),
        cost_estimate=cost(1e7, 4e6),
        name="finish_attention",
    )(stream, own, other, grad, gain)


def reduce_rows(value):
    count = lax.axis_size("wide")
    index = lax.axis_index("wide")
    width = value.shape[1]
    block = value.shape[0] // count
    value = value.astype(BF16)
    bit = 1
    parts = count
    while bit < count:
        view = value.reshape(parts // 2, 2, block, width)
        mine = (index // bit) % 2
        sent = lax.dynamic_index_in_dim(view, 1 - mine, 1, keepdims=False)
        kept = lax.dynamic_index_in_dim(view, mine, 1, keepdims=False)
        value = kept.astype(F32) + swap(sent, "wide", bit).astype(F32)
        parts //= 2
        bit *= 2
        if bit < count:
            value = value.astype(BF16)
    return value.reshape(block, width)


def sum_rows(value, widths):
    total = lax.psum_scatter(value, "wide", scatter_dimension=0, tiled=True).astype(F32)
    ends = [0]
    for width in widths:
        ends.append(ends[-1] + width)
    return [total[:, low:high] for low, high in zip(ends, ends[1:])]


def sum_wide(value):
    for bit in range(lax.axis_size("wide").bit_length() - 1):
        value = value + swap(value, "wide", 1 << bit)
    return value


def shards(
    first_in, second_in, attn_norm_gain, attn_norm_bias, qk_weight, value_weight, out_weight,
    out_bias, ffn_norm_gain, ffn_norm_bias, up_weight, up_bias, down_weight, down_bias,
    bucket_perm, first_cot, second_cot,
):
    seqs, rows, half = first_in.shape
    wide = lax.axis_size("wide")
    wide_index = lax.axis_index("wide")
    narrow_index = lax.axis_index("narrow")
    pos = jnp.stack([wide_index % 2, narrow_index]).astype(jnp.int32)
    weight_rows, head_width = qk_weight.shape[1:]
    heads = head_width // HD
    width = 2 * half
    hidden_width = up_bias.shape[1]
    chunks = range(CHUNKS)

    def own_half(full):
        return lax.dynamic_slice_in_dim(full, narrow_index * half, half, full.ndim - 1)

    def flat_weight(layer):
        pair = jnp.stack([qk_weight[layer], value_weight[layer]], axis=1)
        pair = pair.reshape(weight_rows, 2, heads, HD)
        return jnp.transpose(pair, (0, 2, 1, 3)).reshape(weight_rows, 2 * head_width)

    def widen(streams, after):
        return [
            widen_chunks(pos, stream, swap(sent, "narrow", 1))
            for stream, sent in zip(streams, lower_arrays(streams, after))
        ]

    second, first = widen((second_in, first_in), [])
    early = lax.all_gather(
        jnp.concatenate([flat_weight(0), out_weight[0]], axis=1), "wide", axis=0, tiled=True
    )

    perm_parts = bucket_perm.reshape(2, ROUNDS // 2, seqs, rows)
    perm_send = jnp.transpose(perm_parts, (2, 0, 1, 3))
    perm_send = jnp.broadcast_to(
        perm_send[:, None], (seqs, heads, 2, ROUNDS // 2, rows)
    ).reshape(wide, ROUNDS // 2, rows)
    perm_got = lax.all_to_all(perm_send, "wide", 0, 0, tiled=True)
    tables = build_tables(jnp.transpose(perm_got, (1, 0, 2)).reshape(ROUNDS // 2, wide * rows))

    unit_columns = 2 * head_width
    gathered = [early]
    biases = jnp.stack([out_bias, down_bias])
    other = swap(biases, "narrow", 1)
    out_bias, down_bias = jnp.where(
        narrow_index == 0,
        jnp.concatenate([biases, other], axis=-1),
        jnp.concatenate([other, biases], axis=-1),
    )

    saved = []
    ffn_parts = [() for _ in chunks]
    afters = [[], [*tables, *first, out_bias, down_bias]]
    for layer in range(LAYERS):
        normed, sources = [], []
        for q in chunks:
            second[q], normed_q, units = enter_attention(
                seqs, layer, second[q], attn_norm_gain, attn_norm_bias, gathered[layer], 0,
                unit_columns, ffn_parts[q], afters[min(q, 1)] if layer == 0 else (),
            )
            normed.append(normed_q)
            own = chip_exchange(units)
            sources += [own, swap(own, "wide", 1)]
        sorted_rows, own, sib = attention_forward(pos, sources, tables, ())
        attn, stats, units = combine_cores(own, swap(sib, "wide", 1))
        after = []
        if layer == 0:
            grad_second, grad_first = widen((second_cot, first_cot), sources[-2:-1])
            after = [*grad_second, *grad_first]
        if layer + 1 < LAYERS:
            pieces = pack_columns([flat_weight(layer + 1), out_weight[layer + 1]], units[:1])
            gathered.append(lax.all_gather(pieces, "wide", axis=0, tiled=True))
        second_now, attn_tok, ffn_in, pre_act = list(second), [], [], []
        backs = [chip_exchange(units[q]) for q in chunks]
        for q in chunks:
            part, attn_tok_q = merge_units(seqs, backs[q], gathered[layer], 2, after)
            attn_tok.append(attn_tok_q)
            first[q], ffn_in_q, pre_q, part = feed_forward(
                layer, first[q], part, swap(part, "narrow", 1), out_bias,
                ffn_norm_gain, ffn_norm_bias, up_weight, up_bias, down_weight,
            )
            ffn_in.append(ffn_in_q)
            pre_act.append(pre_q)
            ffn_parts[q] = (part, swap(part, "narrow", 1), down_bias)
        saved.append((second_now, normed, sorted_rows, attn, stats, attn_tok, list(first), ffn_in, pre_act))
    first_out = narrow_chunks(pos, first, seqs)
    last_parts = [part for q in chunks for part in ffn_parts[q][:2]] + [down_bias]
    second_out = narrow_chunks(pos, second, seqs, LAYERS - 1, last_parts)

    summed, waiting, done = [], [], []
    small_grads = [None] * LAYERS
    after = []
    for layer in reversed(range(LAYERS)):
        second_l, normed, sorted_rows, attn, stats, attn_tok, first_l, ffn_in, pre_act = saved[layer]
        branch, hidden, low, parts = [], [], [], []
        down_bias_grad, up_bias_grad = 0.0, 0.0
        for q in chunks:
            branch_q, hidden_q, low_q, down_bias_q, up_bias_q, part = feed_back(
                layer, grad_second[q], up_weight, down_weight, pre_act[q]
            )
            branch.append(branch_q)
            hidden.append(hidden_q)
            low.append(low_q)
            parts.append((part, swap(part, "narrow", 1)))
            down_bias_grad += down_bias_q
            up_bias_grad += up_bias_q
        pairs = waiting + [(ffn_in, low), (branch, hidden)]
        widths = [right[0].shape[1] for _, right in pairs]
        columns = sum(widths) + head_width
        products = weight_products(pairs, columns, after=done)
        out_low, units = [], []
        ffn_gain_grad, ffn_bias_grad, out_bias_grad = 0.0, 0.0, 0.0
        for q in chunks:
            *results, units_q = leave_ffn(
                seqs, layer, first_l[q], *parts[q], grad_first[q], ffn_norm_gain,
                gathered[layer], 2, head_width, [*units, products] if q > 0 else (),
            )
            grad_first[q] = results[0]
            out_low.append(results[1])
            ffn_gain_grad += results[2]
            ffn_bias_grad += results[3]
            out_bias_grad += results[4]
            units.append(chip_exchange(units_q))
        products = weight_products(
            [(out_low, attn_tok)], columns, columns - head_width, products
        )
        summed += sum_rows(products, widths + [head_width])
        sources = []
        for q in chunks:
            own = join_grads(q, attn, stats, units[q], [products] if q > 0 else ())
            sources += [own, swap(own, "wide", 1)]
        early_small = jnp.concatenate(
            [
                own_half(grad)
                for grad in (ffn_gain_grad, ffn_bias_grad, out_bias_grad, down_bias_grad)
            ]
            + [up_bias_grad.reshape(-1, half)]
        )
        own, sib = attention_backward(pos, sources, sorted_rows, tables, [early_small])
        units = add_cores(own, swap(sib, "wide", 1))
        grad_tok, attn_gain_grad, attn_bias_grad = [], 0.0, 0.0
        backs = [chip_exchange(units[q]) for q in chunks]
        for q in chunks:
            part, grad_tok_q = merge_units(
                seqs, backs[q], gathered[layer], 0, grad_second[:1] if q > 0 and layer == 0 else ()
            )
            grad_tok.append(grad_tok_q)
            grad_second[q], gain_q, shift_q = finish_attention(
                layer, second_l[q], part, swap(part, "narrow", 1), grad_second[q], attn_norm_gain
            )
            attn_gain_grad += gain_q
            attn_bias_grad += shift_q
        waiting = [(normed, grad_tok)]
        done = summed[-1:]
        late_small = jnp.concatenate([own_half(attn_gain_grad), own_half(attn_bias_grad)])
        small_grads[layer] = jnp.concatenate([late_small, early_small])
    summed.append(reduce_rows(weight_products(waiting, unit_columns)))
    first_grad = narrow_chunks(pos, grad_first, seqs)
    second_grad = narrow_chunks(pos, grad_second, seqs)

    small = sum_wide(jnp.stack(small_grads))
    other = swap(small[:, :4], "narrow", 1)
    paired = jnp.where(
        narrow_index == 0,
        jnp.concatenate([small[:, :4], other], axis=-1),
        jnp.concatenate([other, small[:, :4]], axis=-1),
    )
    order = [(4, 5, 6, 7), (0, 1, 2, 3)]
    weight_grads = [None] * LAYERS
    for layer in range(LAYERS):
        up_sum, down_sum, out_sum, unit_sum = [summed[at] for at in order[layer]]
        by_unit = unit_sum.reshape(weight_rows, heads, 2, HD)
        weight_grads[layer] = (
            by_unit[:, :, 0].reshape(weight_rows, head_width),
            by_unit[:, :, 1].reshape(weight_rows, head_width),
            out_sum,
            up_sum,
            down_sum,
        )

    def stacked(slot):
        return jnp.stack([weight_grads[layer][slot] for layer in range(LAYERS)])

    return (
        first_out,
        second_out,
        first_grad,
        second_grad,
        paired[:, 0],
        paired[:, 1],
        stacked(0),
        stacked(1),
        stacked(2),
        small[:, 4],
        paired[:, 2],
        paired[:, 3],
        stacked(3),
        small[:, 6:].reshape(LAYERS, hidden_width),
        stacked(4),
        small[:, 5],
    )


def solution(mesh):
    streams = P(None, "wide", "narrow")
    features = P(None, "narrow")
    hidden = P(None, None, "narrow")
    return jax.shard_map(
        shards,
        mesh=mesh,
        in_specs=(
            streams, streams, P(), P(), streams, streams, streams, features, P(), P(),
            hidden, features, hidden, features, P(None, None, "wide"), streams, streams,
        ),
        out_specs=(
            streams, streams, streams, streams, P(), P(), streams, streams, streams,
            features, P(), P(), streams, features, streams, features,
        ),
        check_vma=False,
    )
```

```python
import functools

import jax
import jax.numpy as jnp
from jax import lax
from jax.experimental import pallas as pl
from jax.experimental.pallas import tpu as pltpu
from jax.sharding import PartitionSpec as P

HD = 128
GROUP = 64
ROUNDS = 4
LAYERS = 2
BLOCK = 256
F32 = jnp.float32
BF16 = jnp.bfloat16
SCALE = HD ** (-0.5)
VMEM_LIMIT = 56 * 1024 * 1024
PAIRS = 8
SHARE = 0.01
CHUNKS = 2
FFN_STEPS = 2


def swap(value, axis, mask):
    count = lax.axis_size(axis)
    return lax.ppermute(value, axis, [(source, source ^ mask) for source in range(count)])


def dot(left, right, dims):
    return lax.dot_general(left, right, (dims, ((), ())), preferred_element_type=F32)


def mm(left, right):
    return dot(left, right, ((1,), (0,)))


def mm_t(left, right):
    return dot(left, right, ((1,), (1,)))


def t_mm(left, right):
    return dot(left, right, ((0,), (0,)))


def chip_exchange(units):
    count = lax.axis_size("wide")
    groups = [list(range(core, count, 2)) for core in range(2)]
    return lax.all_to_all(units, "wide", 0, 0, tiled=True, axis_index_groups=groups)


def split3(value):
    high = value.astype(BF16)
    rest = value - high.astype(F32)
    mid = rest.astype(BF16)
    low = (rest - mid.astype(F32)).astype(BF16)
    return high.astype(F32), mid.astype(F32), low.astype(F32)


def layer_norm(stream, gain, shift):
    centre = stream - jnp.mean(stream, axis=-1, keepdims=True)
    spread = jnp.mean(centre * centre, axis=-1, keepdims=True)
    return centre * lax.rsqrt(spread + 1e-05) * gain + shift


def layer_norm_back(stream, gain, grad):
    centre = stream - jnp.mean(stream, axis=-1, keepdims=True)
    inv = lax.rsqrt(jnp.mean(centre * centre, axis=-1, keepdims=True) + 1e-05)
    unit = centre * inv
    scaled = grad * gain
    back = inv * (
        scaled
        - jnp.mean(scaled, axis=-1, keepdims=True)
        - unit * jnp.mean(scaled * unit, axis=-1, keepdims=True)
    )
    return back, unit


def build_tables(tokens):
    rounds, seq = tokens.shape
    blocks = seq // BLOCK
    rank_rows = BLOCK // blocks
    tokens = tokens.reshape(rounds, blocks, BLOCK)
    run = tokens // BLOCK
    row = tokens % BLOCK
    onehot = (run[..., None] == jnp.arange(blocks, dtype=jnp.int32)).astype(BF16)
    before = (jnp.arange(BLOCK)[:, None] > jnp.arange(BLOCK)[None, :]).astype(BF16)
    counts = jnp.einsum("jl,rkla->rkja", before, onehot, preferred_element_type=F32)
    rank = jnp.sum(onehot.astype(F32) * counts, axis=-1).astype(jnp.int32)
    slot = run * rank_rows + rank
    iota = jnp.arange(BLOCK, dtype=jnp.int32)
    into = (slot[..., None] == iota).astype(BF16)
    into_t = (slot[..., None, :] == iota[:, None]).astype(BF16)
    wants = jnp.einsum("rknj,rkj->rkn", into_t, row.astype(BF16), preferred_element_type=F32)
    wants = wants.reshape(rounds, blocks, blocks, rank_rows)
    wants = jnp.transpose(wants, (0, 2, 1, 3)).reshape(rounds, blocks, BLOCK).astype(jnp.int32)
    out_of = (wants[..., None] == iota).astype(BF16)
    out_of_t = (wants[..., None, :] == iota[:, None]).astype(BF16)
    return jnp.transpose(out_of, (1, 0, 2, 3)), into, out_of_t, into_t


def token_copies(pos_ref, sources, tok, sems):
    core = pos_ref[0]
    chunks = len(sources) // 2
    slots, rows, _ = sources[0].shape
    copies = []
    for place, source in enumerate(sources):
        chunk, half = place // 2, place % 2
        for k in range(slots):
            device = 2 * k + (core ^ half)
            start = pl.multiple_of((device * chunks + chunk) * rows, rows)
            copies.append(
                pltpu.make_async_copy(
                    source.at[k], tok.at[pl.ds(start, rows)], sems.at[len(copies)]
                )
            )
    return copies


def table_copies(sources, targets, sems):
    return [
        pltpu.make_async_copy(source, target, sems.at[k])
        for k, (source, target) in enumerate(zip(sources, targets))
    ]


def store_run(pos_ref, buffer, run, value):
    core = pos_ref[0]
    _, chunks, _, rows, _ = buffer.shape
    for part in range(BLOCK // rows):
        device = run * (BLOCK // (rows * chunks)) + part // chunks
        buffer[(device & 1) ^ core, part % chunks, device >> 1] = value[
            part * rows : (part + 1) * rows
        ]


def send_halves(buffer, own_hbm, sib_hbm, sems):
    copies = [
        pltpu.make_async_copy(buffer.at[1], sib_hbm, sems.at[0]),
        pltpu.make_async_copy(buffer.at[0], own_hbm, sems.at[1]),
    ]
    for copy in copies:
        copy.start()
    for copy in copies:
        copy.wait()


def spread(first, count, width):
    row = lax.broadcasted_iota(jnp.int32, (HD, width), 0)
    return jnp.where((row >= first) & (row < first + count), 1.0, 0.0).astype(BF16)


def pack_stats(columns):
    lane = lax.broadcasted_iota(jnp.int32, columns[0].shape, 1)
    extra = jnp.zeros(columns[0].shape, F32)
    for place, column in enumerate(columns):
        extra = jnp.where(lane == place, column, extra)
    return extra


def permute_in(tok, out_of, mixed, blocks):
    rank = BLOCK // blocks
    for a in range(blocks):
        source = tok[a * BLOCK : (a + 1) * BLOCK, :]
        moved = mm(out_of[a].reshape(2 * BLOCK, BLOCK), source).astype(BF16)
        for r in range(2):
            mixed[r, :, a] = moved[r * BLOCK : (r + 1) * BLOCK].reshape(blocks, rank, 2 * HD)


def split_rows(tile):
    lane = lax.broadcasted_iota(jnp.int32, tile.shape, 1)
    zero = jnp.zeros_like(tile)
    return jnp.concatenate(
        [jnp.where(lane < GROUP, tile, zero), jnp.where(lane >= GROUP, tile, zero)], axis=0
    )


def split_lanes(tile):
    row = lax.broadcasted_iota(jnp.int32, tile.shape, 0)
    zero = jnp.zeros_like(tile)
    return jnp.concatenate(
        [jnp.where(row < GROUP, tile, zero), jnp.where(row >= GROUP, tile, zero)], axis=1
    )


def side_by_side(ref, base):
    return jnp.concatenate(
        [ref[base : base + 2 * GROUP, :], ref[base + GROUP : base + 3 * GROUP, :]], axis=1
    )


def one_above(ref, base):
    return jnp.concatenate(
        [ref[base : base + 2 * GROUP, :], ref[base + GROUP : base + 3 * GROUP, :]], axis=0
    )


def self_mask():
    row = lax.broadcasted_iota(jnp.int32, (2 * GROUP, 2 * GROUP), 0)
    lane = lax.broadcasted_iota(jnp.int32, (2 * GROUP, 2 * GROUP), 1)
    return row == lane % GROUP + GROUP


def unit_keys(query):
    return query * lax.rsqrt(jnp.mean(query * query, axis=-1, keepdims=True) + 1e-06)


def forward_kernel(chunks, extras, pos_ref, *refs):
    sources, refs = refs[: 2 * chunks], refs[2 * chunks + extras :]
    (
        out_of_hbm, into_hbm, out_of_t_hbm, into_t_hbm, sorted_hbm, own_hbm, sib_hbm,
        tok, mixed, keys, vals, placed, buffer, out_of, into, out_of_t, into_t,
        tok_sems, table_sems, out_sems, send_sems,
    ) = refs
    seq = tok.shape[0]
    blocks = seq // BLOCK
    rank = BLOCK // blocks
    loads = token_copies(pos_ref, sources, tok, tok_sems)
    tables = table_copies(
        (out_of_hbm, into_hbm, into_t_hbm, out_of_t_hbm), (out_of, into, into_t, out_of_t), table_sems
    )
    for copy in loads:
        copy.start()
    for copy in tables:
        copy.start()
    for copy in loads:
        copy.wait()
    tables[0].wait()
    permute_in(tok, out_of, mixed, blocks)
    tables[1].wait()
    outs = []
    for r in range(2):
        for k in range(blocks):
            base = k * BLOCK
            rows_sorted = mm(into[r, k], mixed[r, k].reshape(BLOCK, 2 * HD))
            placed[r, base : base + BLOCK, :] = rows_sorted.astype(BF16)
            where = slice(base + GROUP, base + GROUP + BLOCK)
            keys[r, where, :] = unit_keys(rows_sorted[:, :HD]).astype(BF16)
            vals[r, where, :] = rows_sorted[:, HD:].astype(BF16)
        keys[r, 0:GROUP, :] = keys[r, seq : seq + GROUP, :]
        vals[r, 0:GROUP, :] = vals[r, seq : seq + GROUP, :]
        outs.append(pltpu.make_async_copy(placed.at[r], sorted_hbm.at[r], out_sems.at[r]))
        outs[-1].start()
    tables[2].wait()
    own = jnp.concatenate([self_mask()] * PAIRS, axis=1)
    wide = PAIRS * 2 * GROUP
    for r in range(2):
        for first in range(0, seq, wide):
            bases = [first + p * 2 * GROUP for p in range(PAIRS)]
            flipped = [placed[r, base : base + 2 * GROUP, 0:HD].T for base in bases]
            raw = jnp.concatenate(
                [
                    mm(side_by_side(keys.at[r], base), split_rows(tile))
                    for base, tile in zip(bases, flipped)
                ],
                axis=1,
            )
            scores = jnp.where(own, -1000000000.0, raw * SCALE)
            top = jnp.max(scores, axis=0, keepdims=True)
            weight = jnp.exp(scores - top)
            total = jnp.sum(weight, axis=0, keepdims=True)
            probs = (weight * (1.0 / total)).astype(BF16)
            row = lax.broadcasted_iota(jnp.int32, (8, wide), 0)
            stats = jnp.zeros((8, wide), F32)
            for place, part in enumerate(split3(top + jnp.log(total))):
                stats = jnp.where(row == place, part, stats)
            stats = jnp.concatenate([stats, jnp.zeros((HD - 8, wide), F32)], axis=0)
            lanes = [slice(p * 2 * GROUP, (p + 1) * 2 * GROUP) for p in range(PAIRS)]
            turned = [probs[:, lane].T for lane in lanes]
            extra = [stats[:, lane].T.astype(BF16) for lane in lanes]
            result = [
                mm(split_lanes(tile), one_above(vals.at[r], base)).astype(BF16)
                for tile, base in zip(turned, bases)
            ]
            packed = jnp.concatenate(
                [jnp.concatenate(pair, axis=1) for pair in zip(result, extra)], axis=0
            )
            for part in range(wide // BLOCK):
                k = first // BLOCK + part
                back = mm(into_t[r, k], packed[part * BLOCK : (part + 1) * BLOCK]).astype(BF16)
                mixed[r, k] = back.reshape(blocks, rank, 2 * HD)
    tables[3].wait()
    zero = jnp.zeros((HD, HD), BF16)
    ones = spread(0, 3, HD)
    ones = jnp.concatenate(
        [jnp.concatenate([ones, zero], axis=1), jnp.concatenate([zero, ones], axis=1)], axis=0
    )
    for a in range(blocks):
        moved = [mm(out_of_t[r, a], mixed[r, :, a].reshape(BLOCK, 2 * HD)) for r in range(2)]
        lse = mm(jnp.concatenate([m[:, HD:] for m in moved], axis=1).astype(BF16), ones)
        lse_a, lse_b = lse[:, :HD], lse[:, HD:]
        top = jnp.maximum(lse_a, lse_b)
        weight_a, weight_b = jnp.exp(lse_a - top), jnp.exp(lse_b - top)
        total = weight_a + weight_b
        value = (moved[0][:, :HD] * weight_a + moved[1][:, :HD] * weight_b) * (1.0 / total)
        extra = pack_stats(split3(top + jnp.log(total)))
        store_run(pos_ref, buffer, a, jnp.concatenate([value, extra], axis=1).astype(BF16))
    send_halves(buffer, own_hbm, sib_hbm, send_sems)
    for copy in outs:
        copy.wait()


def backward_kernel(chunks, extras, pos_ref, *refs):
    sources, refs = refs[: 2 * chunks], refs[2 * chunks + extras :]
    (
        sorted_hbm, out_of_hbm, into_hbm, out_of_t_hbm, into_t_hbm, own_hbm, sib_hbm,
        tok, mixed, keys, vals, placed, grads, query_use, key_grad, val_grad, buffer,
        out_of, into, out_of_t, into_t, tok_sems, table_sems, in_sems, send_sems,
    ) = refs
    seq = tok.shape[0]
    blocks = seq // BLOCK
    rank = BLOCK // blocks
    loads = token_copies(pos_ref, sources, tok, tok_sems)
    tables = table_copies(
        (out_of_hbm, into_hbm, into_t_hbm, out_of_t_hbm), (out_of, into, into_t, out_of_t), table_sems
    )
    sorted_in = pltpu.make_async_copy(sorted_hbm, placed, in_sems.at[0])
    for copy in loads:
        copy.start()
    tables[0].start()
    sorted_in.start()
    for copy in tables[1:]:
        copy.start()
    for copy in loads:
        copy.wait()
    tables[0].wait()
    permute_in(tok, out_of, mixed, blocks)
    sorted_in.wait()
    tables[1].wait()
    for r in range(2):
        for k in range(blocks):
            here = slice(k * BLOCK, (k + 1) * BLOCK)
            where = slice(k * BLOCK + GROUP, (k + 1) * BLOCK + GROUP)
            grads[r, here, :] = mm(into[r, k], mixed[r, k].reshape(BLOCK, 2 * HD)).astype(BF16)
            keys[r, where, :] = unit_keys(placed[r, here, 0:HD].astype(F32)).astype(BF16)
            vals[r, where, :] = placed[r, here, HD:]
        keys[r, 0:GROUP, :] = keys[r, seq : seq + GROUP, :]
        vals[r, 0:GROUP, :] = vals[r, seq : seq + GROUP, :]
        key_grad[r, 0:GROUP, :] = jnp.zeros((GROUP, HD), F32)
        val_grad[r, 0:GROUP, :] = jnp.zeros((GROUP, HD), F32)
    own = jnp.concatenate([self_mask()] * PAIRS, axis=1)
    wide = PAIRS * 2 * GROUP
    lanes = [slice(p * 2 * GROUP, (p + 1) * 2 * GROUP) for p in range(PAIRS)]
    for r in range(2):
        for first in range(0, seq, wide):
            bases = [first + p * 2 * GROUP for p in range(PAIRS)]
            query = [placed[r, base : base + 2 * GROUP, 0:HD] for base in bases]
            grad = [grads[r, base : base + 2 * GROUP, 0:HD] for base in bases]
            stats = jnp.concatenate(
                [
                    grads[r, base : base + 2 * GROUP, HD:].astype(F32).T[0:8] for base in bases
                ],
                axis=1,
            )
            delta = stats[0:1] + stats[1:2] + stats[2:3]
            lse = stats[3:4] + stats[4:5] + stats[5:6]
            query_t = [split_rows(tile.T) for tile in query]
            grad_t = [split_rows(tile.T) for tile in grad]
            raw = jnp.concatenate(
                [mm(side_by_side(keys.at[r], base), tile) for base, tile in zip(bases, query_t)],
                axis=1,
            )
            prob_grad = jnp.concatenate(
                [mm(side_by_side(vals.at[r], base), tile) for base, tile in zip(bases, grad_t)],
                axis=1,
            )
            probs = jnp.exp(jnp.where(own, -1000000000.0, raw * SCALE) - lse)
            score_grad = (probs * (prob_grad - delta)).astype(BF16)
            probs = probs.astype(BF16)
            turned = [score_grad[:, lane].T for lane in lanes]
            for tile, base in zip(turned, bases):
                query_use[r, base : base + 2 * GROUP, :] = (
                    mm(split_lanes(tile), one_above(keys.at[r], base)) * SCALE
                )
            key_parts = [
                mm(split_rows(score_grad[:, lane]), tile) * SCALE for lane, tile in zip(lanes, query)
            ]
            val_parts = [mm(split_rows(probs[:, lane]), tile) for lane, tile in zip(lanes, grad)]
            for target, parts in ((key_grad, key_parts), (val_grad, val_parts)):
                target[r, first : first + GROUP, :] += parts[0][:GROUP]
                for p, (part, base) in enumerate(zip(parts, bases)):
                    target[r, base + GROUP : base + 2 * GROUP, :] = (
                        part[GROUP : 2 * GROUP] + part[2 * GROUP : 3 * GROUP]
                    )
                    last = part[3 * GROUP :]
                    if p + 1 < PAIRS:
                        last = last + parts[p + 1][:GROUP]
                    target[r, base + 2 * GROUP : base + 3 * GROUP, :] = last
        key_grad[r, seq : seq + GROUP, :] += key_grad[r, 0:GROUP, :]
        val_grad[r, seq : seq + GROUP, :] += val_grad[r, 0:GROUP, :]
    tables[2].wait()
    for r in range(2):
        for k in range(blocks):
            here = slice(k * BLOCK, (k + 1) * BLOCK)
            where = slice(k * BLOCK + GROUP, (k + 1) * BLOCK + GROUP)
            query = placed[r, here, 0:HD].astype(F32)
            inv = lax.rsqrt(jnp.mean(query * query, axis=-1, keepdims=True) + 1e-06)
            grad = key_grad[r, where, :]
            inner = jnp.mean(grad * query, axis=-1, keepdims=True)
            total = query_use[r, here, :] + inv * (grad - query * (inner * inv * inv))
            packed = jnp.concatenate([total, val_grad[r, where, :]], axis=1).astype(BF16)
            back = mm(into_t[r, k], packed).astype(BF16)
            mixed[r, k] = back.reshape(blocks, rank, 2 * HD)
    tables[3].wait()
    for a in range(blocks):
        total = mm(out_of_t[0, a], mixed[0, :, a].reshape(BLOCK, 2 * HD)) + mm(
            out_of_t[1, a], mixed[1, :, a].reshape(BLOCK, 2 * HD)
        )
        store_run(pos_ref, buffer, a, total.astype(BF16))
    send_halves(buffer, own_hbm, sib_hbm, send_sems)


def params():
    return pltpu.CompilerParams(vmem_limit_bytes=VMEM_LIMIT)


def cost(flops, moved):
    return pl.CostEstimate(flops=int(flops * SHARE), bytes_accessed=int(moved * SHARE), transcendentals=0)


IN_SMEM = pl.BlockSpec(memory_space=pltpu.SMEM)
IN_VMEM = pl.BlockSpec(memory_space=pltpu.VMEM)
ANYWHERE = pl.BlockSpec(memory_space=pl.ANY)


def bf16_out(*shape):
    return jax.ShapeDtypeStruct(shape, BF16)


def f32_out(*shape):
    return jax.ShapeDtypeStruct(shape, F32)


def table_scratch(blocks):
    return [
        pltpu.VMEM((blocks, 2, BLOCK, BLOCK), BF16),
        pltpu.VMEM((2, blocks, BLOCK, BLOCK), BF16),
        pltpu.VMEM((2, blocks, BLOCK, BLOCK), BF16),
        pltpu.VMEM((2, blocks, BLOCK, BLOCK), BF16),
    ]


def attention_forward(pos, sources, tables, after):
    chunks = len(sources) // 2
    slots, rows, width = sources[0].shape
    seq = 2 * slots * rows * chunks
    blocks = seq // BLOCK
    half = bf16_out(chunks, slots, rows, width)
    return pl.pallas_call(
        functools.partial(forward_kernel, chunks, len(after)),
        out_shape=(bf16_out(2, seq, width), half, half),
        in_specs=[IN_SMEM] + [ANYWHERE] * (2 * chunks + len(after) + 4),
        out_specs=(ANYWHERE, ANYWHERE, ANYWHERE),
        scratch_shapes=[
            pltpu.VMEM((seq, width), BF16),
            pltpu.VMEM((2, blocks, blocks, BLOCK // blocks, width), BF16),
            pltpu.VMEM((2, seq + GROUP, HD), BF16),
            pltpu.VMEM((2, seq + GROUP, HD), BF16),
            pltpu.VMEM((2, seq, width), BF16),
            pltpu.VMEM((2, chunks, slots, rows, width), BF16),
            *table_scratch(blocks),
            pltpu.SemaphoreType.DMA((2 * slots * chunks,)),
            pltpu.SemaphoreType.DMA((4,)),
            pltpu.SemaphoreType.DMA((2,)),
            pltpu.SemaphoreType.DMA((2,)),
        ],
        compiler_params=params(),
        cost_estimate=cost(16e9, 24e6),
        name="attend_forward",
    )(pos, *sources, *after, *tables)


def attention_backward(pos, sources, sorted_rows, tables, after):
    chunks = len(sources) // 2
    slots, rows, width = sources[0].shape
    seq = 2 * slots * rows * chunks
    blocks = seq // BLOCK
    half = bf16_out(chunks, slots, rows, width)
    return pl.pallas_call(
        functools.partial(backward_kernel, chunks, len(after)),
        out_shape=(half, half),
        in_specs=[IN_SMEM] + [ANYWHERE] * (2 * chunks + len(after) + 5),
        out_specs=(ANYWHERE, ANYWHERE),
        scratch_shapes=[
            pltpu.VMEM((seq, width), BF16),
            pltpu.VMEM((2, blocks, blocks, BLOCK // blocks, width), BF16),
            pltpu.VMEM((2, seq + GROUP, HD), BF16),
            pltpu.VMEM((2, seq + GROUP, HD), BF16),
            pltpu.VMEM((2, seq, width), BF16),
            pltpu.VMEM((2, seq, width), BF16),
            pltpu.VMEM((2, seq, HD), F32),
            pltpu.VMEM((2, seq + GROUP, HD), F32),
            pltpu.VMEM((2, seq + GROUP, HD), F32),
            pltpu.VMEM((2, chunks, slots, rows, width), BF16),
            *table_scratch(blocks),
            pltpu.SemaphoreType.DMA((2 * slots * chunks,)),
            pltpu.SemaphoreType.DMA((4,)),
            pltpu.SemaphoreType.DMA((1,)),
            pltpu.SemaphoreType.DMA((2,)),
        ],
        compiler_params=params(),
        cost_estimate=cost(18e9, 26e6),
        name="attend_backward",
    )(pos, *sources, *after, sorted_rows, *tables)


def unit_slices(seqs, heads, rows, width):
    return [
        (slice(seq * rows, (seq + 1) * rows), slice(head * width, (head + 1) * width))
        for seq in range(seqs)
        for head in range(heads)
    ]


def column_block(rows, width, place):
    return pl.BlockSpec((rows, width), lambda i: (0, place))


def whole_block(array):
    return pl.BlockSpec(array.shape, lambda i: (0,) * len(array.shape))


def pack_kernel(count, *refs):
    out_ref = refs[-1]
    start = 0
    for ref in refs[:count]:
        out_ref[:, start : start + ref.shape[1]] = ref[...]
        start += ref.shape[1]


def pack_columns(pieces, after):
    rows, columns = pieces[0].shape[0], sum(piece.shape[1] for piece in pieces)
    return pl.pallas_call(
        functools.partial(pack_kernel, len(pieces)),
        out_shape=bf16_out(rows, columns),
        in_specs=[IN_VMEM] * len(pieces) + [ANYWHERE] * len(after),
        out_specs=IN_VMEM,
        compiler_params=params(),
        name="pack_columns",
    )(*pieces, *after)


def lower_kernel(count, *refs):
    for source, target in zip(refs[:count], refs[-count:]):
        target[...] = source[...].astype(BF16)


def lower_arrays(arrays, after):
    return pl.pallas_call(
        functools.partial(lower_kernel, len(arrays)),
        out_shape=[bf16_out(*array.shape) for array in arrays],
        in_specs=[IN_VMEM] * len(arrays) + [ANYWHERE] * len(after),
        out_specs=[IN_VMEM] * len(arrays),
        compiler_params=params(),
        name="lower_arrays",
    )(*arrays, *after)


def widen_kernel(pos_ref, mine_ref, other_ref, *out_refs):
    seqs, rows, half = mine_ref.shape
    count = rows // len(out_refs)
    mine_at = pl.ds(pl.multiple_of(pos_ref[1] * half, half), half)
    other_at = pl.ds(pl.multiple_of((1 - pos_ref[1]) * half, half), half)
    for q, out_ref in enumerate(out_refs):
        for seq in range(seqs):
            at = slice(seq * count, (seq + 1) * count)
            source = slice(q * count, (q + 1) * count)
            out_ref[at, mine_at] = mine_ref[seq, source]
            out_ref[at, other_at] = other_ref[seq, source].astype(F32)


def widen_chunks(pos, mine, other):
    seqs, rows, half = mine.shape
    out = f32_out(seqs * rows // CHUNKS, 2 * half)
    return list(
        pl.pallas_call(
            widen_kernel,
            out_shape=[out] * CHUNKS,
            in_specs=[IN_SMEM, IN_VMEM, IN_VMEM],
            out_specs=[IN_VMEM] * CHUNKS,
            compiler_params=params(),
            cost_estimate=cost(1e6, 4e6),
            name="widen_chunks",
        )(pos, mine, other)
    )


def narrow_kernel(layer, pos_ref, *refs):
    out_ref = refs[-1]
    seqs, rows, half = out_ref.shape
    count = rows // CHUNKS
    lanes = pl.ds(pl.multiple_of(pos_ref[1] * half, half), half)
    for q in range(CHUNKS):
        for seq in range(seqs):
            at = slice(seq * count, (seq + 1) * count)
            value = refs[q][at, lanes]
            if layer is not None:
                own, other, bias = refs[CHUNKS + q], refs[2 * CHUNKS], refs[2 * CHUNKS + 1]
                got = other[q * seqs * count + seq * count : q * seqs * count + (seq + 1) * count]
                value = value + (own[at, lanes].astype(F32) + got.astype(F32))
                value = value + bias[layer : layer + 1, lanes]
            out_ref[seq, q * count : (q + 1) * count] = value


def narrow_chunks(pos, chunks, seqs, layer=None, parts=(), after=()):
    toks, width = chunks[0].shape
    return pl.pallas_call(
        functools.partial(narrow_kernel, layer),
        out_shape=f32_out(seqs, toks * CHUNKS // seqs, width // 2),
        in_specs=[IN_SMEM]
        + [IN_VMEM] * (CHUNKS + len(parts))
        + [ANYWHERE] * len(after),
        out_specs=IN_VMEM,
        compiler_params=params(),
        cost_estimate=cost(1e6, 4e6),
        name="narrow_chunks",
    )(pos, *chunks, *parts, *after)


def enter_kernel(
    seqs, layer, parts, after, stream_ref, gain_ref, shift_ref, weight_ref, *refs
):
    stream = stream_ref[...]
    if parts:
        own_ref, other_ref, bias_ref, *refs = refs
        stream = stream + (own_ref[...].astype(F32) + other_ref[...].astype(F32))
        stream = stream + bias_ref[layer - 1 : layer]
    refs = refs[after:]
    if parts:
        refs[0][...] = stream
    normed_ref, out_ref = refs[-2:]
    row = slice(layer, layer + 1)
    normed = layer_norm(stream, gain_ref[row], shift_ref[row]).astype(BF16)
    normed_ref[...] = normed
    flat = mm(normed, weight_ref[...]).astype(BF16)
    slots, rows, width = out_ref.shape
    for k, at in enumerate(unit_slices(seqs, slots // seqs, rows, width)):
        out_ref[k] = flat[at]


def enter_attention(seqs, layer, stream, gain, shift, weight, place, columns, parts=(), after=()):
    toks, width = stream.shape
    slots = seqs * columns // (2 * HD)
    shapes = [bf16_out(toks, width), bf16_out(slots, toks // seqs, 2 * HD)]
    if parts:
        shapes = [f32_out(toks, width)] + shapes
    results = pl.pallas_call(
        functools.partial(enter_kernel, seqs, layer, len(parts) > 0, len(after)),
        grid=(1,),
        out_shape=shapes,
        in_specs=[whole_block(stream), whole_block(gain), whole_block(shift)]
        + [column_block(width, columns, place)]
        + [whole_block(part) for part in parts]
        + [ANYWHERE] * len(after),
        out_specs=[whole_block(shape) for shape in shapes],
        compiler_params=params(),
        cost_estimate=cost(2 * toks * width * columns, 5e6),
        name="enter_attention",
    )(stream, gain, shift, weight, *parts, *after)
    return results if parts else (stream, *results)


def merge_kernel(seqs, weight_ref, in_ref, *refs):
    part_ref, tok_ref = refs[-2:]
    slots, rows, width = in_ref.shape
    for k, at in enumerate(unit_slices(seqs, slots // seqs, rows, width)):
        tok_ref[at] = in_ref[k]
    part_ref[...] = mm_t(tok_ref[...], weight_ref[...]).astype(BF16)


def merge_units(seqs, units, weight, place, after=()):
    slots, rows, width = units.shape
    toks, columns = seqs * rows, slots // seqs * width
    shapes = (bf16_out(toks, weight.shape[0]), bf16_out(toks, columns))
    return pl.pallas_call(
        functools.partial(merge_kernel, seqs),
        grid=(1,),
        out_shape=shapes,
        in_specs=[column_block(weight.shape[0], columns, place), whole_block(units)]
        + [ANYWHERE] * len(after),
        out_specs=[whole_block(shape) for shape in shapes],
        compiler_params=params(),
        cost_estimate=cost(2 * toks * columns * weight.shape[0], 3e6),
        name="merge_units",
    )(weight, units, *after)


def both_stats(own, got):
    zero = jnp.zeros((HD, HD), BF16)
    ones = spread(0, 3, HD)
    ones = jnp.concatenate(
        [jnp.concatenate([ones, zero], axis=1), jnp.concatenate([zero, ones], axis=1)], axis=0
    )
    lse = mm(jnp.concatenate([own, got], axis=1), ones)
    return lse[:, :HD], lse[:, HD:]


def combine_kernel(after, own_ref, got_ref, *refs):
    attn_ref, stats_ref, *out_refs = refs[after:]
    chunks, slots, rows, _ = own_ref.shape
    for q in range(chunks):
        for k in range(slots):
            lse_a, lse_b = both_stats(own_ref[q, k, :, HD:], got_ref[q, k, :, HD:])
            top = jnp.maximum(lse_a, lse_b)
            weight_a, weight_b = jnp.exp(lse_a - top), jnp.exp(lse_b - top)
            total = weight_a + weight_b
            own = own_ref[q, k, :, :HD].astype(F32)
            got = got_ref[q, k, :, :HD].astype(F32)
            value = (own * weight_a + got * weight_b) * (1.0 / total)
            attn_ref[q, k] = value
            zero = jnp.zeros_like(total)
            stats_ref[q, k] = pack_stats(
                (zero, zero, zero) + split3(top + jnp.log(total))
            ).astype(BF16)
            out_refs[q][k] = value.astype(BF16)


def combine_cores(own, got, after=()):
    chunks, slots, rows, _ = own.shape
    results = pl.pallas_call(
        functools.partial(combine_kernel, len(after)),
        out_shape=[f32_out(chunks, slots, rows, HD), bf16_out(chunks, slots, rows, HD)]
        + [bf16_out(slots, rows, HD)] * chunks,
        in_specs=[IN_VMEM] * 2 + [ANYWHERE] * len(after),
        out_specs=[IN_VMEM] * (2 + chunks),
        compiler_params=params(),
        cost_estimate=cost(1e8, 5e6),
        name="combine_cores",
    )(own, got, *after)
    return results[0], results[1], results[2:]


def join_kernel(attn_ref, stats_ref, in_ref, *refs):
    out_ref = refs[-1]
    for k in range(in_ref.shape[0]):
        grad = in_ref[k]
        delta = jnp.sum(attn_ref[0, k] * grad.astype(F32), axis=-1, keepdims=True)
        delta = jnp.broadcast_to(delta, grad.shape)
        extra = pack_stats(split3(delta)) + stats_ref[0, k].astype(F32)
        out_ref[k] = jnp.concatenate([grad, extra.astype(BF16)], axis=1)


def join_grads(chunk, attn, stats, units, after=()):
    slots, rows, _ = units.shape
    spec = pl.BlockSpec((1, slots, rows, HD), lambda i: (chunk, 0, 0, 0))
    return pl.pallas_call(
        join_kernel,
        grid=(1,),
        out_shape=bf16_out(slots, rows, 2 * HD),
        in_specs=[spec, spec, pl.BlockSpec((slots, rows, HD), lambda i: (0, 0, 0))]
        + [ANYWHERE] * len(after),
        out_specs=pl.BlockSpec((slots, rows, 2 * HD), lambda i: (0, 0, 0)),
        compiler_params=params(),
        cost_estimate=cost(1e7, 2e6),
        name="join_grads",
    )(attn, stats, units, *after)


def add_kernel(after, own_ref, got_ref, *refs):
    for q, out_ref in enumerate(refs[after:]):
        total = own_ref[q].astype(F32) + got_ref[q].astype(F32)
        out_ref[...] = total.astype(BF16)


def add_cores(own, got, after=()):
    chunks, slots, rows, width = own.shape
    return pl.pallas_call(
        functools.partial(add_kernel, len(after)),
        out_shape=[bf16_out(slots, rows, width)] * chunks,
        in_specs=[IN_VMEM] * 2 + [ANYWHERE] * len(after),
        out_specs=[IN_VMEM] * chunks,
        compiler_params=params(),
        cost_estimate=cost(1e6, 3e6),
        name="add_cores",
    )(own, got, *after)


def ffn_kernel(
    layer, stream_ref, own_ref, other_ref, bias_ref, gain_ref, shift_ref, up_ref, up_bias_ref,
    down_ref, *refs,
):
    new_ref, normed_ref, pre_ref, part_ref, acc = refs[-5:]
    step = pl.program_id(0)
    row = slice(layer, layer + 1)

    @pl.when(step == 0)
    def _():
        stream = stream_ref[...] + (own_ref[...].astype(F32) + other_ref[...].astype(F32))
        stream = stream + bias_ref[row]
        new_ref[...] = stream
        normed_ref[...] = layer_norm(stream, gain_ref[row], shift_ref[row]).astype(BF16)

    pre = mm(normed_ref[...], up_ref[0]) + up_bias_ref[row]
    pre_ref[...] = pre
    hidden = jax.nn.gelu(pre, approximate=True).astype(BF16)
    part = mm_t(hidden, down_ref[0])

    @pl.when(step == 0)
    def _():
        acc[...] = part

    @pl.when(step > 0)
    def _():
        acc[...] += part

    @pl.when(step == pl.num_programs(0) - 1)
    def _():
        part_ref[...] = acc[...].astype(BF16)


def feed_forward(layer, stream, own, other, bias, gain, shift, up, up_bias, down, after=()):
    toks, width = stream.shape
    hidden = up.shape[2]
    step = hidden // FFN_STEPS
    full = pl.BlockSpec((toks, width), lambda i: (0, 0))
    slab = pl.BlockSpec((1, width, step), lambda i: (layer, 0, i))
    return pl.pallas_call(
        functools.partial(ffn_kernel, layer),
        grid=(FFN_STEPS,),
        out_shape=(
            f32_out(toks, width), bf16_out(toks, width), f32_out(toks, hidden), bf16_out(toks, width),
        ),
        in_specs=[
            full, full, full, whole_block(bias), whole_block(gain), whole_block(shift), slab,
            pl.BlockSpec((LAYERS, step), lambda i: (0, i)), slab,
        ]
        + [ANYWHERE] * len(after),
        out_specs=(full, full, pl.BlockSpec((toks, step), lambda i: (0, i)), full),
        scratch_shapes=[pltpu.VMEM((toks, width), F32)],
        compiler_params=params(),
        cost_estimate=cost(4 * toks * width * hidden, 14e6),
        name="feed_forward",
    )(stream, own, other, bias, gain, shift, up, up_bias, down, *after)


def ffn_back_kernel(
    grad_ref, up_ref, down_ref, pre_ref,
    branch_ref, hidden_ref, low_ref, down_bias_ref, up_bias_ref, part_ref, acc,
):
    step = pl.program_id(0)

    @pl.when(step == 0)
    def _():
        grad = grad_ref[...]
        branch_ref[...] = grad.astype(BF16)
        down_bias_ref[...] = jnp.sum(grad, axis=0, keepdims=True)

    hidden_grad = mm(branch_ref[...], down_ref[0])
    pre = pre_ref[...]
    root = 0.7978845608028654
    square = pre * pre
    bend = jnp.tanh(root * (pre + 0.044715 * (square * pre)))
    half = 0.5 * (1.0 + bend)
    hidden_ref[...] = (pre * half).astype(BF16)
    slope = half + 0.5 * pre * (1.0 - bend * bend) * (root * (1.0 + 3 * 0.044715 * square))
    pre_grad = hidden_grad * slope
    up_bias_ref[...] = jnp.sum(pre_grad, axis=0, keepdims=True)
    low = pre_grad.astype(BF16)
    low_ref[...] = low
    part = mm_t(low, up_ref[0])

    @pl.when(step == 0)
    def _():
        acc[...] = part

    @pl.when(step > 0)
    def _():
        acc[...] += part

    @pl.when(step == pl.num_programs(0) - 1)
    def _():
        part_ref[...] = acc[...].astype(BF16)


def feed_back(layer, grad, up, down, pre):
    toks, width = grad.shape
    hidden = down.shape[2]
    step = hidden // FFN_STEPS
    full = pl.BlockSpec((toks, width), lambda i: (0, 0))
    slab = pl.BlockSpec((1, width, step), lambda i: (layer, 0, i))
    tall = pl.BlockSpec((toks, step), lambda i: (0, i))
    return pl.pallas_call(
        ffn_back_kernel,
        grid=(FFN_STEPS,),
        out_shape=(
            bf16_out(toks, width), bf16_out(toks, hidden), bf16_out(toks, hidden),
            f32_out(1, width), f32_out(1, hidden), bf16_out(toks, width),
        ),
        in_specs=[full, slab, slab, tall],
        out_specs=(
            full, tall, tall, pl.BlockSpec((1, width), lambda i: (0, 0)),
            pl.BlockSpec((1, step), lambda i: (0, i)), full,
        ),
        scratch_shapes=[pltpu.VMEM((toks, width), F32)],
        compiler_params=params(),
        cost_estimate=cost(4 * toks * width * hidden, 15e6),
        name="feed_back",
    )(grad, up, down, pre)


def products_kernel(counts, *refs):
    out_ref, turned = refs[-2:]
    step = pl.program_id(0)
    start = 0
    for place, count in enumerate(counts):
        lefts = refs[2 * CHUNKS * place : 2 * CHUNKS * place + CHUNKS]
        rights = refs[2 * CHUNKS * place + CHUNKS : 2 * CHUNKS * (place + 1)]

        @pl.when(step == start)
        def _(lefts=lefts):
            for q, left in enumerate(lefts):
                toks = left.shape[0]
                turned[:, q * toks : (q + 1) * toks] = left[...].T

        @pl.when((step >= start) & (step < start + count))
        def _(rights=rights):
            right = jnp.concatenate([right[...] for right in rights], axis=0)
            out_ref[...] = mm(turned[...], right).astype(BF16)

        start += count


def weight_products(pairs, columns, at=0, target=None, after=()):
    block = min(right[0].shape[1] for _, right in pairs)
    block = min(block, 512)
    counts = [right[0].shape[1] // block for _, right in pairs]
    toks, rows = pairs[0][0][0].shape
    specs, operands, start = [], [], 0
    for (left, right), count in zip(pairs, counts):
        specs += [pl.BlockSpec((toks, rows), lambda i: (0, 0))] * CHUNKS
        specs += [
            pl.BlockSpec(
                (toks, block),
                lambda i, start=start, count=count: (0, jnp.clip(i - start, 0, count - 1)),
            )
        ] * CHUNKS
        operands += [*left, *right]
        start += count
    more = [*after] if target is None else [target, *after]
    return pl.pallas_call(
        functools.partial(products_kernel, counts),
        grid=(start,),
        out_shape=bf16_out(rows, columns),
        in_specs=specs + [ANYWHERE] * len(more),
        out_specs=pl.BlockSpec((rows, block), lambda i: (0, i + at // block)),
        scratch_shapes=[pltpu.VMEM((rows, CHUNKS * toks), BF16)],
        input_output_aliases={} if target is None else {len(operands): 0},
        compiler_params=params(),
        cost_estimate=cost(2 * rows * CHUNKS * toks * start * block, 20e6),
        name="weight_products",
    )(*operands, *more)


def norm_back(
    layer, stream_ref, own_ref, other_ref, grad_ref, gain_ref, gain_out, shift_out
):
    grad = own_ref[...].astype(F32) + other_ref[...].astype(F32)
    back, unit = layer_norm_back(stream_ref[...], gain_ref[layer : layer + 1], grad)
    gain_out[...] = jnp.sum(grad * unit, axis=0, keepdims=True)
    shift_out[...] = jnp.sum(grad, axis=0, keepdims=True)
    return grad_ref[...] + back


def leave_kernel(
    seqs, layer, after, stream_ref, own_ref, other_ref, grad_ref, gain_ref, weight_ref, *refs
):
    new_ref, low_ref, gain_out, shift_out, bias_out, out_ref = refs[after:]
    grad = norm_back(
        layer, stream_ref, own_ref, other_ref, grad_ref, gain_ref, gain_out, shift_out
    )
    new_ref[...] = grad
    bias_out[...] = jnp.sum(grad, axis=0, keepdims=True)
    low = grad.astype(BF16)
    low_ref[...] = low
    flat = mm(low, weight_ref[...]).astype(BF16)
    slots, rows, width = out_ref.shape
    for k, at in enumerate(unit_slices(seqs, slots // seqs, rows, width)):
        out_ref[k] = flat[at]


def leave_ffn(
    seqs, layer, stream, own, other, grad, gain, weight, place, columns, after=()
):
    toks, width = stream.shape
    shapes = [f32_out(toks, width), bf16_out(toks, width)] + [f32_out(1, width)] * 3
    shapes.append(bf16_out(seqs * columns // HD, toks // seqs, HD))
    operands = (stream, own, other, grad, gain)
    return pl.pallas_call(
        functools.partial(leave_kernel, seqs, layer, len(after)),
        grid=(1,),
        out_shape=shapes,
        in_specs=[whole_block(operand) for operand in operands]
        + [column_block(width, columns, place)]
        + [ANYWHERE] * len(after),
        out_specs=[whole_block(shape) for shape in shapes],
        compiler_params=params(),
        cost_estimate=cost(2 * toks * width * columns, 6e6),
        name="leave_ffn",
    )(*operands, weight, *after)


def finish_kernel(layer, stream_ref, own_ref, other_ref, grad_ref, gain_ref, *refs):
    new_ref, gain_out, shift_out = refs[-3:]
    new_ref[...] = norm_back(
        layer, stream_ref, own_ref, other_ref, grad_ref, gain_ref, gain_out, shift_out
    )


def finish_attention(layer, stream, own, other, grad, gain, after=()):
    toks, width = stream.shape
    return pl.pallas_call(
        functools.partial(finish_kernel, layer),
        out_shape=(f32_out(toks, width), f32_out(1, width), f32_out(1, width)),
        in_specs=[IN_VMEM] * 5 + [ANYWHERE] * len(after),
        out_specs=(IN_VMEM,) * 3,
        compiler_params=params(),
        cost_estimate=cost(1e7, 4e6),
        name="finish_attention",
    )(stream, own, other, grad, gain, *after)


def reduce_rows(value):
    count = lax.axis_size("wide")
    index = lax.axis_index("wide")
    width = value.shape[1]
    block = value.shape[0] // count
    value = value.astype(BF16)
    stages = []
    bit = 1
    parts = count
    while bit < count:
        view = value.reshape(parts // 2, 2, block, width)
        mine = (index // bit) % 2
        sent = lax.dynamic_index_in_dim(view, 1 - mine, 1, keepdims=False)
        kept = lax.dynamic_index_in_dim(view, mine, 1, keepdims=False)
        value = kept.astype(F32) + swap(sent, "wide", bit).astype(F32)
        parts //= 2
        bit *= 2
        if bit < count:
            value = value.astype(BF16)
        stages.append(value)
    return stages[:-1] + [value.reshape(block, width)]


def sum_rows(value, widths):
    total = lax.psum_scatter(value, "wide", scatter_dimension=0, tiled=True).astype(F32)
    ends = [0]
    for width in widths:
        ends.append(ends[-1] + width)
    return [total[:, low:high] for low, high in zip(ends, ends[1:])]


def sum_wide(value):
    for bit in range(lax.axis_size("wide").bit_length() - 1):
        value = value + swap(value, "wide", 1 << bit)
    return value


def shards(
    first_in, second_in, attn_norm_gain, attn_norm_bias, qk_weight, value_weight, out_weight,
    out_bias, ffn_norm_gain, ffn_norm_bias, up_weight, up_bias, down_weight, down_bias,
    bucket_perm, first_cot, second_cot,
):
    seqs, rows, half = first_in.shape
    wide = lax.axis_size("wide")
    wide_index = lax.axis_index("wide")
    narrow_index = lax.axis_index("narrow")
    pos = jnp.stack([wide_index % 2, narrow_index]).astype(jnp.int32)
    weight_rows, head_width = qk_weight.shape[1:]
    heads = head_width // HD
    width = 2 * half
    hidden_width = up_bias.shape[1]
    chunks = range(CHUNKS)

    def own_half(full):
        return lax.dynamic_slice_in_dim(full, narrow_index * half, half, full.ndim - 1)

    def flat_weight(layer):
        pair = jnp.stack([qk_weight[layer], value_weight[layer]], axis=1)
        pair = pair.reshape(weight_rows, 2, heads, HD)
        return jnp.transpose(pair, (0, 2, 1, 3)).reshape(weight_rows, 2 * head_width)

    streams = (second_in, first_in, second_cot, first_cot)
    others = [swap(sent, "narrow", 1) for sent in lower_arrays(streams, ())]
    second, first = [widen_chunks(pos, streams[k], others[k]) for k in range(2)]
    early = lax.all_gather(
        jnp.concatenate([flat_weight(0), out_weight[0]], axis=1), "wide", axis=0, tiled=True
    )

    perm_parts = bucket_perm.reshape(2, ROUNDS // 2, seqs, rows)
    perm_send = jnp.transpose(perm_parts, (2, 0, 1, 3))
    perm_send = jnp.broadcast_to(
        perm_send[:, None], (seqs, heads, 2, ROUNDS // 2, rows)
    ).reshape(wide, ROUNDS // 2, rows)
    perm_got = lax.all_to_all(perm_send, "wide", 0, 0, tiled=True)
    tables = build_tables(jnp.transpose(perm_got, (1, 0, 2)).reshape(ROUNDS // 2, wide * rows))

    unit_columns = 2 * head_width
    gathered = [early]
    biases = jnp.stack([out_bias, down_bias])
    other = swap(biases, "narrow", 1)
    out_bias, down_bias = jnp.where(
        narrow_index == 0,
        jnp.concatenate([biases, other], axis=-1),
        jnp.concatenate([other, biases], axis=-1),
    )

    saved = []
    ffn_parts = [() for _ in chunks]
    afters = [[], [*tables, *first, *others[2:], out_bias, down_bias]]
    for layer in range(LAYERS):
        normed, sources = [], []
        for q in chunks:
            second[q], normed_q, units = enter_attention(
                seqs, layer, second[q], attn_norm_gain, attn_norm_bias, gathered[layer], 0,
                unit_columns, ffn_parts[q], afters[min(q, 1)],
            )
            normed.append(normed_q)
            own = chip_exchange(units)
            sources += [own, swap(own, "wide", 1)]
        sorted_rows, own, sib = attention_forward(pos, sources, tables, ())
        attn, stats, units = combine_cores(own, swap(sib, "wide", 1))
        after = []
        if layer == 0:
            grad_second, grad_first = [
                widen_chunks(pos, streams[k], others[k]) for k in range(2, 4)
            ]
            after = [*grad_second, *grad_first]
        if layer + 1 < LAYERS:
            pieces = pack_columns([flat_weight(layer + 1), out_weight[layer + 1]], units[:1])
            gathered.append(lax.all_gather(pieces, "wide", axis=0, tiled=True))
        second_now, attn_tok, ffn_in, pre_act = list(second), [], [], []
        backs = [chip_exchange(units[q]) for q in chunks]
        merged = []
        for q in chunks:
            part, attn_tok_q = merge_units(
                seqs, backs[q], gathered[layer], 2, after + attn_tok if q > 0 else ()
            )
            attn_tok.append(attn_tok_q)
            merged.append((part, swap(part, "narrow", 1)))
        for q in chunks:
            first[q], ffn_in_q, pre_q, part = feed_forward(
                layer, first[q], *merged[q], out_bias, ffn_norm_gain, ffn_norm_bias,
                up_weight, up_bias, down_weight, attn_tok[1:] + ffn_in,
            )
            ffn_in.append(ffn_in_q)
            pre_act.append(pre_q)
            if layer + 1 < LAYERS:
                ffn_parts[q] = (part, swap(part, "narrow", 1), down_bias)
            else:
                ffn_parts[q] = part
        afters = [ffn_in[1:], []]
        saved.append((second_now, normed, sorted_rows, attn, stats, attn_tok, list(first), ffn_in, pre_act))
    first_out = narrow_chunks(pos, first, seqs)
    sent = [
        lax.dynamic_slice_in_dim(part, (1 - narrow_index) * half, half, 1) for part in ffn_parts
    ]
    got = swap(jnp.concatenate(sent), "narrow", 1)
    second_out = narrow_chunks(pos, second, seqs, LAYERS - 1, [*ffn_parts, got, down_bias])
    summed, waiting = [], []
    done = []
    small_grads = [None] * LAYERS
    after = []
    for layer in reversed(range(LAYERS)):
        second_l, normed, sorted_rows, attn, stats, attn_tok, first_l, ffn_in, pre_act = saved[layer]
        branch, hidden, low, parts = [], [], [], []
        down_bias_grad, up_bias_grad = 0.0, 0.0
        for q in chunks:
            branch_q, hidden_q, low_q, down_bias_q, up_bias_q, part = feed_back(
                layer, grad_second[q], up_weight, down_weight, pre_act[q]
            )
            branch.append(branch_q)
            hidden.append(hidden_q)
            low.append(low_q)
            parts.append((part, swap(part, "narrow", 1)))
            down_bias_grad += down_bias_q
            up_bias_grad += up_bias_q
        pairs = waiting + [(ffn_in, low), (branch, hidden)]
        widths = [right[0].shape[1] for _, right in pairs]
        columns = sum(widths) + head_width
        if layer == 0:
            products = [weight_products(pairs, columns)]
        else:
            products = []
        out_low, units = [], []
        ffn_gain_grad, ffn_bias_grad, out_bias_grad = 0.0, 0.0, 0.0
        for q in chunks:
            *results, units_q = leave_ffn(
                seqs, layer, first_l[q], *parts[q], grad_first[q], ffn_norm_gain,
                gathered[layer], 2, head_width, [*units, *products] if q > 0 else (),
            )
            grad_first[q] = results[0]
            out_low.append(results[1])
            ffn_gain_grad += results[2]
            ffn_bias_grad += results[3]
            out_bias_grad += results[4]
            units.append(chip_exchange(units_q))
        if layer == 0:
            products = [
                weight_products([(out_low, attn_tok)], columns, columns - head_width, *products)
            ]
            summed += sum_rows(*products, widths + [head_width])
        sources = []
        for q in chunks:
            own = join_grads(q, attn, stats, units[q], products if q > 0 else ())
            sources += [own, swap(own, "wide", 1)]
        early_small = jnp.concatenate(
            [
                own_half(grad)
                for grad in (ffn_gain_grad, ffn_bias_grad, out_bias_grad, down_bias_grad)
            ]
            + [up_bias_grad.reshape(-1, half)]
        )
        own, sib = attention_backward(pos, sources, sorted_rows, tables, [early_small])
        units = add_cores(own, swap(sib, "wide", 1), done)
        grad_tok, attn_gain_grad, attn_bias_grad = [], 0.0, 0.0
        backs = [chip_exchange(units[q]) for q in chunks]
        after = []
        if layer > 0:
            pairs.append((out_low, attn_tok))
        merged = []
        for q in chunks:
            part, grad_tok_q = merge_units(seqs, backs[q], gathered[layer], 0, after + grad_tok)
            if layer > 0 and q == 0:
                products = weight_products(pairs, columns, after=[grad_tok_q])
                summed += sum_rows(products, widths + [head_width])
                after = [products]
            grad_tok.append(grad_tok_q)
            merged.append((part, swap(part, "narrow", 1)))
        waiting = [(normed, grad_tok)]
        stages = [None]
        if layer == 0:
            stages = reduce_rows(weight_products(waiting, unit_columns))
            summed.append(stages[-1])
        for q in chunks:
            grad_second[q], gain_q, shift_q = finish_attention(
                layer, second_l[q], *merged[q], grad_second[q], attn_norm_gain,
                stages[q + 1 : q + 2] if layer == 0 else (),
            )
            attn_gain_grad += gain_q
            attn_bias_grad += shift_q
        done = summed[-1:]
        late_small = jnp.concatenate([own_half(attn_gain_grad), own_half(attn_bias_grad)])
        small_grads[layer] = jnp.concatenate([late_small, early_small])
    first_grad = narrow_chunks(pos, grad_first, seqs)
    second_grad = narrow_chunks(pos, grad_second, seqs)

    small = sum_wide(jnp.stack(small_grads))
    other = swap(small[:, :4], "narrow", 1)
    paired = jnp.where(
        narrow_index == 0,
        jnp.concatenate([small[:, :4], other], axis=-1),
        jnp.concatenate([other, small[:, :4]], axis=-1),
    )
    order = [(4, 5, 6, 7), (0, 1, 2, 3)]
    weight_grads = [None] * LAYERS
    for layer in range(LAYERS):
        up_sum, down_sum, out_sum, unit_sum = [summed[at] for at in order[layer]]
        by_unit = unit_sum.reshape(weight_rows, heads, 2, HD)
        weight_grads[layer] = (
            by_unit[:, :, 0].reshape(weight_rows, head_width),
            by_unit[:, :, 1].reshape(weight_rows, head_width),
            out_sum,
            up_sum,
            down_sum,
        )

    def stacked(slot):
        return jnp.stack([weight_grads[layer][slot] for layer in range(LAYERS)])

    return (
        first_out,
        second_out,
        first_grad,
        second_grad,
        paired[:, 0],
        paired[:, 1],
        stacked(0),
        stacked(1),
        stacked(2),
        small[:, 4],
        paired[:, 2],
        paired[:, 3],
        stacked(3),
        small[:, 6:].reshape(LAYERS, hidden_width),
        stacked(4),
        small[:, 5],
    )


def solution(mesh):
    streams = P(None, "wide", "narrow")
    features = P(None, "narrow")
    hidden = P(None, None, "narrow")
    return jax.shard_map(
        shards,
        mesh=mesh,
        in_specs=(
            streams, streams, P(), P(), streams, streams, streams, features, P(), P(),
            hidden, features, hidden, features, P(None, None, "wide"), streams, streams,
        ),
        out_specs=(
            streams, streams, streams, streams, P(), P(), streams, streams, streams,
            features, P(), P(), streams, features, streams, features,
        ),
        check_vma=False,
    )
```

```python
import functools

import jax
import jax.numpy as jnp
from jax import lax
from jax.experimental import pallas as pl
from jax.experimental.pallas import tpu as pltpu
from jax.sharding import PartitionSpec as P

HD = 128
GROUP = 64
ROUNDS = 4
LAYERS = 2
BLOCK = 256
F32 = jnp.float32
BF16 = jnp.bfloat16
SCALE = HD ** (-0.5)
VMEM_LIMIT = 63 * 1024 * 1024
PAIRS = 8
SHARE = 0.01
CHUNKS = 2
FFN_STEPS = 2


def swap(value, axis, mask):
    count = lax.axis_size(axis)
    return lax.ppermute(value, axis, [(source, source ^ mask) for source in range(count)])


def dot(left, right, dims):
    return lax.dot_general(left, right, (dims, ((), ())), preferred_element_type=F32)


def mm(left, right):
    return dot(left, right, ((1,), (0,)))


def mm_t(left, right):
    return dot(left, right, ((1,), (1,)))


def t_mm(left, right):
    return dot(left, right, ((0,), (0,)))


def chip_exchange(units):
    count = lax.axis_size("wide")
    groups = [list(range(core, count, 2)) for core in range(2)]
    return lax.all_to_all(units, "wide", 0, 0, tiled=True, axis_index_groups=groups)


def split3(value):
    high = value.astype(BF16)
    rest = value - high.astype(F32)
    mid = rest.astype(BF16)
    low = (rest - mid.astype(F32)).astype(BF16)
    return high.astype(F32), mid.astype(F32), low.astype(F32)


def layer_norm(stream, gain, shift):
    centre = stream - jnp.mean(stream, axis=-1, keepdims=True)
    spread = jnp.mean(centre * centre, axis=-1, keepdims=True)
    return centre * lax.rsqrt(spread + 1e-05) * gain + shift


def layer_norm_back(stream, gain, grad):
    centre = stream - jnp.mean(stream, axis=-1, keepdims=True)
    inv = lax.rsqrt(jnp.mean(centre * centre, axis=-1, keepdims=True) + 1e-05)
    unit = centre * inv
    scaled = grad * gain
    back = inv * (
        scaled
        - jnp.mean(scaled, axis=-1, keepdims=True)
        - unit * jnp.mean(scaled * unit, axis=-1, keepdims=True)
    )
    return back, unit


def build_tables(tokens):
    rounds, seq = tokens.shape
    blocks = seq // BLOCK
    rank_rows = BLOCK // blocks
    tokens = tokens.reshape(rounds, blocks, BLOCK)
    run = tokens // BLOCK
    row = tokens % BLOCK
    onehot = (run[..., None] == jnp.arange(blocks, dtype=jnp.int32)).astype(BF16)
    before = (jnp.arange(BLOCK)[:, None] > jnp.arange(BLOCK)[None, :]).astype(BF16)
    counts = jnp.einsum("jl,rkla->rkja", before, onehot, preferred_element_type=F32)
    rank = jnp.sum(onehot.astype(F32) * counts, axis=-1).astype(jnp.int32)
    slot = run * rank_rows + rank
    iota = jnp.arange(BLOCK, dtype=jnp.int32)
    into = (slot[..., None] == iota).astype(BF16)
    into_t = (slot[..., None, :] == iota[:, None]).astype(BF16)
    wants = jnp.einsum("rknj,rkj->rkn", into_t, row.astype(BF16), preferred_element_type=F32)
    wants = wants.reshape(rounds, blocks, blocks, rank_rows)
    wants = jnp.transpose(wants, (0, 2, 1, 3)).reshape(rounds, blocks, BLOCK).astype(jnp.int32)
    out_of = (wants[..., None] == iota).astype(BF16)
    out_of_t = (wants[..., None, :] == iota[:, None]).astype(BF16)
    return jnp.transpose(out_of, (1, 0, 2, 3)), into, out_of_t, into_t


def token_copies(pos_ref, sources, tok, sems):
    core = pos_ref[0]
    chunks = len(sources) // 2
    slots, rows, _ = sources[0].shape
    copies = []
    for place, source in enumerate(sources):
        chunk, half = place // 2, place % 2
        for k in range(slots):
            device = 2 * k + (core ^ half)
            start = pl.multiple_of((device * chunks + chunk) * rows, rows)
            copies.append(
                pltpu.make_async_copy(
                    source.at[k], tok.at[pl.ds(start, rows)], sems.at[len(copies)]
                )
            )
    return copies


def table_copies(sources, targets, sems):
    return [
        pltpu.make_async_copy(source, target, sems.at[k])
        for k, (source, target) in enumerate(zip(sources, targets))
    ]


def store_run(pos_ref, buffer, run, value):
    core = pos_ref[0]
    _, chunks, _, rows, _ = buffer.shape
    for part in range(BLOCK // rows):
        device = run * (BLOCK // (rows * chunks)) + part // chunks
        buffer[(device & 1) ^ core, part % chunks, device >> 1] = value[
            part * rows : (part + 1) * rows
        ]


def send_halves(buffer, own_hbm, sib_hbm, sems):
    copies = [
        pltpu.make_async_copy(buffer.at[1], sib_hbm, sems.at[0]),
        pltpu.make_async_copy(buffer.at[0], own_hbm, sems.at[1]),
    ]
    for copy in copies:
        copy.start()
    for copy in copies:
        copy.wait()


def spread(first, count, width):
    row = lax.broadcasted_iota(jnp.int32, (HD, width), 0)
    return jnp.where((row >= first) & (row < first + count), 1.0, 0.0).astype(BF16)


def pack_stats(columns):
    lane = lax.broadcasted_iota(jnp.int32, columns[0].shape, 1)
    extra = jnp.zeros(columns[0].shape, F32)
    for place, column in enumerate(columns):
        extra = jnp.where(lane == place, column, extra)
    return extra


def permute_in(tok, out_of, mixed, blocks):
    rank = BLOCK // blocks
    for a in range(blocks):
        source = tok[a * BLOCK : (a + 1) * BLOCK, :]
        moved = mm(out_of[a].reshape(2 * BLOCK, BLOCK), source).astype(BF16)
        for r in range(2):
            mixed[r, :, a] = moved[r * BLOCK : (r + 1) * BLOCK].reshape(blocks, rank, 2 * HD)


def split_rows(tile):
    lane = lax.broadcasted_iota(jnp.int32, tile.shape, 1)
    zero = jnp.zeros_like(tile)
    return jnp.concatenate(
        [jnp.where(lane < GROUP, tile, zero), jnp.where(lane >= GROUP, tile, zero)], axis=0
    )


def split_lanes(tile):
    row = lax.broadcasted_iota(jnp.int32, tile.shape, 0)
    zero = jnp.zeros_like(tile)
    return jnp.concatenate(
        [jnp.where(row < GROUP, tile, zero), jnp.where(row >= GROUP, tile, zero)], axis=1
    )


def side_by_side(ref, base):
    return jnp.concatenate(
        [ref[base : base + 2 * GROUP, :], ref[base + GROUP : base + 3 * GROUP, :]], axis=1
    )


def one_above(ref, base):
    return jnp.concatenate(
        [ref[base : base + 2 * GROUP, :], ref[base + GROUP : base + 3 * GROUP, :]], axis=0
    )


def self_mask():
    row = lax.broadcasted_iota(jnp.int32, (2 * GROUP, 2 * GROUP), 0)
    lane = lax.broadcasted_iota(jnp.int32, (2 * GROUP, 2 * GROUP), 1)
    return row == lane % GROUP + GROUP


def unit_keys(query):
    return query * lax.rsqrt(jnp.mean(query * query, axis=-1, keepdims=True) + 1e-06)


def forward_kernel(chunks, extras, pos_ref, *refs):
    sources, refs = refs[: 2 * chunks], refs[2 * chunks + extras :]
    (
        out_of_hbm, into_hbm, out_of_t_hbm, into_t_hbm, sorted_hbm, own_hbm, sib_hbm,
        tok, mixed, keys, vals, placed, buffer, out_of, into, out_of_t, into_t,
        tok_sems, table_sems, out_sems, send_sems,
    ) = refs
    seq = tok.shape[0]
    blocks = seq // BLOCK
    rank = BLOCK // blocks
    loads = token_copies(pos_ref, sources, tok, tok_sems)
    tables = table_copies(
        (out_of_hbm, into_hbm, into_t_hbm, out_of_t_hbm), (out_of, into, into_t, out_of_t), table_sems
    )
    for copy in loads:
        copy.start()
    for copy in tables:
        copy.start()
    for copy in loads:
        copy.wait()
    tables[0].wait()
    permute_in(tok, out_of, mixed, blocks)
    tables[1].wait()
    outs = []
    for r in range(2):
        for k in range(blocks):
            base = k * BLOCK
            rows_sorted = mm(into[r, k], mixed[r, k].reshape(BLOCK, 2 * HD))
            placed[r, base : base + BLOCK, :] = rows_sorted.astype(BF16)
            where = slice(base + GROUP, base + GROUP + BLOCK)
            keys[r, where, :] = unit_keys(rows_sorted[:, :HD]).astype(BF16)
            vals[r, where, :] = rows_sorted[:, HD:].astype(BF16)
        keys[r, 0:GROUP, :] = keys[r, seq : seq + GROUP, :]
        vals[r, 0:GROUP, :] = vals[r, seq : seq + GROUP, :]
        outs.append(pltpu.make_async_copy(placed.at[r], sorted_hbm.at[r], out_sems.at[r]))
        outs[-1].start()
    tables[2].wait()
    own = jnp.concatenate([self_mask()] * PAIRS, axis=1)
    wide = PAIRS * 2 * GROUP
    for r in range(2):
        for first in range(0, seq, wide):
            bases = [first + p * 2 * GROUP for p in range(PAIRS)]
            flipped = [placed[r, base : base + 2 * GROUP, 0:HD].T for base in bases]
            raw = jnp.concatenate(
                [
                    mm(side_by_side(keys.at[r], base), split_rows(tile))
                    for base, tile in zip(bases, flipped)
                ],
                axis=1,
            )
            scores = jnp.where(own, -1000000000.0, raw * SCALE)
            top = jnp.max(scores, axis=0, keepdims=True)
            weight = jnp.exp(scores - top)
            total = jnp.sum(weight, axis=0, keepdims=True)
            probs = (weight * (1.0 / total)).astype(BF16)
            row = lax.broadcasted_iota(jnp.int32, (8, wide), 0)
            stats = jnp.zeros((8, wide), F32)
            for place, part in enumerate(split3(top + jnp.log(total))):
                stats = jnp.where(row == place, part, stats)
            stats = jnp.concatenate([stats, jnp.zeros((HD - 8, wide), F32)], axis=0)
            lanes = [slice(p * 2 * GROUP, (p + 1) * 2 * GROUP) for p in range(PAIRS)]
            turned = [probs[:, lane].T for lane in lanes]
            extra = [stats[:, lane].T.astype(BF16) for lane in lanes]
            result = [
                mm(split_lanes(tile), one_above(vals.at[r], base)).astype(BF16)
                for tile, base in zip(turned, bases)
            ]
            packed = jnp.concatenate(
                [jnp.concatenate(pair, axis=1) for pair in zip(result, extra)], axis=0
            )
            for part in range(wide // BLOCK):
                k = first // BLOCK + part
                back = mm(into_t[r, k], packed[part * BLOCK : (part + 1) * BLOCK]).astype(BF16)
                mixed[r, k] = back.reshape(blocks, rank, 2 * HD)
    tables[3].wait()
    zero = jnp.zeros((HD, HD), BF16)
    ones = spread(0, 3, HD)
    ones = jnp.concatenate(
        [jnp.concatenate([ones, zero], axis=1), jnp.concatenate([zero, ones], axis=1)], axis=0
    )
    for a in range(blocks):
        moved = [mm(out_of_t[r, a], mixed[r, :, a].reshape(BLOCK, 2 * HD)) for r in range(2)]
        lse = mm(jnp.concatenate([m[:, HD:] for m in moved], axis=1).astype(BF16), ones)
        lse_a, lse_b = lse[:, :HD], lse[:, HD:]
        top = jnp.maximum(lse_a, lse_b)
        weight_a, weight_b = jnp.exp(lse_a - top), jnp.exp(lse_b - top)
        total = weight_a + weight_b
        value = (moved[0][:, :HD] * weight_a + moved[1][:, :HD] * weight_b) * (1.0 / total)
        extra = pack_stats(split3(top + jnp.log(total)))
        store_run(pos_ref, buffer, a, jnp.concatenate([value, extra], axis=1).astype(BF16))
    send_halves(buffer, own_hbm, sib_hbm, send_sems)
    for copy in outs:
        copy.wait()


def backward_kernel(chunks, extras, pos_ref, *refs):
    sources, refs = refs[: 2 * chunks], refs[2 * chunks + extras :]
    (
        sorted_hbm, out_of_hbm, into_hbm, out_of_t_hbm, into_t_hbm, own_hbm, sib_hbm,
        tok, mixed, keys, vals, placed, grads, query_use, key_grad, val_grad, buffer,
        out_of, into, out_of_t, into_t, tok_sems, table_sems, in_sems, send_sems,
    ) = refs
    seq = tok.shape[0]
    blocks = seq // BLOCK
    rank = BLOCK // blocks
    loads = token_copies(pos_ref, sources, tok, tok_sems)
    tables = table_copies(
        (out_of_hbm, into_hbm, into_t_hbm, out_of_t_hbm), (out_of, into, into_t, out_of_t), table_sems
    )
    sorted_in = pltpu.make_async_copy(sorted_hbm, placed, in_sems.at[0])
    for copy in loads:
        copy.start()
    tables[0].start()
    sorted_in.start()
    for copy in tables[1:]:
        copy.start()
    for copy in loads:
        copy.wait()
    tables[0].wait()
    permute_in(tok, out_of, mixed, blocks)
    sorted_in.wait()
    tables[1].wait()
    for r in range(2):
        for k in range(blocks):
            here = slice(k * BLOCK, (k + 1) * BLOCK)
            where = slice(k * BLOCK + GROUP, (k + 1) * BLOCK + GROUP)
            grads[r, here, :] = mm(into[r, k], mixed[r, k].reshape(BLOCK, 2 * HD)).astype(BF16)
            keys[r, where, :] = unit_keys(placed[r, here, 0:HD].astype(F32)).astype(BF16)
            vals[r, where, :] = placed[r, here, HD:]
        keys[r, 0:GROUP, :] = keys[r, seq : seq + GROUP, :]
        vals[r, 0:GROUP, :] = vals[r, seq : seq + GROUP, :]
        key_grad[r, 0:GROUP, :] = jnp.zeros((GROUP, HD), F32)
        val_grad[r, 0:GROUP, :] = jnp.zeros((GROUP, HD), F32)
    own = jnp.concatenate([self_mask()] * PAIRS, axis=1)
    wide = PAIRS * 2 * GROUP
    lanes = [slice(p * 2 * GROUP, (p + 1) * 2 * GROUP) for p in range(PAIRS)]
    for r in range(2):
        for first in range(0, seq, wide):
            bases = [first + p * 2 * GROUP for p in range(PAIRS)]
            query = [placed[r, base : base + 2 * GROUP, 0:HD] for base in bases]
            grad = [grads[r, base : base + 2 * GROUP, 0:HD] for base in bases]
            stats = jnp.concatenate(
                [
                    grads[r, base : base + 2 * GROUP, HD:].astype(F32).T[0:8] for base in bases
                ],
                axis=1,
            )
            delta = stats[0:1] + stats[1:2] + stats[2:3]
            lse = stats[3:4] + stats[4:5] + stats[5:6]
            query_t = [split_rows(tile.T) for tile in query]
            grad_t = [split_rows(tile.T) for tile in grad]
            raw = jnp.concatenate(
                [mm(side_by_side(keys.at[r], base), tile) for base, tile in zip(bases, query_t)],
                axis=1,
            )
            prob_grad = jnp.concatenate(
                [mm(side_by_side(vals.at[r], base), tile) for base, tile in zip(bases, grad_t)],
                axis=1,
            )
            probs = jnp.exp(jnp.where(own, -1000000000.0, raw * SCALE) - lse)
            score_grad = (probs * (prob_grad - delta)).astype(BF16)
            probs = probs.astype(BF16)
            turned = [score_grad[:, lane].T for lane in lanes]
            for tile, base in zip(turned, bases):
                query_use[r, base : base + 2 * GROUP, :] = (
                    mm(split_lanes(tile), one_above(keys.at[r], base)) * SCALE
                )
            key_parts = [
                mm(split_rows(score_grad[:, lane]), tile) * SCALE for lane, tile in zip(lanes, query)
            ]
            val_parts = [mm(split_rows(probs[:, lane]), tile) for lane, tile in zip(lanes, grad)]
            for target, parts in ((key_grad, key_parts), (val_grad, val_parts)):
                target[r, first : first + GROUP, :] += parts[0][:GROUP]
                for p, (part, base) in enumerate(zip(parts, bases)):
                    target[r, base + GROUP : base + 2 * GROUP, :] = (
                        part[GROUP : 2 * GROUP] + part[2 * GROUP : 3 * GROUP]
                    )
                    last = part[3 * GROUP :]
                    if p + 1 < PAIRS:
                        last = last + parts[p + 1][:GROUP]
                    target[r, base + 2 * GROUP : base + 3 * GROUP, :] = last
        key_grad[r, seq : seq + GROUP, :] += key_grad[r, 0:GROUP, :]
        val_grad[r, seq : seq + GROUP, :] += val_grad[r, 0:GROUP, :]
    tables[2].wait()
    for r in range(2):
        for k in range(blocks):
            here = slice(k * BLOCK, (k + 1) * BLOCK)
            where = slice(k * BLOCK + GROUP, (k + 1) * BLOCK + GROUP)
            query = placed[r, here, 0:HD].astype(F32)
            inv = lax.rsqrt(jnp.mean(query * query, axis=-1, keepdims=True) + 1e-06)
            grad = key_grad[r, where, :]
            inner = jnp.mean(grad * query, axis=-1, keepdims=True)
            total = query_use[r, here, :] + inv * (grad - query * (inner * inv * inv))
            packed = jnp.concatenate([total, val_grad[r, where, :]], axis=1).astype(BF16)
            back = mm(into_t[r, k], packed).astype(BF16)
            mixed[r, k] = back.reshape(blocks, rank, 2 * HD)
    tables[3].wait()
    for a in range(blocks):
        total = mm(out_of_t[0, a], mixed[0, :, a].reshape(BLOCK, 2 * HD)) + mm(
            out_of_t[1, a], mixed[1, :, a].reshape(BLOCK, 2 * HD)
        )
        store_run(pos_ref, buffer, a, total.astype(BF16))
    send_halves(buffer, own_hbm, sib_hbm, send_sems)


def params():
    return pltpu.CompilerParams(vmem_limit_bytes=VMEM_LIMIT)


def cost(flops, moved):
    return pl.CostEstimate(flops=int(flops * SHARE), bytes_accessed=int(moved * SHARE), transcendentals=0)


IN_SMEM = pl.BlockSpec(memory_space=pltpu.SMEM)
IN_VMEM = pl.BlockSpec(memory_space=pltpu.VMEM)
ANYWHERE = pl.BlockSpec(memory_space=pl.ANY)


def bf16_out(*shape):
    return jax.ShapeDtypeStruct(shape, BF16)


def f32_out(*shape):
    return jax.ShapeDtypeStruct(shape, F32)


def table_scratch(blocks):
    return [
        pltpu.VMEM((blocks, 2, BLOCK, BLOCK), BF16),
        pltpu.VMEM((2, blocks, BLOCK, BLOCK), BF16),
        pltpu.VMEM((2, blocks, BLOCK, BLOCK), BF16),
        pltpu.VMEM((2, blocks, BLOCK, BLOCK), BF16),
    ]


def attention_forward(pos, sources, tables, after):
    chunks = len(sources) // 2
    slots, rows, width = sources[0].shape
    seq = 2 * slots * rows * chunks
    blocks = seq // BLOCK
    half = bf16_out(chunks, slots, rows, width)
    return pl.pallas_call(
        functools.partial(forward_kernel, chunks, len(after)),
        out_shape=(bf16_out(2, seq, width), half, half),
        in_specs=[IN_SMEM] + [ANYWHERE] * (2 * chunks + len(after) + 4),
        out_specs=(ANYWHERE, ANYWHERE, ANYWHERE),
        scratch_shapes=[
            pltpu.VMEM((seq, width), BF16),
            pltpu.VMEM((2, blocks, blocks, BLOCK // blocks, width), BF16),
            pltpu.VMEM((2, seq + GROUP, HD), BF16),
            pltpu.VMEM((2, seq + GROUP, HD), BF16),
            pltpu.VMEM((2, seq, width), BF16),
            pltpu.VMEM((2, chunks, slots, rows, width), BF16),
            *table_scratch(blocks),
            pltpu.SemaphoreType.DMA((2 * slots * chunks,)),
            pltpu.SemaphoreType.DMA((4,)),
            pltpu.SemaphoreType.DMA((2,)),
            pltpu.SemaphoreType.DMA((2,)),
        ],
        compiler_params=params(),
        cost_estimate=cost(16e9, 24e6),
        name="attend_forward",
    )(pos, *sources, *after, *tables)


def attention_backward(pos, sources, sorted_rows, tables, after):
    chunks = len(sources) // 2
    slots, rows, width = sources[0].shape
    seq = 2 * slots * rows * chunks
    blocks = seq // BLOCK
    half = bf16_out(chunks, slots, rows, width)
    return pl.pallas_call(
        functools.partial(backward_kernel, chunks, len(after)),
        out_shape=(half, half),
        in_specs=[IN_SMEM] + [ANYWHERE] * (2 * chunks + len(after) + 5),
        out_specs=(ANYWHERE, ANYWHERE),
        scratch_shapes=[
            pltpu.VMEM((seq, width), BF16),
            pltpu.VMEM((2, blocks, blocks, BLOCK // blocks, width), BF16),
            pltpu.VMEM((2, seq + GROUP, HD), BF16),
            pltpu.VMEM((2, seq + GROUP, HD), BF16),
            pltpu.VMEM((2, seq, width), BF16),
            pltpu.VMEM((2, seq, width), BF16),
            pltpu.VMEM((2, seq, HD), F32),
            pltpu.VMEM((2, seq + GROUP, HD), F32),
            pltpu.VMEM((2, seq + GROUP, HD), F32),
            pltpu.VMEM((2, chunks, slots, rows, width), BF16),
            *table_scratch(blocks),
            pltpu.SemaphoreType.DMA((2 * slots * chunks,)),
            pltpu.SemaphoreType.DMA((4,)),
            pltpu.SemaphoreType.DMA((1,)),
            pltpu.SemaphoreType.DMA((2,)),
        ],
        compiler_params=params(),
        cost_estimate=cost(18e9, 26e6),
        name="attend_backward",
    )(pos, *sources, *after, sorted_rows, *tables)


def unit_slices(seqs, heads, rows, width):
    return [
        (slice(seq * rows, (seq + 1) * rows), slice(head * width, (head + 1) * width))
        for seq in range(seqs)
        for head in range(heads)
    ]


def column_block(rows, width, place):
    return pl.BlockSpec((rows, width), lambda i: (0, place))


def whole_block(array):
    return pl.BlockSpec(array.shape, lambda i: (0,) * len(array.shape))


def pack_kernel(count, *refs):
    out_ref = refs[-1]
    start = 0
    for ref in refs[:count]:
        out_ref[:, start : start + ref.shape[1]] = ref[...]
        start += ref.shape[1]


def pack_columns(pieces, after):
    rows, columns = pieces[0].shape[0], sum(piece.shape[1] for piece in pieces)
    return pl.pallas_call(
        functools.partial(pack_kernel, len(pieces)),
        out_shape=bf16_out(rows, columns),
        in_specs=[IN_VMEM] * len(pieces) + [ANYWHERE] * len(after),
        out_specs=IN_VMEM,
        compiler_params=params(),
        name="pack_columns",
    )(*pieces, *after)


def lower_kernel(count, *refs):
    for source, target in zip(refs[:count], refs[-count:]):
        target[...] = source[...].astype(BF16)


def lower_arrays(arrays, after):
    return pl.pallas_call(
        functools.partial(lower_kernel, len(arrays)),
        out_shape=[bf16_out(*array.shape) for array in arrays],
        in_specs=[IN_VMEM] * len(arrays) + [ANYWHERE] * len(after),
        out_specs=[IN_VMEM] * len(arrays),
        compiler_params=params(),
        name="lower_arrays",
    )(*arrays, *after)


def widen_kernel(pos_ref, mine_ref, other_ref, *out_refs):
    seqs, rows, half = mine_ref.shape
    count = rows // len(out_refs)
    mine_at = pl.ds(pl.multiple_of(pos_ref[1] * half, half), half)
    other_at = pl.ds(pl.multiple_of((1 - pos_ref[1]) * half, half), half)
    for q, out_ref in enumerate(out_refs):
        for seq in range(seqs):
            at = slice(seq * count, (seq + 1) * count)
            source = slice(q * count, (q + 1) * count)
            out_ref[at, mine_at] = mine_ref[seq, source]
            out_ref[at, other_at] = other_ref[seq, source].astype(F32)


def widen_chunks(pos, mine, other):
    seqs, rows, half = mine.shape
    out = f32_out(seqs * rows // CHUNKS, 2 * half)
    return list(
        pl.pallas_call(
            widen_kernel,
            out_shape=[out] * CHUNKS,
            in_specs=[IN_SMEM, IN_VMEM, IN_VMEM],
            out_specs=[IN_VMEM] * CHUNKS,
            compiler_params=params(),
            cost_estimate=cost(1e6, 4e6),
            name="widen_chunks",
        )(pos, mine, other)
    )


def narrow_kernel(layer, pos_ref, *refs):
    out_ref = refs[-1]
    seqs, rows, half = out_ref.shape
    count = rows // CHUNKS
    lanes = pl.ds(pl.multiple_of(pos_ref[1] * half, half), half)
    for q in range(CHUNKS):
        for seq in range(seqs):
            at = slice(seq * count, (seq + 1) * count)
            value = refs[q][at, lanes]
            if layer is not None:
                own, other, bias = refs[CHUNKS + q], refs[2 * CHUNKS], refs[2 * CHUNKS + 1]
                got = other[q * seqs * count + seq * count : q * seqs * count + (seq + 1) * count]
                value = value + (own[at, lanes].astype(F32) + got.astype(F32))
                value = value + bias[layer : layer + 1, lanes]
            out_ref[seq, q * count : (q + 1) * count] = value


def narrow_chunks(pos, chunks, seqs, layer=None, parts=(), after=()):
    toks, width = chunks[0].shape
    return pl.pallas_call(
        functools.partial(narrow_kernel, layer),
        out_shape=f32_out(seqs, toks * CHUNKS // seqs, width // 2),
        in_specs=[IN_SMEM]
        + [IN_VMEM] * (CHUNKS + len(parts))
        + [ANYWHERE] * len(after),
        out_specs=IN_VMEM,
        compiler_params=params(),
        cost_estimate=cost(1e6, 4e6),
        name="narrow_chunks",
    )(pos, *chunks, *parts, *after)


def enter_kernel(
    seqs, layer, parts, after, stream_ref, gain_ref, shift_ref, weight_ref, *refs
):
    stream = stream_ref[...]
    if parts:
        own_ref, other_ref, bias_ref, *refs = refs
        stream = stream + (own_ref[...].astype(F32) + other_ref[...].astype(F32))
        stream = stream + bias_ref[layer - 1 : layer]
    refs = refs[after:]
    if parts:
        refs[0][...] = stream
    normed_ref, out_ref = refs[-2:]
    row = slice(layer, layer + 1)
    normed = layer_norm(stream, gain_ref[row], shift_ref[row]).astype(BF16)
    normed_ref[...] = normed
    flat = mm(normed, weight_ref[...]).astype(BF16)
    slots, rows, width = out_ref.shape
    for k, at in enumerate(unit_slices(seqs, slots // seqs, rows, width)):
        out_ref[k] = flat[at]


def enter_attention(seqs, layer, stream, gain, shift, weight, place, columns, parts=(), after=()):
    toks, width = stream.shape
    slots = seqs * columns // (2 * HD)
    shapes = [bf16_out(toks, width), bf16_out(slots, toks // seqs, 2 * HD)]
    if parts:
        shapes = [f32_out(toks, width)] + shapes
    results = pl.pallas_call(
        functools.partial(enter_kernel, seqs, layer, len(parts) > 0, len(after)),
        grid=(1,),
        out_shape=shapes,
        in_specs=[whole_block(stream), whole_block(gain), whole_block(shift)]
        + [column_block(width, columns, place)]
        + [whole_block(part) for part in parts]
        + [ANYWHERE] * len(after),
        out_specs=[whole_block(shape) for shape in shapes],
        compiler_params=params(),
        cost_estimate=cost(2 * toks * width * columns, 5e6),
        name="enter_attention",
    )(stream, gain, shift, weight, *parts, *after)
    return results if parts else (stream, *results)


def merge_kernel(seqs, weight_ref, in_ref, *refs):
    part_ref, tok_ref = refs[-2:]
    slots, rows, width = in_ref.shape
    for k, at in enumerate(unit_slices(seqs, slots // seqs, rows, width)):
        tok_ref[at] = in_ref[k]
    part_ref[...] = mm_t(tok_ref[...], weight_ref[...]).astype(BF16)


def merge_units(seqs, units, weight, place, after=()):
    slots, rows, width = units.shape
    toks, columns = seqs * rows, slots // seqs * width
    shapes = (bf16_out(toks, weight.shape[0]), bf16_out(toks, columns))
    return pl.pallas_call(
        functools.partial(merge_kernel, seqs),
        grid=(1,),
        out_shape=shapes,
        in_specs=[column_block(weight.shape[0], columns, place), whole_block(units)]
        + [ANYWHERE] * len(after),
        out_specs=[whole_block(shape) for shape in shapes],
        compiler_params=params(),
        cost_estimate=cost(2 * toks * columns * weight.shape[0], 3e6),
        name="merge_units",
    )(weight, units, *after)


def both_stats(own, got):
    zero = jnp.zeros((HD, HD), BF16)
    ones = spread(0, 3, HD)
    ones = jnp.concatenate(
        [jnp.concatenate([ones, zero], axis=1), jnp.concatenate([zero, ones], axis=1)], axis=0
    )
    lse = mm(jnp.concatenate([own, got], axis=1), ones)
    return lse[:, :HD], lse[:, HD:]


def combine_kernel(after, own_ref, got_ref, *refs):
    attn_ref, stats_ref, *out_refs = refs[after:]
    chunks, slots, rows, _ = own_ref.shape
    for q in range(chunks):
        for k in range(slots):
            lse_a, lse_b = both_stats(own_ref[q, k, :, HD:], got_ref[q, k, :, HD:])
            top = jnp.maximum(lse_a, lse_b)
            weight_a, weight_b = jnp.exp(lse_a - top), jnp.exp(lse_b - top)
            total = weight_a + weight_b
            own = own_ref[q, k, :, :HD].astype(F32)
            got = got_ref[q, k, :, :HD].astype(F32)
            value = (own * weight_a + got * weight_b) * (1.0 / total)
            attn_ref[q, k] = value
            zero = jnp.zeros_like(total)
            stats_ref[q, k] = pack_stats(
                (zero, zero, zero) + split3(top + jnp.log(total))
            ).astype(BF16)
            out_refs[q][k] = value.astype(BF16)


def combine_cores(own, got, after=()):
    chunks, slots, rows, _ = own.shape
    results = pl.pallas_call(
        functools.partial(combine_kernel, len(after)),
        out_shape=[f32_out(chunks, slots, rows, HD), bf16_out(chunks, slots, rows, HD)]
        + [bf16_out(slots, rows, HD)] * chunks,
        in_specs=[IN_VMEM] * 2 + [ANYWHERE] * len(after),
        out_specs=[IN_VMEM] * (2 + chunks),
        compiler_params=params(),
        cost_estimate=cost(1e8, 5e6),
        name="combine_cores",
    )(own, got, *after)
    return results[0], results[1], results[2:]


def join_kernel(attn_ref, stats_ref, in_ref, *refs):
    out_ref = refs[-1]
    for k in range(in_ref.shape[0]):
        grad = in_ref[k]
        delta = jnp.sum(attn_ref[0, k] * grad.astype(F32), axis=-1, keepdims=True)
        delta = jnp.broadcast_to(delta, grad.shape)
        extra = pack_stats(split3(delta)) + stats_ref[0, k].astype(F32)
        out_ref[k] = jnp.concatenate([grad, extra.astype(BF16)], axis=1)


def join_grads(chunk, attn, stats, units, after=()):
    slots, rows, _ = units.shape
    spec = pl.BlockSpec((1, slots, rows, HD), lambda i: (chunk, 0, 0, 0))
    return pl.pallas_call(
        join_kernel,
        grid=(1,),
        out_shape=bf16_out(slots, rows, 2 * HD),
        in_specs=[spec, spec, pl.BlockSpec((slots, rows, HD), lambda i: (0, 0, 0))]
        + [ANYWHERE] * len(after),
        out_specs=pl.BlockSpec((slots, rows, 2 * HD), lambda i: (0, 0, 0)),
        compiler_params=params(),
        cost_estimate=cost(1e7, 2e6),
        name="join_grads",
    )(attn, stats, units, *after)


def add_kernel(after, own_ref, got_ref, *refs):
    for q, out_ref in enumerate(refs[after:]):
        total = own_ref[q].astype(F32) + got_ref[q].astype(F32)
        out_ref[...] = total.astype(BF16)


def add_cores(own, got, after=()):
    chunks, slots, rows, width = own.shape
    return pl.pallas_call(
        functools.partial(add_kernel, len(after)),
        out_shape=[bf16_out(slots, rows, width)] * chunks,
        in_specs=[IN_VMEM] * 2 + [ANYWHERE] * len(after),
        out_specs=[IN_VMEM] * chunks,
        compiler_params=params(),
        cost_estimate=cost(1e6, 3e6),
        name="add_cores",
    )(own, got, *after)


def ffn_kernel(
    layer, stream_ref, own_ref, other_ref, bias_ref, gain_ref, shift_ref, up_ref, up_bias_ref,
    down_ref, *refs,
):
    new_ref, normed_ref, pre_ref, part_ref, acc = refs[-5:]
    step = pl.program_id(0)
    row = slice(layer, layer + 1)

    @pl.when(step == 0)
    def _():
        stream = stream_ref[...] + (own_ref[...].astype(F32) + other_ref[...].astype(F32))
        stream = stream + bias_ref[row]
        new_ref[...] = stream
        normed_ref[...] = layer_norm(stream, gain_ref[row], shift_ref[row]).astype(BF16)

    pre = mm(normed_ref[...], up_ref[0]) + up_bias_ref[row]
    pre_ref[...] = pre
    hidden = jax.nn.gelu(pre, approximate=True).astype(BF16)
    part = mm_t(hidden, down_ref[0])

    @pl.when(step == 0)
    def _():
        acc[...] = part

    @pl.when(step > 0)
    def _():
        acc[...] += part

    @pl.when(step == pl.num_programs(0) - 1)
    def _():
        part_ref[...] = acc[...].astype(BF16)


def feed_forward(layer, stream, own, other, bias, gain, shift, up, up_bias, down, after=()):
    toks, width = stream.shape
    hidden = up.shape[2]
    step = hidden // FFN_STEPS
    full = pl.BlockSpec((toks, width), lambda i: (0, 0))
    slab = pl.BlockSpec((1, width, step), lambda i: (layer, 0, i))
    return pl.pallas_call(
        functools.partial(ffn_kernel, layer),
        grid=(FFN_STEPS,),
        out_shape=(
            f32_out(toks, width), bf16_out(toks, width), f32_out(toks, hidden), bf16_out(toks, width),
        ),
        in_specs=[
            full, full, full, whole_block(bias), whole_block(gain), whole_block(shift), slab,
            pl.BlockSpec((LAYERS, step), lambda i: (0, i)), slab,
        ]
        + [ANYWHERE] * len(after),
        out_specs=(full, full, pl.BlockSpec((toks, step), lambda i: (0, i)), full),
        scratch_shapes=[pltpu.VMEM((toks, width), F32)],
        compiler_params=params(),
        cost_estimate=cost(4 * toks * width * hidden, 14e6),
        name="feed_forward",
    )(stream, own, other, bias, gain, shift, up, up_bias, down, *after)


def ffn_back_kernel(norm, *refs):
    if norm is None:
        grad_ref, up_ref, down_ref, pre_ref, *refs = refs
    else:
        stream_ref, own_ref, other_ref, grad_ref, gain_ref, up_ref, down_ref, pre_ref, *refs = refs
        new_ref, gain_out, shift_out, *refs = refs
    branch_ref, hidden_ref, low_ref, down_bias_ref, up_bias_ref, part_ref, acc = refs
    step = pl.program_id(0)

    @pl.when(step == 0)
    def _():
        if norm is None:
            grad = grad_ref[...]
        else:
            grad = norm_back(
                norm, stream_ref, own_ref, other_ref, grad_ref, gain_ref, gain_out, shift_out
            )
            new_ref[...] = grad
        branch_ref[...] = grad.astype(BF16)
        down_bias_ref[...] = jnp.sum(grad, axis=0, keepdims=True)

    hidden_grad = mm(branch_ref[...], down_ref[0])
    pre = pre_ref[...]
    root = 0.7978845608028654
    square = pre * pre
    bend = jnp.tanh(root * (pre + 0.044715 * (square * pre)))
    half = 0.5 * (1.0 + bend)
    hidden_ref[...] = (pre * half).astype(BF16)
    slope = half + 0.5 * pre * (1.0 - bend * bend) * (root * (1.0 + 3 * 0.044715 * square))
    pre_grad = hidden_grad * slope
    up_bias_ref[...] = jnp.sum(pre_grad, axis=0, keepdims=True)
    low = pre_grad.astype(BF16)
    low_ref[...] = low
    part = mm_t(low, up_ref[0])

    @pl.when(step == 0)
    def _():
        acc[...] = part

    @pl.when(step > 0)
    def _():
        acc[...] += part

    @pl.when(step == pl.num_programs(0) - 1)
    def _():
        part_ref[...] = acc[...].astype(BF16)


def feed_back(layer, grad, up, down, pre, before=None):
    toks, width = grad.shape
    hidden = down.shape[2]
    step = hidden // FFN_STEPS
    full = pl.BlockSpec((toks, width), lambda i: (0, 0))
    line = pl.BlockSpec((1, width), lambda i: (0, 0))
    slab = pl.BlockSpec((1, width, step), lambda i: (layer, 0, i))
    tall = pl.BlockSpec((toks, step), lambda i: (0, i))
    shapes = [
        bf16_out(toks, width), bf16_out(toks, hidden), bf16_out(toks, hidden),
        f32_out(1, width), f32_out(1, hidden), bf16_out(toks, width),
    ]
    out_specs = [full, tall, tall, line, pl.BlockSpec((1, step), lambda i: (0, i)), full]
    operands, in_specs = [grad], [full]
    if before is not None:
        norm, stream, own, other, gain = before
        operands = [stream, own, other, grad, gain]
        in_specs = [full] * 4 + [whole_block(gain)]
        shapes = [f32_out(toks, width), f32_out(1, width), f32_out(1, width)] + shapes
        out_specs = [full, line, line] + out_specs
    return pl.pallas_call(
        functools.partial(ffn_back_kernel, None if before is None else norm),
        grid=(FFN_STEPS,),
        out_shape=shapes,
        in_specs=in_specs + [slab, slab, tall],
        out_specs=out_specs,
        scratch_shapes=[pltpu.VMEM((toks, width), F32)],
        compiler_params=params(),
        cost_estimate=cost(4 * toks * width * hidden, 15e6),
        name="feed_back",
    )(*operands, up, down, pre)


def products_kernel(counts, *refs):
    out_ref, turned = refs[-2:]
    step = pl.program_id(0)
    start = 0
    for place, count in enumerate(counts):
        lefts = refs[2 * CHUNKS * place : 2 * CHUNKS * place + CHUNKS]
        rights = refs[2 * CHUNKS * place + CHUNKS : 2 * CHUNKS * (place + 1)]

        @pl.when(step == start)
        def _(lefts=lefts):
            for q, left in enumerate(lefts):
                toks = left.shape[0]
                turned[:, q * toks : (q + 1) * toks] = left[...].T

        @pl.when((step >= start) & (step < start + count))
        def _(rights=rights):
            right = jnp.concatenate([right[...] for right in rights], axis=0)
            out_ref[...] = mm(turned[...], right).astype(BF16)

        start += count


def weight_products(pairs, columns, at=0, target=None, after=()):
    block = min(right[0].shape[1] for _, right in pairs)
    block = min(block, 512)
    counts = [right[0].shape[1] // block for _, right in pairs]
    toks, rows = pairs[0][0][0].shape
    specs, operands, start = [], [], 0
    for (left, right), count in zip(pairs, counts):
        specs += [pl.BlockSpec((toks, rows), lambda i: (0, 0))] * CHUNKS
        specs += [
            pl.BlockSpec(
                (toks, block),
                lambda i, start=start, count=count: (0, jnp.clip(i - start, 0, count - 1)),
            )
        ] * CHUNKS
        operands += [*left, *right]
        start += count
    more = [*after] if target is None else [target, *after]
    return pl.pallas_call(
        functools.partial(products_kernel, counts),
        grid=(start,),
        out_shape=bf16_out(rows, columns),
        in_specs=specs + [ANYWHERE] * len(more),
        out_specs=pl.BlockSpec((rows, block), lambda i: (0, i + at // block)),
        scratch_shapes=[pltpu.VMEM((rows, CHUNKS * toks), BF16)],
        input_output_aliases={} if target is None else {len(operands): 0},
        compiler_params=params(),
        cost_estimate=cost(2 * rows * CHUNKS * toks * start * block, 20e6),
        name="weight_products",
    )(*operands, *more)


def norm_back(
    layer, stream_ref, own_ref, other_ref, grad_ref, gain_ref, gain_out, shift_out
):
    grad = own_ref[...].astype(F32) + other_ref[...].astype(F32)
    back, unit = layer_norm_back(stream_ref[...], gain_ref[layer : layer + 1], grad)
    gain_out[...] = jnp.sum(grad * unit, axis=0, keepdims=True)
    shift_out[...] = jnp.sum(grad, axis=0, keepdims=True)
    return grad_ref[...] + back


def leave_kernel(
    seqs, layer, after, stream_ref, own_ref, other_ref, grad_ref, gain_ref, weight_ref, *refs
):
    new_ref, low_ref, gain_out, shift_out, bias_out, out_ref = refs[after:]
    grad = norm_back(
        layer, stream_ref, own_ref, other_ref, grad_ref, gain_ref, gain_out, shift_out
    )
    new_ref[...] = grad
    bias_out[...] = jnp.sum(grad, axis=0, keepdims=True)
    low = grad.astype(BF16)
    low_ref[...] = low
    flat = mm(low, weight_ref[...]).astype(BF16)
    slots, rows, width = out_ref.shape
    for k, at in enumerate(unit_slices(seqs, slots // seqs, rows, width)):
        out_ref[k] = flat[at]


def leave_ffn(
    seqs, layer, stream, own, other, grad, gain, weight, place, columns, after=()
):
    toks, width = stream.shape
    shapes = [f32_out(toks, width), bf16_out(toks, width)] + [f32_out(1, width)] * 3
    shapes.append(bf16_out(seqs * columns // HD, toks // seqs, HD))
    operands = (stream, own, other, grad, gain)
    return pl.pallas_call(
        functools.partial(leave_kernel, seqs, layer, len(after)),
        grid=(1,),
        out_shape=shapes,
        in_specs=[whole_block(operand) for operand in operands]
        + [column_block(width, columns, place)]
        + [ANYWHERE] * len(after),
        out_specs=[whole_block(shape) for shape in shapes],
        compiler_params=params(),
        cost_estimate=cost(2 * toks * width * columns, 6e6),
        name="leave_ffn",
    )(*operands, weight, *after)


def finish_kernel(layer, stream_ref, own_ref, other_ref, grad_ref, gain_ref, *refs):
    new_ref, gain_out, shift_out = refs[-3:]
    new_ref[...] = norm_back(
        layer, stream_ref, own_ref, other_ref, grad_ref, gain_ref, gain_out, shift_out
    )


def finish_attention(layer, stream, own, other, grad, gain, after=()):
    toks, width = stream.shape
    return pl.pallas_call(
        functools.partial(finish_kernel, layer),
        out_shape=(f32_out(toks, width), f32_out(1, width), f32_out(1, width)),
        in_specs=[IN_VMEM] * 5 + [ANYWHERE] * len(after),
        out_specs=(IN_VMEM,) * 3,
        compiler_params=params(),
        cost_estimate=cost(1e7, 4e6),
        name="finish_attention",
    )(stream, own, other, grad, gain, *after)


def reduce_rows(value):
    count = lax.axis_size("wide")
    index = lax.axis_index("wide")
    width = value.shape[1]
    block = value.shape[0] // count
    value = value.astype(BF16)
    stages = []
    bit = 1
    parts = count
    while bit < count:
        view = value.reshape(parts // 2, 2, block, width)
        mine = (index // bit) % 2
        sent = lax.dynamic_index_in_dim(view, 1 - mine, 1, keepdims=False)
        kept = lax.dynamic_index_in_dim(view, mine, 1, keepdims=False)
        value = kept.astype(F32) + swap(sent, "wide", bit).astype(F32)
        parts //= 2
        bit *= 2
        if bit < count:
            value = value.astype(BF16)
        stages.append(value)
    return stages[:-1] + [value.reshape(block, width)]


def sum_rows(value, widths):
    total = lax.psum_scatter(value, "wide", scatter_dimension=0, tiled=True).astype(F32)
    ends = [0]
    for width in widths:
        ends.append(ends[-1] + width)
    return [total[:, low:high] for low, high in zip(ends, ends[1:])]


def sum_wide(value):
    for bit in range(lax.axis_size("wide").bit_length() - 1):
        value = value + swap(value, "wide", 1 << bit)
    return value


def shards(
    first_in, second_in, attn_norm_gain, attn_norm_bias, qk_weight, value_weight, out_weight,
    out_bias, ffn_norm_gain, ffn_norm_bias, up_weight, up_bias, down_weight, down_bias,
    bucket_perm, first_cot, second_cot,
):
    seqs, rows, half = first_in.shape
    wide = lax.axis_size("wide")
    wide_index = lax.axis_index("wide")
    narrow_index = lax.axis_index("narrow")
    pos = jnp.stack([wide_index % 2, narrow_index]).astype(jnp.int32)
    weight_rows, head_width = qk_weight.shape[1:]
    heads = head_width // HD
    width = 2 * half
    hidden_width = up_bias.shape[1]
    chunks = range(CHUNKS)

    def own_half(full):
        return lax.dynamic_slice_in_dim(full, narrow_index * half, half, full.ndim - 1)

    def flat_weight(layer):
        pair = jnp.stack([qk_weight[layer], value_weight[layer]], axis=1)
        pair = pair.reshape(weight_rows, 2, heads, HD)
        return jnp.transpose(pair, (0, 2, 1, 3)).reshape(weight_rows, 2 * head_width)

    streams = (second_in, first_in, second_cot, first_cot)
    others = [swap(sent, "narrow", 1) for sent in lower_arrays(streams, ())]
    second, first = [widen_chunks(pos, streams[k], others[k]) for k in range(2)]
    early = lax.all_gather(
        jnp.concatenate([flat_weight(0), out_weight[0]], axis=1), "wide", axis=0, tiled=True
    )

    perm_parts = bucket_perm.reshape(2, ROUNDS // 2, seqs, rows)
    perm_send = jnp.transpose(perm_parts, (2, 0, 1, 3))
    perm_send = jnp.broadcast_to(
        perm_send[:, None], (seqs, heads, 2, ROUNDS // 2, rows)
    ).reshape(wide, ROUNDS // 2, rows)
    perm_got = lax.all_to_all(perm_send, "wide", 0, 0, tiled=True)
    tables = build_tables(jnp.transpose(perm_got, (1, 0, 2)).reshape(ROUNDS // 2, wide * rows))

    unit_columns = 2 * head_width
    gathered = [early]
    biases = jnp.stack([out_bias, down_bias])
    other = swap(biases, "narrow", 1)
    out_bias, down_bias = jnp.where(
        narrow_index == 0,
        jnp.concatenate([biases, other], axis=-1),
        jnp.concatenate([other, biases], axis=-1),
    )

    saved = []
    ffn_parts = [() for _ in chunks]
    afters = [[], [*tables, *first, *others[2:], out_bias, down_bias]]
    for layer in range(LAYERS):
        normed, sources = [], []
        for q in chunks:
            second[q], normed_q, units = enter_attention(
                seqs, layer, second[q], attn_norm_gain, attn_norm_bias, gathered[layer], 0,
                unit_columns, ffn_parts[q], afters[min(q, 1)],
            )
            normed.append(normed_q)
            own = chip_exchange(units)
            sources += [own, swap(own, "wide", 1)]
        sorted_rows, own, sib = attention_forward(pos, sources, tables, ())
        attn, stats, units = combine_cores(own, swap(sib, "wide", 1))
        after = []
        if layer == 0:
            grad_second, grad_first = [
                widen_chunks(pos, streams[k], others[k]) for k in range(2, 4)
            ]
            after = [*grad_second, *grad_first]
        if layer + 1 < LAYERS:
            pieces = pack_columns([flat_weight(layer + 1), out_weight[layer + 1]], units[:1])
            gathered.append(lax.all_gather(pieces, "wide", axis=0, tiled=True))
        second_now, attn_tok, ffn_in, pre_act = list(second), [], [], []
        backs = [chip_exchange(units[q]) for q in chunks]
        merged = []
        for q in chunks:
            part, attn_tok_q = merge_units(
                seqs, backs[q], gathered[layer], 2, after + attn_tok if q > 0 else ()
            )
            attn_tok.append(attn_tok_q)
            merged.append((part, swap(part, "narrow", 1)))
        for q in chunks:
            first[q], ffn_in_q, pre_q, part = feed_forward(
                layer, first[q], *merged[q], out_bias, ffn_norm_gain, ffn_norm_bias,
                up_weight, up_bias, down_weight, attn_tok[1:] + ffn_in,
            )
            ffn_in.append(ffn_in_q)
            pre_act.append(pre_q)
            if layer + 1 < LAYERS:
                ffn_parts[q] = (part, swap(part, "narrow", 1), down_bias)
            else:
                ffn_parts[q] = part
        afters = [ffn_in[1:], []]
        saved.append((second_now, normed, sorted_rows, attn, stats, attn_tok, list(first), ffn_in, pre_act))
    first_out = narrow_chunks(pos, first, seqs)
    sent = [
        lax.dynamic_slice_in_dim(part, (1 - narrow_index) * half, half, 1) for part in ffn_parts
    ]
    got = swap(jnp.concatenate(sent), "narrow", 1)
    second_out = narrow_chunks(pos, second, seqs, LAYERS - 1, [*ffn_parts, got, down_bias])
    summed, waiting = [], []
    done = []
    early_smalls, late_smalls = [None] * LAYERS, [None] * LAYERS
    after = []
    for layer in reversed(range(LAYERS)):
        second_l, normed, sorted_rows, attn, stats, attn_tok, first_l, ffn_in, pre_act = saved[layer]
        branch, hidden, low, parts = [], [], [], []
        late_gain, late_shift = 0.0, 0.0
        down_bias_grad, up_bias_grad = 0.0, 0.0
        for q in chunks:
            *results, branch_q, hidden_q, low_q, down_bias_q, up_bias_q, part = feed_back(
                layer, grad_second[q], up_weight, down_weight, pre_act[q],
                before[q] if layer + 1 < LAYERS else None,
            )
            if results:
                grad_second[q], gain_q, shift_q = results
                late_gain += gain_q
                late_shift += shift_q
            branch.append(branch_q)
            hidden.append(hidden_q)
            low.append(low_q)
            parts.append((part, swap(part, "narrow", 1)))
            down_bias_grad += down_bias_q
            up_bias_grad += up_bias_q
        pairs = waiting + [(ffn_in, low), (branch, hidden)]
        widths = [right[0].shape[1] for _, right in pairs]
        columns = sum(widths) + head_width
        if layer == 0:
            products = [weight_products(pairs, columns)]
        else:
            products = []
        out_low, units = [], []
        ffn_gain_grad, ffn_bias_grad, out_bias_grad = 0.0, 0.0, 0.0
        for q in chunks:
            *results, units_q = leave_ffn(
                seqs, layer, first_l[q], *parts[q], grad_first[q], ffn_norm_gain,
                gathered[layer], 2, head_width, [*units, *products] if q > 0 else (),
            )
            grad_first[q] = results[0]
            out_low.append(results[1])
            ffn_gain_grad += results[2]
            ffn_bias_grad += results[3]
            out_bias_grad += results[4]
            units.append(chip_exchange(units_q))
        if layer == 0:
            products = [
                weight_products([(out_low, attn_tok)], columns, columns - head_width, *products)
            ]
            summed += sum_rows(*products, widths + [head_width])
        sources = []
        for q in chunks:
            own = join_grads(q, attn, stats, units[q], products if q > 0 else ())
            sources += [own, swap(own, "wide", 1)]
        early_small = jnp.concatenate(
            [
                own_half(grad)
                for grad in (ffn_gain_grad, ffn_bias_grad, out_bias_grad, down_bias_grad)
            ]
            + [up_bias_grad.reshape(-1, half)]
        )
        own, sib = attention_backward(pos, sources, sorted_rows, tables, [early_small])
        units = add_cores(own, swap(sib, "wide", 1), done)
        grad_tok = []
        backs = [chip_exchange(units[q]) for q in chunks]
        after = []
        if layer > 0:
            pairs.append((out_low, attn_tok))
        merged = []
        for q in chunks:
            part, grad_tok_q = merge_units(seqs, backs[q], gathered[layer], 0, after + grad_tok)
            if layer > 0 and q == 0:
                products = weight_products(pairs, columns, after=[grad_tok_q])
                summed += sum_rows(products, widths + [head_width])
                after = [products]
            grad_tok.append(grad_tok_q)
            merged.append((part, swap(part, "narrow", 1)))
        waiting = [(normed, grad_tok)]
        stages = [None]
        if layer == 0:
            stages = reduce_rows(weight_products(waiting, unit_columns))
            summed.append(stages[-1])
        before = [
            (layer, second_l[q], *merged[q], attn_norm_gain) for q in chunks
        ]
        if layer + 1 < LAYERS:
            late_smalls[layer + 1] = (late_gain, late_shift)
        done = summed[-1:]
        early_smalls[layer] = early_small
    late_gain, late_shift = 0.0, 0.0
    for q in chunks:
        norm, stream, own, other, gain = before[q]
        grad_second[q], gain_q, shift_q = finish_attention(
            norm, stream, own, other, grad_second[q], gain, stages[q + 1 : q + 2]
        )
        late_gain += gain_q
        late_shift += shift_q
    late_smalls[0] = (late_gain, late_shift)
    small_grads = [
        jnp.concatenate([own_half(grad) for grad in late_smalls[layer]] + [early_smalls[layer]])
        for layer in range(LAYERS)
    ]
    first_grad = narrow_chunks(pos, grad_first, seqs)
    second_grad = narrow_chunks(pos, grad_second, seqs)

    small = sum_wide(jnp.stack(small_grads))
    other = swap(small[:, :4], "narrow", 1)
    paired = jnp.where(
        narrow_index == 0,
        jnp.concatenate([small[:, :4], other], axis=-1),
        jnp.concatenate([other, small[:, :4]], axis=-1),
    )
    order = [(4, 5, 6, 7), (0, 1, 2, 3)]
    weight_grads = [None] * LAYERS
    for layer in range(LAYERS):
        up_sum, down_sum, out_sum, unit_sum = [summed[at] for at in order[layer]]
        by_unit = unit_sum.reshape(weight_rows, heads, 2, HD)
        weight_grads[layer] = (
            by_unit[:, :, 0].reshape(weight_rows, head_width),
            by_unit[:, :, 1].reshape(weight_rows, head_width),
            out_sum,
            up_sum,
            down_sum,
        )

    def stacked(slot):
        return jnp.stack([weight_grads[layer][slot] for layer in range(LAYERS)])

    return (
        first_out,
        second_out,
        first_grad,
        second_grad,
        paired[:, 0],
        paired[:, 1],
        stacked(0),
        stacked(1),
        stacked(2),
        small[:, 4],
        paired[:, 2],
        paired[:, 3],
        stacked(3),
        small[:, 6:].reshape(LAYERS, hidden_width),
        stacked(4),
        small[:, 5],
    )


def solution(mesh):
    streams = P(None, "wide", "narrow")
    features = P(None, "narrow")
    hidden = P(None, None, "narrow")
    return jax.shard_map(
        shards,
        mesh=mesh,
        in_specs=(
            streams, streams, P(), P(), streams, streams, streams, features, P(), P(),
            hidden, features, hidden, features, P(None, None, "wide"), streams, streams,
        ),
        out_specs=(
            streams, streams, streams, streams, P(), P(), streams, streams, streams,
            features, P(), P(), streams, features, streams, features,
        ),
        check_vma=False,
    )
```

```python
import functools

import jax
import jax.numpy as jnp
from jax import lax
from jax.experimental import pallas as pl
from jax.experimental.pallas import tpu as pltpu
from jax.sharding import PartitionSpec as P

HD = 128
GROUP = 64
ROUNDS = 4
LAYERS = 2
BLOCK = 256
F32 = jnp.float32
BF16 = jnp.bfloat16
SCALE = HD ** (-0.5)
VMEM_LIMIT = 63 * 1024 * 1024
PAIRS = 8
SHARE = 0.01
CHUNKS = 2
FFN_STEPS = 2


def swap(value, axis, mask):
    count = lax.axis_size(axis)
    return lax.ppermute(value, axis, [(source, source ^ mask) for source in range(count)])


def dot(left, right, dims):
    return lax.dot_general(left, right, (dims, ((), ())), preferred_element_type=F32)


def mm(left, right):
    return dot(left, right, ((1,), (0,)))


def mm_t(left, right):
    return dot(left, right, ((1,), (1,)))


def t_mm(left, right):
    return dot(left, right, ((0,), (0,)))


def chip_exchange(units):
    count = lax.axis_size("wide")
    groups = [list(range(core, count, 2)) for core in range(2)]
    return lax.all_to_all(units, "wide", 0, 0, tiled=True, axis_index_groups=groups)


def split3(value):
    high = value.astype(BF16)
    rest = value - high.astype(F32)
    mid = rest.astype(BF16)
    low = (rest - mid.astype(F32)).astype(BF16)
    return high.astype(F32), mid.astype(F32), low.astype(F32)


def layer_norm(stream, gain, shift):
    centre = stream - jnp.mean(stream, axis=-1, keepdims=True)
    spread = jnp.mean(centre * centre, axis=-1, keepdims=True)
    return centre * lax.rsqrt(spread + 1e-05) * gain + shift


def layer_norm_back(stream, gain, grad):
    centre = stream - jnp.mean(stream, axis=-1, keepdims=True)
    inv = lax.rsqrt(jnp.mean(centre * centre, axis=-1, keepdims=True) + 1e-05)
    unit = centre * inv
    scaled = grad * gain
    back = inv * (
        scaled
        - jnp.mean(scaled, axis=-1, keepdims=True)
        - unit * jnp.mean(scaled * unit, axis=-1, keepdims=True)
    )
    return back, unit


def build_tables(tokens):
    rounds, seq = tokens.shape
    blocks = seq // BLOCK
    rank_rows = BLOCK // blocks
    tokens = tokens.reshape(rounds, blocks, BLOCK)
    run = tokens // BLOCK
    row = tokens % BLOCK
    onehot = (run[..., None] == jnp.arange(blocks, dtype=jnp.int32)).astype(BF16)
    before = (jnp.arange(BLOCK)[:, None] > jnp.arange(BLOCK)[None, :]).astype(BF16)
    counts = jnp.einsum("jl,rkla->rkja", before, onehot, preferred_element_type=F32)
    rank = jnp.sum(onehot.astype(F32) * counts, axis=-1).astype(jnp.int32)
    slot = run * rank_rows + rank
    iota = jnp.arange(BLOCK, dtype=jnp.int32)
    into = (slot[..., None] == iota).astype(BF16)
    into_t = (slot[..., None, :] == iota[:, None]).astype(BF16)
    wants = jnp.einsum("rknj,rkj->rkn", into_t, row.astype(BF16), preferred_element_type=F32)
    wants = wants.reshape(rounds, blocks, blocks, rank_rows)
    wants = jnp.transpose(wants, (0, 2, 1, 3)).reshape(rounds, blocks, BLOCK).astype(jnp.int32)
    out_of = (wants[..., None] == iota).astype(BF16)
    out_of_t = (wants[..., None, :] == iota[:, None]).astype(BF16)
    return jnp.transpose(out_of, (1, 0, 2, 3)), into, out_of_t, into_t


def token_copies(pos_ref, sources, tok, sems):
    core = pos_ref[0]
    chunks = len(sources) // 2
    slots, rows, _ = sources[0].shape
    copies = []
    for place, source in enumerate(sources):
        chunk, half = place // 2, place % 2
        for k in range(slots):
            device = 2 * k + (core ^ half)
            start = pl.multiple_of((device * chunks + chunk) * rows, rows)
            copies.append(
                pltpu.make_async_copy(
                    source.at[k], tok.at[pl.ds(start, rows)], sems.at[len(copies)]
                )
            )
    return copies


def table_copies(sources, targets, sems):
    return [
        pltpu.make_async_copy(source, target, sems.at[k])
        for k, (source, target) in enumerate(zip(sources, targets))
    ]


def store_run(pos_ref, buffer, run, value):
    core = pos_ref[0]
    _, chunks, _, rows, _ = buffer.shape
    for part in range(BLOCK // rows):
        device = run * (BLOCK // (rows * chunks)) + part // chunks
        buffer[(device & 1) ^ core, part % chunks, device >> 1] = value[
            part * rows : (part + 1) * rows
        ]


def send_halves(buffer, own_hbm, sib_hbm, sems):
    copies = [
        pltpu.make_async_copy(buffer.at[1], sib_hbm, sems.at[0]),
        pltpu.make_async_copy(buffer.at[0], own_hbm, sems.at[1]),
    ]
    for copy in copies:
        copy.start()
    for copy in copies:
        copy.wait()


def spread(first, count, width):
    row = lax.broadcasted_iota(jnp.int32, (HD, width), 0)
    return jnp.where((row >= first) & (row < first + count), 1.0, 0.0).astype(BF16)


def pack_stats(columns):
    lane = lax.broadcasted_iota(jnp.int32, columns[0].shape, 1)
    extra = jnp.zeros(columns[0].shape, F32)
    for place, column in enumerate(columns):
        extra = jnp.where(lane == place, column, extra)
    return extra


def permute_in(tok, out_of, mixed, blocks):
    rank = BLOCK // blocks
    for a in range(blocks):
        source = tok[a * BLOCK : (a + 1) * BLOCK, :]
        moved = mm(out_of[a].reshape(2 * BLOCK, BLOCK), source).astype(BF16)
        for r in range(2):
            mixed[r, :, a] = moved[r * BLOCK : (r + 1) * BLOCK].reshape(blocks, rank, 2 * HD)


def split_rows(tile):
    lane = lax.broadcasted_iota(jnp.int32, tile.shape, 1)
    zero = jnp.zeros_like(tile)
    return jnp.concatenate(
        [jnp.where(lane < GROUP, tile, zero), jnp.where(lane >= GROUP, tile, zero)], axis=0
    )


def split_lanes(tile):
    row = lax.broadcasted_iota(jnp.int32, tile.shape, 0)
    zero = jnp.zeros_like(tile)
    return jnp.concatenate(
        [jnp.where(row < GROUP, tile, zero), jnp.where(row >= GROUP, tile, zero)], axis=1
    )


def side_by_side(ref, base):
    return jnp.concatenate(
        [ref[base : base + 2 * GROUP, :], ref[base + GROUP : base + 3 * GROUP, :]], axis=1
    )


def one_above(ref, base):
    return jnp.concatenate(
        [ref[base : base + 2 * GROUP, :], ref[base + GROUP : base + 3 * GROUP, :]], axis=0
    )


def self_mask():
    row = lax.broadcasted_iota(jnp.int32, (2 * GROUP, 2 * GROUP), 0)
    lane = lax.broadcasted_iota(jnp.int32, (2 * GROUP, 2 * GROUP), 1)
    return row == lane % GROUP + GROUP


def unit_keys(query):
    return query * lax.rsqrt(jnp.mean(query * query, axis=-1, keepdims=True) + 1e-06)


def forward_kernel(chunks, extras, pos_ref, *refs):
    sources, refs = refs[: 2 * chunks], refs[2 * chunks + extras :]
    (
        out_of_hbm, into_hbm, out_of_t_hbm, into_t_hbm, sorted_hbm, own_hbm, sib_hbm,
        tok, mixed, keys, vals, placed, buffer, out_of, into, out_of_t, into_t,
        tok_sems, table_sems, out_sems, send_sems,
    ) = refs
    seq = tok.shape[0]
    blocks = seq // BLOCK
    rank = BLOCK // blocks
    loads = token_copies(pos_ref, sources, tok, tok_sems)
    tables = table_copies(
        (out_of_hbm, into_hbm, into_t_hbm, out_of_t_hbm), (out_of, into, into_t, out_of_t), table_sems
    )
    for copy in loads:
        copy.start()
    for copy in tables:
        copy.start()
    for copy in loads:
        copy.wait()
    tables[0].wait()
    permute_in(tok, out_of, mixed, blocks)
    tables[1].wait()
    outs = []
    for r in range(2):
        for k in range(blocks):
            base = k * BLOCK
            rows_sorted = mm(into[r, k], mixed[r, k].reshape(BLOCK, 2 * HD))
            placed[r, base : base + BLOCK, :] = rows_sorted.astype(BF16)
            where = slice(base + GROUP, base + GROUP + BLOCK)
            keys[r, where, :] = unit_keys(rows_sorted[:, :HD]).astype(BF16)
            vals[r, where, :] = rows_sorted[:, HD:].astype(BF16)
        keys[r, 0:GROUP, :] = keys[r, seq : seq + GROUP, :]
        vals[r, 0:GROUP, :] = vals[r, seq : seq + GROUP, :]
        outs.append(pltpu.make_async_copy(placed.at[r], sorted_hbm.at[r], out_sems.at[r]))
        outs[-1].start()
    tables[2].wait()
    own = jnp.concatenate([self_mask()] * PAIRS, axis=1)
    wide = PAIRS * 2 * GROUP
    for r in range(2):
        for first in range(0, seq, wide):
            bases = [first + p * 2 * GROUP for p in range(PAIRS)]
            flipped = [placed[r, base : base + 2 * GROUP, 0:HD].T for base in bases]
            raw = jnp.concatenate(
                [
                    mm(side_by_side(keys.at[r], base), split_rows(tile))
                    for base, tile in zip(bases, flipped)
                ],
                axis=1,
            )
            scores = jnp.where(own, -1000000000.0, raw * SCALE)
            top = jnp.max(scores, axis=0, keepdims=True)
            weight = jnp.exp(scores - top)
            total = jnp.sum(weight, axis=0, keepdims=True)
            probs = (weight * (1.0 / total)).astype(BF16)
            row = lax.broadcasted_iota(jnp.int32, (8, wide), 0)
            stats = jnp.zeros((8, wide), F32)
            for place, part in enumerate(split3(top + jnp.log(total))):
                stats = jnp.where(row == place, part, stats)
            stats = jnp.concatenate([stats, jnp.zeros((HD - 8, wide), F32)], axis=0)
            lanes = [slice(p * 2 * GROUP, (p + 1) * 2 * GROUP) for p in range(PAIRS)]
            turned = [probs[:, lane].T for lane in lanes]
            extra = [stats[:, lane].T.astype(BF16) for lane in lanes]
            result = [
                mm(split_lanes(tile), one_above(vals.at[r], base)).astype(BF16)
                for tile, base in zip(turned, bases)
            ]
            packed = jnp.concatenate(
                [jnp.concatenate(pair, axis=1) for pair in zip(result, extra)], axis=0
            )
            for part in range(wide // BLOCK):
                k = first // BLOCK + part
                back = mm(into_t[r, k], packed[part * BLOCK : (part + 1) * BLOCK]).astype(BF16)
                mixed[r, k] = back.reshape(blocks, rank, 2 * HD)
    tables[3].wait()
    zero = jnp.zeros((HD, HD), BF16)
    ones = spread(0, 3, HD)
    ones = jnp.concatenate(
        [jnp.concatenate([ones, zero], axis=1), jnp.concatenate([zero, ones], axis=1)], axis=0
    )
    for a in range(blocks):
        moved = [mm(out_of_t[r, a], mixed[r, :, a].reshape(BLOCK, 2 * HD)) for r in range(2)]
        lse = mm(jnp.concatenate([m[:, HD:] for m in moved], axis=1).astype(BF16), ones)
        lse_a, lse_b = lse[:, :HD], lse[:, HD:]
        top = jnp.maximum(lse_a, lse_b)
        weight_a, weight_b = jnp.exp(lse_a - top), jnp.exp(lse_b - top)
        total = weight_a + weight_b
        value = (moved[0][:, :HD] * weight_a + moved[1][:, :HD] * weight_b) * (1.0 / total)
        extra = pack_stats(split3(top + jnp.log(total)))
        store_run(pos_ref, buffer, a, jnp.concatenate([value, extra], axis=1).astype(BF16))
    send_halves(buffer, own_hbm, sib_hbm, send_sems)
    for copy in outs:
        copy.wait()


def backward_kernel(chunks, extras, pos_ref, *refs):
    sources, refs = refs[: 2 * chunks], refs[2 * chunks + extras :]
    (
        sorted_hbm, out_of_hbm, into_hbm, out_of_t_hbm, into_t_hbm, own_hbm, sib_hbm,
        tok, mixed, keys, vals, placed, grads, query_use, key_grad, val_grad, buffer,
        out_of, into, out_of_t, into_t, tok_sems, table_sems, in_sems, send_sems,
    ) = refs
    seq = tok.shape[0]
    blocks = seq // BLOCK
    rank = BLOCK // blocks
    loads = token_copies(pos_ref, sources, tok, tok_sems)
    tables = table_copies(
        (out_of_hbm, into_hbm, into_t_hbm, out_of_t_hbm), (out_of, into, into_t, out_of_t), table_sems
    )
    sorted_in = pltpu.make_async_copy(sorted_hbm, placed, in_sems.at[0])
    for copy in loads:
        copy.start()
    tables[0].start()
    sorted_in.start()
    for copy in tables[1:]:
        copy.start()
    for copy in loads:
        copy.wait()
    tables[0].wait()
    permute_in(tok, out_of, mixed, blocks)
    sorted_in.wait()
    tables[1].wait()
    for r in range(2):
        for k in range(blocks):
            here = slice(k * BLOCK, (k + 1) * BLOCK)
            where = slice(k * BLOCK + GROUP, (k + 1) * BLOCK + GROUP)
            grads[r, here, :] = mm(into[r, k], mixed[r, k].reshape(BLOCK, 2 * HD)).astype(BF16)
            keys[r, where, :] = unit_keys(placed[r, here, 0:HD].astype(F32)).astype(BF16)
            vals[r, where, :] = placed[r, here, HD:]
        keys[r, 0:GROUP, :] = keys[r, seq : seq + GROUP, :]
        vals[r, 0:GROUP, :] = vals[r, seq : seq + GROUP, :]
        key_grad[r, 0:GROUP, :] = jnp.zeros((GROUP, HD), F32)
        val_grad[r, 0:GROUP, :] = jnp.zeros((GROUP, HD), F32)
    own = jnp.concatenate([self_mask()] * PAIRS, axis=1)
    wide = PAIRS * 2 * GROUP
    lanes = [slice(p * 2 * GROUP, (p + 1) * 2 * GROUP) for p in range(PAIRS)]
    for r in range(2):
        for first in range(0, seq, wide):
            bases = [first + p * 2 * GROUP for p in range(PAIRS)]
            query = [placed[r, base : base + 2 * GROUP, 0:HD] for base in bases]
            grad = [grads[r, base : base + 2 * GROUP, 0:HD] for base in bases]
            stats = jnp.concatenate(
                [
                    grads[r, base : base + 2 * GROUP, HD:].astype(F32).T[0:8] for base in bases
                ],
                axis=1,
            )
            delta = stats[0:1] + stats[1:2] + stats[2:3]
            lse = stats[3:4] + stats[4:5] + stats[5:6]
            query_t = [split_rows(tile.T) for tile in query]
            grad_t = [split_rows(tile.T) for tile in grad]
            raw = jnp.concatenate(
                [mm(side_by_side(keys.at[r], base), tile) for base, tile in zip(bases, query_t)],
                axis=1,
            )
            prob_grad = jnp.concatenate(
                [mm(side_by_side(vals.at[r], base), tile) for base, tile in zip(bases, grad_t)],
                axis=1,
            )
            probs = jnp.exp(jnp.where(own, -1000000000.0, raw * SCALE) - lse)
            score_grad = (probs * (prob_grad - delta)).astype(BF16)
            probs = probs.astype(BF16)
            turned = [score_grad[:, lane].T for lane in lanes]
            for tile, base in zip(turned, bases):
                query_use[r, base : base + 2 * GROUP, :] = (
                    mm(split_lanes(tile), one_above(keys.at[r], base)) * SCALE
                )
            key_parts = [
                mm(split_rows(score_grad[:, lane]), tile) * SCALE for lane, tile in zip(lanes, query)
            ]
            val_parts = [mm(split_rows(probs[:, lane]), tile) for lane, tile in zip(lanes, grad)]
            for target, parts in ((key_grad, key_parts), (val_grad, val_parts)):
                target[r, first : first + GROUP, :] += parts[0][:GROUP]
                for p, (part, base) in enumerate(zip(parts, bases)):
                    target[r, base + GROUP : base + 2 * GROUP, :] = (
                        part[GROUP : 2 * GROUP] + part[2 * GROUP : 3 * GROUP]
                    )
                    last = part[3 * GROUP :]
                    if p + 1 < PAIRS:
                        last = last + parts[p + 1][:GROUP]
                    target[r, base + 2 * GROUP : base + 3 * GROUP, :] = last
        key_grad[r, seq : seq + GROUP, :] += key_grad[r, 0:GROUP, :]
        val_grad[r, seq : seq + GROUP, :] += val_grad[r, 0:GROUP, :]
    tables[2].wait()
    for r in range(2):
        for k in range(blocks):
            here = slice(k * BLOCK, (k + 1) * BLOCK)
            where = slice(k * BLOCK + GROUP, (k + 1) * BLOCK + GROUP)
            query = placed[r, here, 0:HD].astype(F32)
            inv = lax.rsqrt(jnp.mean(query * query, axis=-1, keepdims=True) + 1e-06)
            grad = key_grad[r, where, :]
            inner = jnp.mean(grad * query, axis=-1, keepdims=True)
            total = query_use[r, here, :] + inv * (grad - query * (inner * inv * inv))
            packed = jnp.concatenate([total, val_grad[r, where, :]], axis=1).astype(BF16)
            back = mm(into_t[r, k], packed).astype(BF16)
            mixed[r, k] = back.reshape(blocks, rank, 2 * HD)
    tables[3].wait()
    for a in range(blocks):
        total = mm(out_of_t[0, a], mixed[0, :, a].reshape(BLOCK, 2 * HD)) + mm(
            out_of_t[1, a], mixed[1, :, a].reshape(BLOCK, 2 * HD)
        )
        store_run(pos_ref, buffer, a, total.astype(BF16))
    send_halves(buffer, own_hbm, sib_hbm, send_sems)


def params():
    return pltpu.CompilerParams(vmem_limit_bytes=VMEM_LIMIT)


def cost(flops, moved):
    return pl.CostEstimate(flops=int(flops * SHARE), bytes_accessed=int(moved * SHARE), transcendentals=0)


IN_SMEM = pl.BlockSpec(memory_space=pltpu.SMEM)
IN_VMEM = pl.BlockSpec(memory_space=pltpu.VMEM)
ANYWHERE = pl.BlockSpec(memory_space=pl.ANY)


def bf16_out(*shape):
    return jax.ShapeDtypeStruct(shape, BF16)


def f32_out(*shape):
    return jax.ShapeDtypeStruct(shape, F32)


def table_scratch(blocks):
    return [
        pltpu.VMEM((blocks, 2, BLOCK, BLOCK), BF16),
        pltpu.VMEM((2, blocks, BLOCK, BLOCK), BF16),
        pltpu.VMEM((2, blocks, BLOCK, BLOCK), BF16),
        pltpu.VMEM((2, blocks, BLOCK, BLOCK), BF16),
    ]


def attention_forward(pos, sources, tables, after):
    chunks = len(sources) // 2
    slots, rows, width = sources[0].shape
    seq = 2 * slots * rows * chunks
    blocks = seq // BLOCK
    half = bf16_out(chunks, slots, rows, width)
    return pl.pallas_call(
        functools.partial(forward_kernel, chunks, len(after)),
        out_shape=(bf16_out(2, seq, width), half, half),
        in_specs=[IN_SMEM] + [ANYWHERE] * (2 * chunks + len(after) + 4),
        out_specs=(ANYWHERE, ANYWHERE, ANYWHERE),
        scratch_shapes=[
            pltpu.VMEM((seq, width), BF16),
            pltpu.VMEM((2, blocks, blocks, BLOCK // blocks, width), BF16),
            pltpu.VMEM((2, seq + GROUP, HD), BF16),
            pltpu.VMEM((2, seq + GROUP, HD), BF16),
            pltpu.VMEM((2, seq, width), BF16),
            pltpu.VMEM((2, chunks, slots, rows, width), BF16),
            *table_scratch(blocks),
            pltpu.SemaphoreType.DMA((2 * slots * chunks,)),
            pltpu.SemaphoreType.DMA((4,)),
            pltpu.SemaphoreType.DMA((2,)),
            pltpu.SemaphoreType.DMA((2,)),
        ],
        compiler_params=params(),
        cost_estimate=cost(16e9, 24e6),
        name="attend_forward",
    )(pos, *sources, *after, *tables)


def attention_backward(pos, sources, sorted_rows, tables, after):
    chunks = len(sources) // 2
    slots, rows, width = sources[0].shape
    seq = 2 * slots * rows * chunks
    blocks = seq // BLOCK
    half = bf16_out(chunks, slots, rows, width)
    return pl.pallas_call(
        functools.partial(backward_kernel, chunks, len(after)),
        out_shape=(half, half),
        in_specs=[IN_SMEM] + [ANYWHERE] * (2 * chunks + len(after) + 5),
        out_specs=(ANYWHERE, ANYWHERE),
        scratch_shapes=[
            pltpu.VMEM((seq, width), BF16),
            pltpu.VMEM((2, blocks, blocks, BLOCK // blocks, width), BF16),
            pltpu.VMEM((2, seq + GROUP, HD), BF16),
            pltpu.VMEM((2, seq + GROUP, HD), BF16),
            pltpu.VMEM((2, seq, width), BF16),
            pltpu.VMEM((2, seq, width), BF16),
            pltpu.VMEM((2, seq, HD), F32),
            pltpu.VMEM((2, seq + GROUP, HD), F32),
            pltpu.VMEM((2, seq + GROUP, HD), F32),
            pltpu.VMEM((2, chunks, slots, rows, width), BF16),
            *table_scratch(blocks),
            pltpu.SemaphoreType.DMA((2 * slots * chunks,)),
            pltpu.SemaphoreType.DMA((4,)),
            pltpu.SemaphoreType.DMA((1,)),
            pltpu.SemaphoreType.DMA((2,)),
        ],
        compiler_params=params(),
        cost_estimate=cost(18e9, 26e6),
        name="attend_backward",
    )(pos, *sources, *after, sorted_rows, *tables)


def unit_slices(seqs, heads, rows, width):
    return [
        (slice(seq * rows, (seq + 1) * rows), slice(head * width, (head + 1) * width))
        for seq in range(seqs)
        for head in range(heads)
    ]


def column_block(rows, width, place):
    return pl.BlockSpec((rows, width), lambda i: (0, place))


def whole_block(array):
    return pl.BlockSpec(array.shape, lambda i: (0,) * len(array.shape))


def pack_kernel(count, *refs):
    out_ref = refs[-1]
    start = 0
    for ref in refs[:count]:
        out_ref[:, start : start + ref.shape[1]] = ref[...]
        start += ref.shape[1]


def pack_columns(pieces, after):
    rows, columns = pieces[0].shape[0], sum(piece.shape[1] for piece in pieces)
    return pl.pallas_call(
        functools.partial(pack_kernel, len(pieces)),
        out_shape=bf16_out(rows, columns),
        in_specs=[IN_VMEM] * len(pieces) + [ANYWHERE] * len(after),
        out_specs=IN_VMEM,
        compiler_params=params(),
        name="pack_columns",
    )(*pieces, *after)


def lower_kernel(count, *refs):
    for source, target in zip(refs[:count], refs[-count:]):
        target[...] = source[...].astype(BF16)


def lower_arrays(arrays, after):
    return pl.pallas_call(
        functools.partial(lower_kernel, len(arrays)),
        out_shape=[bf16_out(*array.shape) for array in arrays],
        in_specs=[IN_VMEM] * len(arrays) + [ANYWHERE] * len(after),
        out_specs=[IN_VMEM] * len(arrays),
        compiler_params=params(),
        name="lower_arrays",
    )(*arrays, *after)


def widen_kernel(pos_ref, mine_ref, other_ref, *out_refs):
    seqs, rows, half = mine_ref.shape
    count = rows // len(out_refs)
    mine_at = pl.ds(pl.multiple_of(pos_ref[1] * half, half), half)
    other_at = pl.ds(pl.multiple_of((1 - pos_ref[1]) * half, half), half)
    for q, out_ref in enumerate(out_refs):
        for seq in range(seqs):
            at = slice(seq * count, (seq + 1) * count)
            source = slice(q * count, (q + 1) * count)
            out_ref[at, mine_at] = mine_ref[seq, source]
            out_ref[at, other_at] = other_ref[seq, source].astype(F32)


def widen_chunks(pos, mine, other):
    seqs, rows, half = mine.shape
    out = f32_out(seqs * rows // CHUNKS, 2 * half)
    return list(
        pl.pallas_call(
            widen_kernel,
            out_shape=[out] * CHUNKS,
            in_specs=[IN_SMEM, IN_VMEM, IN_VMEM],
            out_specs=[IN_VMEM] * CHUNKS,
            compiler_params=params(),
            cost_estimate=cost(1e6, 4e6),
            name="widen_chunks",
        )(pos, mine, other)
    )


def narrow_kernel(layer, pos_ref, *refs):
    out_ref = refs[-1]
    seqs, rows, half = out_ref.shape
    count = rows // CHUNKS
    lanes = pl.ds(pl.multiple_of(pos_ref[1] * half, half), half)
    for q in range(CHUNKS):
        for seq in range(seqs):
            at = slice(seq * count, (seq + 1) * count)
            value = refs[q][at, lanes]
            if layer is not None:
                own, other, bias = refs[CHUNKS + q], refs[2 * CHUNKS], refs[2 * CHUNKS + 1]
                got = other[q * seqs * count + seq * count : q * seqs * count + (seq + 1) * count]
                value = value + (own[at, lanes].astype(F32) + got.astype(F32))
                value = value + bias[layer : layer + 1, lanes]
            out_ref[seq, q * count : (q + 1) * count] = value


def narrow_chunks(pos, chunks, seqs, layer=None, parts=(), after=()):
    toks, width = chunks[0].shape
    return pl.pallas_call(
        functools.partial(narrow_kernel, layer),
        out_shape=f32_out(seqs, toks * CHUNKS // seqs, width // 2),
        in_specs=[IN_SMEM]
        + [IN_VMEM] * (CHUNKS + len(parts))
        + [ANYWHERE] * len(after),
        out_specs=IN_VMEM,
        compiler_params=params(),
        cost_estimate=cost(1e6, 4e6),
        name="narrow_chunks",
    )(pos, *chunks, *parts, *after)


def enter_kernel(
    seqs, layer, parts, after, stream_ref, gain_ref, shift_ref, weight_ref, *refs
):
    stream = stream_ref[...]
    if parts:
        own_ref, other_ref, bias_ref, *refs = refs
        stream = stream + (own_ref[...].astype(F32) + other_ref[...].astype(F32))
        stream = stream + bias_ref[layer - 1 : layer]
    refs = refs[after:]
    if parts:
        refs[0][...] = stream
    normed_ref, out_ref = refs[-2:]
    row = slice(layer, layer + 1)
    normed = layer_norm(stream, gain_ref[row], shift_ref[row]).astype(BF16)
    normed_ref[...] = normed
    flat = mm(normed, weight_ref[...]).astype(BF16)
    slots, rows, width = out_ref.shape
    for k, at in enumerate(unit_slices(seqs, slots // seqs, rows, width)):
        out_ref[k] = flat[at]


def enter_attention(seqs, layer, stream, gain, shift, weight, place, columns, parts=(), after=()):
    toks, width = stream.shape
    slots = seqs * columns // (2 * HD)
    shapes = [bf16_out(toks, width), bf16_out(slots, toks // seqs, 2 * HD)]
    if parts:
        shapes = [f32_out(toks, width)] + shapes
    results = pl.pallas_call(
        functools.partial(enter_kernel, seqs, layer, len(parts) > 0, len(after)),
        grid=(1,),
        out_shape=shapes,
        in_specs=[whole_block(stream), whole_block(gain), whole_block(shift)]
        + [column_block(width, columns, place)]
        + [whole_block(part) for part in parts]
        + [ANYWHERE] * len(after),
        out_specs=[whole_block(shape) for shape in shapes],
        compiler_params=params(),
        cost_estimate=cost(2 * toks * width * columns, 5e6),
        name="enter_attention",
    )(stream, gain, shift, weight, *parts, *after)
    return results if parts else (stream, *results)


def merge_kernel(seqs, weight_ref, in_ref, *refs):
    part_ref, tok_ref = refs[-2:]
    slots, rows, width = in_ref.shape
    for k, at in enumerate(unit_slices(seqs, slots // seqs, rows, width)):
        tok_ref[at] = in_ref[k]
    part_ref[...] = mm_t(tok_ref[...], weight_ref[...]).astype(BF16)


def merge_units(seqs, units, weight, place, after=()):
    slots, rows, width = units.shape
    toks, columns = seqs * rows, slots // seqs * width
    shapes = (bf16_out(toks, weight.shape[0]), bf16_out(toks, columns))
    return pl.pallas_call(
        functools.partial(merge_kernel, seqs),
        grid=(1,),
        out_shape=shapes,
        in_specs=[column_block(weight.shape[0], columns, place), whole_block(units)]
        + [ANYWHERE] * len(after),
        out_specs=[whole_block(shape) for shape in shapes],
        compiler_params=params(),
        cost_estimate=cost(2 * toks * columns * weight.shape[0], 3e6),
        name="merge_units",
    )(weight, units, *after)


def both_stats(own, got):
    zero = jnp.zeros((HD, HD), BF16)
    ones = spread(0, 3, HD)
    ones = jnp.concatenate(
        [jnp.concatenate([ones, zero], axis=1), jnp.concatenate([zero, ones], axis=1)], axis=0
    )
    lse = mm(jnp.concatenate([own, got], axis=1), ones)
    return lse[:, :HD], lse[:, HD:]


def combine_kernel(after, own_ref, got_ref, *refs):
    attn_ref, stats_ref, *out_refs = refs[after:]
    chunks, slots, rows, _ = own_ref.shape
    for q in range(chunks):
        for k in range(slots):
            lse_a, lse_b = both_stats(own_ref[q, k, :, HD:], got_ref[q, k, :, HD:])
            top = jnp.maximum(lse_a, lse_b)
            weight_a, weight_b = jnp.exp(lse_a - top), jnp.exp(lse_b - top)
            total = weight_a + weight_b
            own = own_ref[q, k, :, :HD].astype(F32)
            got = got_ref[q, k, :, :HD].astype(F32)
            value = (own * weight_a + got * weight_b) * (1.0 / total)
            attn_ref[q, k] = value
            zero = jnp.zeros_like(total)
            stats_ref[q, k] = pack_stats(
                (zero, zero, zero) + split3(top + jnp.log(total))
            ).astype(BF16)
            out_refs[q][k] = value.astype(BF16)


def combine_cores(own, got, after=()):
    chunks, slots, rows, _ = own.shape
    results = pl.pallas_call(
        functools.partial(combine_kernel, len(after)),
        out_shape=[f32_out(chunks, slots, rows, HD), bf16_out(chunks, slots, rows, HD)]
        + [bf16_out(slots, rows, HD)] * chunks,
        in_specs=[IN_VMEM] * 2 + [ANYWHERE] * len(after),
        out_specs=[IN_VMEM] * (2 + chunks),
        compiler_params=params(),
        cost_estimate=cost(1e8, 5e6),
        name="combine_cores",
    )(own, got, *after)
    return results[0], results[1], results[2:]


def join_kernel(attn_ref, stats_ref, in_ref, *refs):
    out_ref = refs[-1]
    for k in range(in_ref.shape[0]):
        grad = in_ref[k]
        delta = jnp.sum(attn_ref[0, k] * grad.astype(F32), axis=-1, keepdims=True)
        delta = jnp.broadcast_to(delta, grad.shape)
        extra = pack_stats(split3(delta)) + stats_ref[0, k].astype(F32)
        out_ref[k] = jnp.concatenate([grad, extra.astype(BF16)], axis=1)


def join_grads(chunk, attn, stats, units, after=()):
    slots, rows, _ = units.shape
    spec = pl.BlockSpec((1, slots, rows, HD), lambda i: (chunk, 0, 0, 0))
    return pl.pallas_call(
        join_kernel,
        grid=(1,),
        out_shape=bf16_out(slots, rows, 2 * HD),
        in_specs=[spec, spec, pl.BlockSpec((slots, rows, HD), lambda i: (0, 0, 0))]
        + [ANYWHERE] * len(after),
        out_specs=pl.BlockSpec((slots, rows, 2 * HD), lambda i: (0, 0, 0)),
        compiler_params=params(),
        cost_estimate=cost(1e7, 2e6),
        name="join_grads",
    )(attn, stats, units, *after)


def add_kernel(after, own_ref, got_ref, *refs):
    for q, out_ref in enumerate(refs[after:]):
        total = own_ref[q].astype(F32) + got_ref[q].astype(F32)
        out_ref[...] = total.astype(BF16)


def add_cores(own, got, after=()):
    chunks, slots, rows, width = own.shape
    return pl.pallas_call(
        functools.partial(add_kernel, len(after)),
        out_shape=[bf16_out(slots, rows, width)] * chunks,
        in_specs=[IN_VMEM] * 2 + [ANYWHERE] * len(after),
        out_specs=[IN_VMEM] * chunks,
        compiler_params=params(),
        cost_estimate=cost(1e6, 3e6),
        name="add_cores",
    )(own, got, *after)


def ffn_kernel(
    layer, stream_ref, own_ref, other_ref, bias_ref, gain_ref, shift_ref, up_ref, up_bias_ref,
    down_ref, *refs,
):
    new_ref, normed_ref, pre_ref, part_ref, acc = refs[-5:]
    step = pl.program_id(0)
    row = slice(layer, layer + 1)

    @pl.when(step == 0)
    def _():
        stream = stream_ref[...] + (own_ref[...].astype(F32) + other_ref[...].astype(F32))
        stream = stream + bias_ref[row]
        new_ref[...] = stream
        normed_ref[...] = layer_norm(stream, gain_ref[row], shift_ref[row]).astype(BF16)

    pre = mm(normed_ref[...], up_ref[0]) + up_bias_ref[row]
    pre_ref[...] = pre
    hidden = jax.nn.gelu(pre, approximate=True).astype(BF16)
    part = mm_t(hidden, down_ref[0])

    @pl.when(step == 0)
    def _():
        acc[...] = part

    @pl.when(step > 0)
    def _():
        acc[...] += part

    @pl.when(step == pl.num_programs(0) - 1)
    def _():
        part_ref[...] = acc[...].astype(BF16)


def feed_forward(layer, stream, own, other, bias, gain, shift, up, up_bias, down, after=()):
    toks, width = stream.shape
    hidden = up.shape[2]
    step = hidden // FFN_STEPS
    full = pl.BlockSpec((toks, width), lambda i: (0, 0))
    slab = pl.BlockSpec((1, width, step), lambda i: (layer, 0, i))
    return pl.pallas_call(
        functools.partial(ffn_kernel, layer),
        grid=(FFN_STEPS,),
        out_shape=(
            f32_out(toks, width), bf16_out(toks, width), f32_out(toks, hidden), bf16_out(toks, width),
        ),
        in_specs=[
            full, full, full, whole_block(bias), whole_block(gain), whole_block(shift), slab,
            pl.BlockSpec((LAYERS, step), lambda i: (0, i)), slab,
        ]
        + [ANYWHERE] * len(after),
        out_specs=(full, full, pl.BlockSpec((toks, step), lambda i: (0, i)), full),
        scratch_shapes=[pltpu.VMEM((toks, width), F32)],
        compiler_params=params(),
        cost_estimate=cost(4 * toks * width * hidden, 14e6),
        name="feed_forward",
    )(stream, own, other, bias, gain, shift, up, up_bias, down, *after)


def ffn_back_kernel(norm, *refs):
    if norm is None:
        grad_ref, up_ref, down_ref, pre_ref, *refs = refs
    else:
        stream_ref, own_ref, other_ref, grad_ref, gain_ref, up_ref, down_ref, pre_ref, *refs = refs
        new_ref, gain_out, shift_out, *refs = refs
    branch_ref, hidden_ref, low_ref, down_bias_ref, up_bias_ref, part_ref, acc = refs
    step = pl.program_id(0)

    @pl.when(step == 0)
    def _():
        if norm is None:
            grad = grad_ref[...]
        else:
            grad = norm_back(
                norm, stream_ref, own_ref, other_ref, grad_ref, gain_ref, gain_out, shift_out
            )
            new_ref[...] = grad
        branch_ref[...] = grad.astype(BF16)
        down_bias_ref[...] = jnp.sum(grad, axis=0, keepdims=True)

    hidden_grad = mm(branch_ref[...], down_ref[0])
    pre = pre_ref[...]
    root = 0.7978845608028654
    square = pre * pre
    bend = jnp.tanh(root * (pre + 0.044715 * (square * pre)))
    half = 0.5 * (1.0 + bend)
    hidden_ref[...] = (pre * half).astype(BF16)
    slope = half + 0.5 * pre * (1.0 - bend * bend) * (root * (1.0 + 3 * 0.044715 * square))
    pre_grad = hidden_grad * slope
    up_bias_ref[...] = jnp.sum(pre_grad, axis=0, keepdims=True)
    low = pre_grad.astype(BF16)
    low_ref[...] = low
    part = mm_t(low, up_ref[0])

    @pl.when(step == 0)
    def _():
        acc[...] = part

    @pl.when(step > 0)
    def _():
        acc[...] += part

    @pl.when(step == pl.num_programs(0) - 1)
    def _():
        part_ref[...] = acc[...].astype(BF16)


def feed_back(layer, grad, up, down, pre, before=None):
    toks, width = grad.shape
    hidden = down.shape[2]
    step = hidden // FFN_STEPS
    full = pl.BlockSpec((toks, width), lambda i: (0, 0))
    line = pl.BlockSpec((1, width), lambda i: (0, 0))
    slab = pl.BlockSpec((1, width, step), lambda i: (layer, 0, i))
    tall = pl.BlockSpec((toks, step), lambda i: (0, i))
    shapes = [
        bf16_out(toks, width), bf16_out(toks, hidden), bf16_out(toks, hidden),
        f32_out(1, width), f32_out(1, hidden), bf16_out(toks, width),
    ]
    out_specs = [full, tall, tall, line, pl.BlockSpec((1, step), lambda i: (0, i)), full]
    operands, in_specs = [grad], [full]
    if before is not None:
        norm, stream, own, other, gain = before
        operands = [stream, own, other, grad, gain]
        in_specs = [full] * 4 + [whole_block(gain)]
        shapes = [f32_out(toks, width), f32_out(1, width), f32_out(1, width)] + shapes
        out_specs = [full, line, line] + out_specs
    return pl.pallas_call(
        functools.partial(ffn_back_kernel, None if before is None else norm),
        grid=(FFN_STEPS,),
        out_shape=shapes,
        in_specs=in_specs + [slab, slab, tall],
        out_specs=out_specs,
        scratch_shapes=[pltpu.VMEM((toks, width), F32)],
        compiler_params=params(),
        cost_estimate=cost(4 * toks * width * hidden, 15e6),
        name="feed_back",
    )(*operands, up, down, pre)


def products_kernel(counts, *refs):
    out_ref, turned = refs[-2:]
    step = pl.program_id(0)
    start = 0
    for place, count in enumerate(counts):
        lefts = refs[2 * CHUNKS * place : 2 * CHUNKS * place + CHUNKS]
        rights = refs[2 * CHUNKS * place + CHUNKS : 2 * CHUNKS * (place + 1)]

        @pl.when(step == start)
        def _(lefts=lefts):
            for q, left in enumerate(lefts):
                toks = left.shape[0]
                turned[:, q * toks : (q + 1) * toks] = left[...].T

        @pl.when((step >= start) & (step < start + count))
        def _(rights=rights):
            right = jnp.concatenate([right[...] for right in rights], axis=0)
            out_ref[...] = mm(turned[...], right).astype(BF16)

        start += count


def weight_products(pairs, columns, at=0, target=None, after=()):
    block = min(right[0].shape[1] for _, right in pairs)
    block = min(block, 512)
    counts = [right[0].shape[1] // block for _, right in pairs]
    toks, rows = pairs[0][0][0].shape
    specs, operands, start = [], [], 0
    for (left, right), count in zip(pairs, counts):
        specs += [pl.BlockSpec((toks, rows), lambda i: (0, 0))] * CHUNKS
        specs += [
            pl.BlockSpec(
                (toks, block),
                lambda i, start=start, count=count: (0, jnp.clip(i - start, 0, count - 1)),
            )
        ] * CHUNKS
        operands += [*left, *right]
        start += count
    more = [*after] if target is None else [target, *after]
    return pl.pallas_call(
        functools.partial(products_kernel, counts),
        grid=(start,),
        out_shape=bf16_out(rows, columns),
        in_specs=specs + [ANYWHERE] * len(more),
        out_specs=pl.BlockSpec((rows, block), lambda i: (0, i + at // block)),
        scratch_shapes=[pltpu.VMEM((rows, CHUNKS * toks), BF16)],
        input_output_aliases={} if target is None else {len(operands): 0},
        compiler_params=params(),
        cost_estimate=cost(2 * rows * CHUNKS * toks * start * block, 20e6),
        name="weight_products",
    )(*operands, *more)


def norm_back(
    layer, stream_ref, own_ref, other_ref, grad_ref, gain_ref, gain_out, shift_out
):
    grad = own_ref[...].astype(F32) + other_ref[...].astype(F32)
    back, unit = layer_norm_back(stream_ref[...], gain_ref[layer : layer + 1], grad)
    gain_out[...] = jnp.sum(grad * unit, axis=0, keepdims=True)
    shift_out[...] = jnp.sum(grad, axis=0, keepdims=True)
    return grad_ref[...] + back


def leave_kernel(
    seqs, layer, after, stream_ref, own_ref, other_ref, grad_ref, gain_ref, weight_ref, *refs
):
    new_ref, low_ref, gain_out, shift_out, bias_out, out_ref = refs[after:]
    grad = norm_back(
        layer, stream_ref, own_ref, other_ref, grad_ref, gain_ref, gain_out, shift_out
    )
    new_ref[...] = grad
    bias_out[...] = jnp.sum(grad, axis=0, keepdims=True)
    low = grad.astype(BF16)
    low_ref[...] = low
    flat = mm(low, weight_ref[...]).astype(BF16)
    slots, rows, width = out_ref.shape
    for k, at in enumerate(unit_slices(seqs, slots // seqs, rows, width)):
        out_ref[k] = flat[at]


def leave_ffn(
    seqs, layer, stream, own, other, grad, gain, weight, place, columns, after=()
):
    toks, width = stream.shape
    shapes = [f32_out(toks, width), bf16_out(toks, width)] + [f32_out(1, width)] * 3
    shapes.append(bf16_out(seqs * columns // HD, toks // seqs, HD))
    operands = (stream, own, other, grad, gain)
    return pl.pallas_call(
        functools.partial(leave_kernel, seqs, layer, len(after)),
        grid=(1,),
        out_shape=shapes,
        in_specs=[whole_block(operand) for operand in operands]
        + [column_block(width, columns, place)]
        + [ANYWHERE] * len(after),
        out_specs=[whole_block(shape) for shape in shapes],
        compiler_params=params(),
        cost_estimate=cost(2 * toks * width * columns, 6e6),
        name="leave_ffn",
    )(*operands, weight, *after)


def finish_kernel(layer, stream_ref, own_ref, other_ref, grad_ref, gain_ref, *refs):
    new_ref, gain_out, shift_out = refs[-3:]
    new_ref[...] = norm_back(
        layer, stream_ref, own_ref, other_ref, grad_ref, gain_ref, gain_out, shift_out
    )


def finish_attention(layer, stream, own, other, grad, gain, after=()):
    toks, width = stream.shape
    return pl.pallas_call(
        functools.partial(finish_kernel, layer),
        out_shape=(f32_out(toks, width), f32_out(1, width), f32_out(1, width)),
        in_specs=[IN_VMEM] * 5 + [ANYWHERE] * len(after),
        out_specs=(IN_VMEM,) * 3,
        compiler_params=params(),
        cost_estimate=cost(1e7, 4e6),
        name="finish_attention",
    )(stream, own, other, grad, gain, *after)


def reduce_rows(value):
    count = lax.axis_size("wide")
    index = lax.axis_index("wide")
    width = value.shape[1]
    block = value.shape[0] // count
    value = value.astype(BF16)
    stages = []
    bit = 1
    parts = count
    while bit < count:
        view = value.reshape(parts // 2, 2, block, width)
        mine = (index // bit) % 2
        sent = lax.dynamic_index_in_dim(view, 1 - mine, 1, keepdims=False)
        kept = lax.dynamic_index_in_dim(view, mine, 1, keepdims=False)
        value = kept.astype(F32) + swap(sent, "wide", bit).astype(F32)
        parts //= 2
        bit *= 2
        if bit < count:
            value = value.astype(BF16)
        stages.append(value)
    return stages[:-1] + [value.reshape(block, width)]


def sum_rows(value, widths):
    total = lax.psum_scatter(value, "wide", scatter_dimension=0, tiled=True).astype(F32)
    ends = [0]
    for width in widths:
        ends.append(ends[-1] + width)
    return [total[:, low:high] for low, high in zip(ends, ends[1:])]


def sum_wide(value):
    for bit in range(lax.axis_size("wide").bit_length() - 1):
        value = value + swap(value, "wide", 1 << bit)
    return value


def shards(
    first_in, second_in, attn_norm_gain, attn_norm_bias, qk_weight, value_weight, out_weight,
    out_bias, ffn_norm_gain, ffn_norm_bias, up_weight, up_bias, down_weight, down_bias,
    bucket_perm, first_cot, second_cot,
):
    seqs, rows, half = first_in.shape
    wide = lax.axis_size("wide")
    wide_index = lax.axis_index("wide")
    narrow_index = lax.axis_index("narrow")
    pos = jnp.stack([wide_index % 2, narrow_index]).astype(jnp.int32)
    weight_rows, head_width = qk_weight.shape[1:]
    heads = head_width // HD
    width = 2 * half
    hidden_width = up_bias.shape[1]
    chunks = range(CHUNKS)

    def own_half(full):
        return lax.dynamic_slice_in_dim(full, narrow_index * half, half, full.ndim - 1)

    def flat_weight(layer):
        pair = jnp.stack([qk_weight[layer], value_weight[layer]], axis=1)
        pair = pair.reshape(weight_rows, 2, heads, HD)
        return jnp.transpose(pair, (0, 2, 1, 3)).reshape(weight_rows, 2 * head_width)

    streams = (second_in, first_in, second_cot, first_cot)
    others = [swap(sent, "narrow", 1) for sent in lower_arrays(streams, ())]
    second, first = [widen_chunks(pos, streams[k], others[k]) for k in range(2)]
    early = lax.all_gather(
        jnp.concatenate([flat_weight(0), out_weight[0]], axis=1), "wide", axis=0, tiled=True
    )

    perm_parts = bucket_perm.reshape(2, ROUNDS // 2, seqs, rows)
    perm_send = jnp.transpose(perm_parts, (2, 0, 1, 3))
    perm_send = jnp.broadcast_to(
        perm_send[:, None], (seqs, heads, 2, ROUNDS // 2, rows)
    ).reshape(wide, ROUNDS // 2, rows)
    perm_got = lax.all_to_all(perm_send, "wide", 0, 0, tiled=True)
    tables = build_tables(jnp.transpose(perm_got, (1, 0, 2)).reshape(ROUNDS // 2, wide * rows))

    unit_columns = 2 * head_width
    gathered = [early]
    biases = jnp.stack([out_bias, down_bias])
    other = swap(biases, "narrow", 1)
    out_bias, down_bias = jnp.where(
        narrow_index == 0,
        jnp.concatenate([biases, other], axis=-1),
        jnp.concatenate([other, biases], axis=-1),
    )

    saved = []
    ffn_parts = [() for _ in chunks]
    afters = [[], [*tables, *first, *others[2:], out_bias, down_bias]]
    for layer in range(LAYERS):
        normed, sources = [], []
        for q in chunks:
            second[q], normed_q, units = enter_attention(
                seqs, layer, second[q], attn_norm_gain, attn_norm_bias, gathered[layer], 0,
                unit_columns, ffn_parts[q], afters[min(q, 1)],
            )
            normed.append(normed_q)
            own = chip_exchange(units)
            sources += [own, swap(own, "wide", 1)]
        sorted_rows, own, sib = attention_forward(pos, sources, tables, ())
        attn, stats, units = combine_cores(own, swap(sib, "wide", 1))
        after = []
        if layer == 0:
            grad_second, grad_first = [
                widen_chunks(pos, streams[k], others[k]) for k in range(2, 4)
            ]
            after = [*grad_second, *grad_first]
        if layer + 1 < LAYERS:
            pieces = pack_columns([flat_weight(layer + 1), out_weight[layer + 1]], units[:1])
            gathered.append(lax.all_gather(pieces, "wide", axis=0, tiled=True))
        second_now, attn_tok, ffn_in, pre_act = list(second), [], [], []
        backs = [chip_exchange(units[q]) for q in chunks]
        merged = []
        for q in chunks:
            part, attn_tok_q = merge_units(
                seqs, backs[q], gathered[layer], 2, after + attn_tok if q > 0 else ()
            )
            attn_tok.append(attn_tok_q)
            merged.append((part, swap(part, "narrow", 1)))
        for q in chunks:
            first[q], ffn_in_q, pre_q, part = feed_forward(
                layer, first[q], *merged[q], out_bias, ffn_norm_gain, ffn_norm_bias,
                up_weight, up_bias, down_weight, attn_tok[1:] + ffn_in,
            )
            ffn_in.append(ffn_in_q)
            pre_act.append(pre_q)
            if layer + 1 < LAYERS:
                ffn_parts[q] = (part, swap(part, "narrow", 1), down_bias)
            else:
                ffn_parts[q] = part
        afters = [ffn_in[1:], []]
        saved.append((second_now, normed, sorted_rows, attn, stats, attn_tok, list(first), ffn_in, pre_act))
    first_out = narrow_chunks(pos, first, seqs)
    sent = [
        lax.dynamic_slice_in_dim(part, (1 - narrow_index) * half, half, 1) for part in ffn_parts
    ]
    got = swap(jnp.concatenate(sent), "narrow", 1)
    summed, waiting = [], []
    done = []
    early_smalls, late_smalls = [None] * LAYERS, [None] * LAYERS
    after = []
    for layer in reversed(range(LAYERS)):
        second_l, normed, sorted_rows, attn, stats, attn_tok, first_l, ffn_in, pre_act = saved[layer]
        branch, hidden, low, parts = [], [], [], []
        late_gain, late_shift = 0.0, 0.0
        down_bias_grad, up_bias_grad = 0.0, 0.0
        for q in chunks:
            *results, branch_q, hidden_q, low_q, down_bias_q, up_bias_q, part = feed_back(
                layer, grad_second[q], up_weight, down_weight, pre_act[q],
                before[q] if layer + 1 < LAYERS else None,
            )
            if results:
                grad_second[q], gain_q, shift_q = results
                late_gain += gain_q
                late_shift += shift_q
            branch.append(branch_q)
            hidden.append(hidden_q)
            low.append(low_q)
            parts.append((part, swap(part, "narrow", 1)))
            down_bias_grad += down_bias_q
            up_bias_grad += up_bias_q
        pairs = waiting + [(ffn_in, low), (branch, hidden)]
        widths = [right[0].shape[1] for _, right in pairs]
        columns = sum(widths) + head_width
        products = [weight_products(pairs, columns)]
        out_low, units = [], []
        ffn_gain_grad, ffn_bias_grad, out_bias_grad = 0.0, 0.0, 0.0
        for q in chunks:
            *results, units_q = leave_ffn(
                seqs, layer, first_l[q], *parts[q], grad_first[q], ffn_norm_gain,
                gathered[layer], 2, head_width, [*units, *products] if q > 0 else (),
            )
            grad_first[q] = results[0]
            out_low.append(results[1])
            ffn_gain_grad += results[2]
            ffn_bias_grad += results[3]
            out_bias_grad += results[4]
            units.append(chip_exchange(units_q))
        if layer == 0:
            products = [
                weight_products([(out_low, attn_tok)], columns, columns - head_width, *products)
            ]
            summed += sum_rows(*products, widths + [head_width])
        sources = []
        for q in chunks:
            own = join_grads(
                q, attn, stats, units[q], products if q > 0 and layer == 0 else ()
            )
            sources += [own, swap(own, "wide", 1)]
        early_small = jnp.concatenate(
            [
                own_half(grad)
                for grad in (ffn_gain_grad, ffn_bias_grad, out_bias_grad, down_bias_grad)
            ]
            + [up_bias_grad.reshape(-1, half)]
        )
        own, sib = attention_backward(pos, sources, sorted_rows, tables, [early_small])
        units = add_cores(own, swap(sib, "wide", 1), done)
        grad_tok = []
        backs = [chip_exchange(units[q]) for q in chunks]
        after = []
        merged = []
        for q in chunks:
            part, grad_tok_q = merge_units(seqs, backs[q], gathered[layer], 0, after + grad_tok)
            if layer > 0 and q == 0:
                after = [
                    weight_products(
                        [(out_low, attn_tok)], columns, columns - head_width, *products, [grad_tok_q]
                    )
                ]
                summed += sum_rows(*after, widths + [head_width])
            grad_tok.append(grad_tok_q)
            merged.append((part, swap(part, "narrow", 1)))
        waiting = [(normed, grad_tok)]
        stages = [None]
        if layer == 0:
            stages = reduce_rows(weight_products(waiting, unit_columns))
            summed.append(stages[-1])
        before = [
            (layer, second_l[q], *merged[q], attn_norm_gain) for q in chunks
        ]
        if layer + 1 < LAYERS:
            late_smalls[layer + 1] = (late_gain, late_shift)
        done = summed[-1:]
        early_smalls[layer] = early_small
    late_gain, late_shift = 0.0, 0.0
    for q in chunks:
        norm, stream, own, other, gain = before[q]
        grad_second[q], gain_q, shift_q = finish_attention(
            norm, stream, own, other, grad_second[q], gain, stages[1:2] if q > 0 else ()
        )
        late_gain += gain_q
        late_shift += shift_q
    late_smalls[0] = (late_gain, late_shift)
    small_grads = [
        jnp.concatenate([own_half(grad) for grad in late_smalls[layer]] + [early_smalls[layer]])
        for layer in range(LAYERS)
    ]
    first_grad = narrow_chunks(pos, grad_first, seqs)
    second_grad = narrow_chunks(pos, grad_second, seqs)
    second_out = narrow_chunks(
        pos, second, seqs, LAYERS - 1, [*ffn_parts, got, down_bias], grad_second[-1:]
    )

    small = sum_wide(jnp.stack(small_grads))
    other = swap(small[:, :4], "narrow", 1)
    paired = jnp.where(
        narrow_index == 0,
        jnp.concatenate([small[:, :4], other], axis=-1),
        jnp.concatenate([other, small[:, :4]], axis=-1),
    )
    order = [(4, 5, 6, 7), (0, 1, 2, 3)]
    weight_grads = [None] * LAYERS
    for layer in range(LAYERS):
        up_sum, down_sum, out_sum, unit_sum = [summed[at] for at in order[layer]]
        by_unit = unit_sum.reshape(weight_rows, heads, 2, HD)
        weight_grads[layer] = (
            by_unit[:, :, 0].reshape(weight_rows, head_width),
            by_unit[:, :, 1].reshape(weight_rows, head_width),
            out_sum,
            up_sum,
            down_sum,
        )

    def stacked(slot):
        return jnp.stack([weight_grads[layer][slot] for layer in range(LAYERS)])

    return (
        first_out,
        second_out,
        first_grad,
        second_grad,
        paired[:, 0],
        paired[:, 1],
        stacked(0),
        stacked(1),
        stacked(2),
        small[:, 4],
        paired[:, 2],
        paired[:, 3],
        stacked(3),
        small[:, 6:].reshape(LAYERS, hidden_width),
        stacked(4),
        small[:, 5],
    )


def solution(mesh):
    streams = P(None, "wide", "narrow")
    features = P(None, "narrow")
    hidden = P(None, None, "narrow")
    return jax.shard_map(
        shards,
        mesh=mesh,
        in_specs=(
            streams, streams, P(), P(), streams, streams, streams, features, P(), P(),
            hidden, features, hidden, features, P(None, None, "wide"), streams, streams,
        ),
        out_specs=(
            streams, streams, streams, streams, P(), P(), streams, streams, streams,
            features, P(), P(), streams, features, streams, features,
        ),
        check_vma=False,
    )
```
